32 devices in a mesh: groups: 2 (over y), col: 8 (over z, x), rep: 2 (over core).
Axes of the slice: x: 2, y: 2, z: 4, core: 2. Of those that a mesh axis runs over, the one named last changes fastest.
Arguments:
- features: bfloat16 [768, 131072], P('col', ('groups', 'rep')), parts along dimension 1, may hold values from -6 to 6
- self_ids: int32 [11264], P(('groups', 'rep')), parts along dimension 0, may hold values from 0 to 65535
- neighbour_ids: int32 [15, 11264], P(None, ('groups', 'rep')), parts along dimension 1, may hold values from 0 to 65535
- count_one: int32 [11264], P(('groups', 'rep')), parts along dimension 0, may hold values from 1 to 15
- count_two: int32 [1024], P(('groups', 'col', 'rep')), parts along dimension 0, may hold values from 1 to 10
- self_one: bfloat16 [768, 256], P('col'), may hold values from -0.21875 to 0.21875
- neigh_one: bfloat16 [768, 256], P('col'), may hold values from -0.21875 to 0.21875
- bias_one: float32 [256], replicated, may hold values from -3 to 3
- self_two: bfloat16 [256, 256], replicated, may hold values from -0.375 to 0.375
- neigh_two: bfloat16 [256, 256], replicated, may hold values from -0.375 to 0.375
- bias_two: float32 [256], replicated, may hold values from -3 to 3
- out_weight: bfloat16 [256, 153], replicated, may hold values from -0.375 to 0.375
- out_bias: float32 [153], replicated, may hold values from -3 to 3
Outputs:
- logits: float32 [1024, 153], P(('groups', 'col', 'rep')), parts along dimension 0
The draws below stay inside these ranges and needn't reach their ends.
There are 2 independent parts, one for each index of `groups`. The reference program is written for one: setup_inputs(seed, part) draws one part's arguments, and reference() takes and returns one part's arrays. A program takes and returns all parts, laid end to end along the dimension named above; an argument that names none is the same for every part. Nothing has to cross between parts.
All inputs are finite; a program needn't handle non-finite values.
Results may differ from the reference program's by a relative error of at most 0.0039.
Values may be sent and summed in bfloat16 or wider, within the bound.
No kernel may reach another device: no remote copies, remote signals or barrier semaphores. Data moves between devices by JAX's collectives and lax.ppermute only.
A program may use at most 256 MiB of HBM per device.

```python
import jax
import jax.numpy as jnp
from jax import lax

D_IN = 768
HID = 256
CLASSES = 153
F1 = 15
F2 = 10
TABLE = 65536
R_DEV = 352
SEEDS = 512
N_COL = 8
N_REP = 2


def set_ends(result, key, low, top_value):
    place = [jax.random.randint(jax.random.fold_in(key, axis), (), 0, length) for axis, length in enumerate(result.shape)]
    widest = result.shape.index(max(result.shape))
    next_to = place[:widest] + [(place[widest] + 1) % result.shape[widest]] + place[widest + 1:]
    return result.at[tuple(place)].set(low).at[tuple(next_to)].set(top_value)


def shard_levels(rng, shape, pieces, smallest, top_value):
    def one(axis_at, blocks):
        heights = jax.random.uniform(jax.random.fold_in(jax.random.fold_in(rng, 6), axis_at), (blocks,), jnp.float32, smallest / len(pieces), top_value / len(pieces))
        return jnp.repeat(jnp.exp(heights), shape[axis_at] // blocks).reshape((-1,) + (1,) * (len(shape) - axis_at - 1))

    factor_of = one(*pieces[0])
    for cut in pieces[1:]:
        factor_of = factor_of * one(*cut)
    return factor_of


def bell_draw(key, dims, deviation, reach, shards=(), kind=jnp.bfloat16):
    level = shard_levels(key, dims, shards, -0.22, 0.18) if shards else 1.0
    array = jax.random.normal(key, dims, jnp.float32) * deviation * level
    return jnp.minimum(jnp.maximum(array, -reach), reach).astype(kind)


def setup_inputs(seed: int = 0, part: int = 0) -> dict:
    arg_keys = jax.random.split(jax.random.key(seed), 14)
    part_keys = jax.random.split(jax.random.fold_in(arg_keys[13], part), 14)
    features = bell_draw(part_keys[0], (D_IN, TABLE), 1.0, 6.0, ((0, 8), (1, 2)))
    self_ids = set_ends(jax.random.randint(part_keys[1], (N_REP * N_COL * R_DEV,), 0, TABLE), jax.random.fold_in(part_keys[1], 1), 0, TABLE - 1).astype(jnp.int32)
    neighbour_ids = set_ends(jax.random.randint(part_keys[2], (F1, N_REP * N_COL * R_DEV), 0, TABLE), jax.random.fold_in(part_keys[2], 1), 0, TABLE - 1).astype(jnp.int32)
    count_one = set_ends(jax.random.randint(part_keys[3], (N_REP * N_COL * R_DEV,), 1, F1 + 1), jax.random.fold_in(part_keys[3], 1), 1, F1).astype(jnp.int32)
    count_two = set_ends(jax.random.randint(part_keys[4], (SEEDS,), 1, F2 + 1), jax.random.fold_in(part_keys[4], 1), 1, F2).astype(jnp.int32)
    self_one = bell_draw(arg_keys[5], (D_IN, HID), D_IN ** -0.5, 0.21875, ((0, 8),))
    neigh_one = bell_draw(arg_keys[6], (D_IN, HID), D_IN ** -0.5, 0.21875, ((0, 8),))
    bias_one = bell_draw(arg_keys[7], (HID,), 0.5, 3.0, (), jnp.float32)
    self_two = bell_draw(arg_keys[8], (HID, HID), HID ** -0.5, 0.375)
    neigh_two = bell_draw(arg_keys[9], (HID, HID), HID ** -0.5, 0.375)
    bias_two = bell_draw(arg_keys[10], (HID,), 0.5, 3.0, (), jnp.float32)
    out_weight = bell_draw(arg_keys[11], (HID, CLASSES), HID ** -0.5, 0.375)
    out_bias = bell_draw(arg_keys[12], (CLASSES,), 0.5, 3.0, (), jnp.float32)
    return dict(features=features, self_ids=self_ids, neighbour_ids=neighbour_ids, count_one=count_one, count_two=count_two, self_one=self_one, neigh_one=neigh_one, bias_one=bias_one, self_two=self_two, neigh_two=neigh_two, bias_two=bias_two, out_weight=out_weight, out_bias=out_bias)


def reference(features, self_ids, neighbour_ids, count_one, count_two, self_one, neigh_one, bias_one, self_two, neigh_two, bias_two, out_weight, out_bias):
    table = features.T
    owners = N_REP * N_COL
    ids_blocks = self_ids.reshape(owners, R_DEV)
    nbr_blocks = neighbour_ids.reshape(F1, owners, R_DEV).transpose(1, 2, 0)
    cnt_blocks = count_one.reshape(owners, R_DEV)

    def block(items):
        ids, nbr, cnt = items
        self_x = table[ids]
        gathered = table[nbr].astype(jnp.float32)
        mask = (jnp.arange(F1)[None, :] < cnt[:, None]).astype(jnp.float32)
        mean_one = (jnp.sum(gathered * mask[:, :, None], axis=1) / cnt[:, None].astype(jnp.float32)).astype(jnp.bfloat16)
        pre_one = jnp.dot(self_x, self_one, preferred_element_type=jnp.float32) + jnp.dot(mean_one, neigh_one, preferred_element_type=jnp.float32)
        return jax.nn.relu(pre_one + bias_one).astype(jnp.bfloat16)

    hidden_one = lax.map(block, (ids_blocks, nbr_blocks, cnt_blocks))
    hidden_one = hidden_one.reshape(N_REP, N_COL, R_DEV, HID).transpose(1, 0, 2, 3)
    grouped = hidden_one.reshape(SEEDS, 1 + F2, HID)
    mask = (jnp.arange(F2)[None, :] < count_two[:, None]).astype(jnp.float32)
    summed = jnp.sum(grouped[:, 1:, :].astype(jnp.float32) * mask[:, :, None], axis=1)
    mean_two = (summed / count_two[:, None].astype(jnp.float32)).astype(jnp.bfloat16)
    pre_two = jnp.dot(grouped[:, 0, :], self_two, preferred_element_type=jnp.float32) + jnp.dot(mean_two, neigh_two, preferred_element_type=jnp.float32)
    hidden_two = jax.nn.relu(pre_two + bias_two).astype(jnp.bfloat16)
    return jnp.dot(hidden_two, out_weight, preferred_element_type=jnp.float32) + out_bias
```

```python
import functools

import jax
import jax.numpy as jnp
import numpy as np
from jax import lax
from jax.experimental import pallas as pl
from jax.experimental.pallas import tpu as pltpu
from jax.sharding import PartitionSpec as P

CAP = 256
UNROLL = 4
LANES = 128
MIB = 2**20
BF16 = jnp.bfloat16
F32 = jnp.float32
I32 = jnp.int32


def general(
    features,
    self_ids,
    neighbour_ids,
    count_one,
    count_two,
    self_one,
    neigh_one,
    bias_one,
    self_two,
    neigh_two,
    bias_two,
    out_weight,
    out_bias,
):
    table_cols = lax.all_gather(features, "rep", axis=1, tiled=True)
    table_rows = table_cols.T
    blocks = lax.axis_size("col")
    total_rows = self_ids.shape[0]
    per_owner = total_rows // blocks
    fanout = neighbour_ids.shape[0]
    width = table_rows.shape[1]
    all_ids = jnp.concatenate([self_ids[None, :], neighbour_ids], axis=0)
    fetched = jnp.take(table_rows, all_ids, axis=0)
    self_x = fetched[0]
    mask = (jnp.arange(fanout)[:, None] < count_one[None, :]).astype(BF16)
    summed = jnp.einsum("kmc,km->mc", fetched[1:], mask, preferred_element_type=F32)
    mean_one = (summed / count_one[:, None].astype(F32)).astype(BF16)
    full_self, full_neigh = (
        lax.all_gather(self_one, "col", axis=0, tiled=True),
        lax.all_gather(neigh_one, "col", axis=0, tiled=True),
    )
    stacked = jnp.stack([self_x, mean_one], axis=0).reshape(2, blocks, per_owner, width)
    pieces = lax.all_to_all(stacked, "col", split_axis=1, concat_axis=3, tiled=True)
    pre_one = jnp.dot(pieces[0, 0], full_self, preferred_element_type=F32) + jnp.dot(
        pieces[1, 0], full_neigh, preferred_element_type=F32
    )
    hidden_one = jax.nn.relu(pre_one + bias_one).astype(BF16)
    seeds = count_two.shape[0]
    hidden = hidden_one.shape[1]
    grouped = hidden_one.reshape(seeds, per_owner // seeds, hidden)
    mask_two = (jnp.arange(grouped.shape[1] - 1)[None, :] < count_two[:, None]).astype(BF16)
    summed_two = jnp.einsum("skh,sk->sh", grouped[:, 1:, :], mask_two, preferred_element_type=F32)
    mean_two = (summed_two / count_two[:, None].astype(F32)).astype(BF16)
    pre_two = jnp.dot(grouped[:, 0, :], self_two, preferred_element_type=F32) + jnp.dot(
        mean_two, neigh_two, preferred_element_type=F32
    )
    hidden_two = jax.nn.relu(pre_two + bias_two).astype(BF16)
    return jnp.dot(hidden_two, out_weight, preferred_element_type=F32) + out_bias


def iota(shape, dim):
    return lax.broadcasted_iota(I32, shape, dim)


def tree_sum(terms):
    while len(terms) > 1:
        odd = [terms[-1]] if len(terms) % 2 else []
        terms = [a + b for a, b in zip(terms[::2], terms[1::2])] + odd
    return terms[0]


VMEM = pl.BlockSpec(memory_space=pltpu.VMEM)
SMEM = pl.BlockSpec(memory_space=pltpu.SMEM)
HBM = pl.BlockSpec(memory_space=pltpu.HBM)
ANY = pl.BlockSpec(memory_space=pl.ANY)


def start_all(copies):
    for copy in copies:
        copy.start()


def turn(copies, staged, table, base, done=None):
    blocks, width, length = staged.shape
    step = 512
    unroll = 2
    for block in range(blocks):
        copies[block].wait()

        def body(i, carry, block=block):
            for u in range(unroll):
                off = pl.multiple_of((i * unroll + u) * step, step)
                rows = staged[block, :, pl.ds(off, step)].T.astype(F32)
                at = pl.multiple_of(base + block * length + off, step)
                table[pl.ds(at, step), 0:width] = rows
            return carry

        lax.fori_loop(0, length // step // unroll, body, 0)
        if done is not None:
            done[block].start()


def feature_copies(features, staged, sems):
    blocks, _, length = staged.shape
    return [
        pltpu.make_async_copy(features.at[:, pl.ds(b * length, length)], staged.at[b], sems.at[b])
        for b in range(blocks)
    ]


def own_rows_kernel(me, features, rows, table, staged, sems, out_sems):
    copies = feature_copies(features, staged, sems)
    start_all(copies)
    blocks, _, length = staged.shape
    done = []
    for b in range(blocks):
        to = pl.multiple_of((me[2] * blocks + b) * length, length)
        done.append(
            pltpu.make_async_copy(
                table.at[pl.ds(b * length, length), :], rows.at[pl.ds(to, length), :], out_sems.at[b]
            )
        )
    turn(copies, staged, table, 0, done)
    for copy in done:
        copy.wait()


def order_kernel(fanout, per_seed, counts_rel, me, count_one, lists):
    owners, seeds = counts_rel.shape
    per_owner = count_one.shape[1]
    half = owners // 2
    mine = me[0]
    counts = jnp.concatenate(
        [counts_rel[pl.ds(jnp.bitwise_xor(mine, c), 1), :] for c in range(owners)], axis=0
    ).astype(F32)
    needs = (counts + 1.0).astype(BF16)
    before = (iota((seeds, seeds), 0) < iota((seeds, seeds), 1)).astype(BF16)
    offset = jnp.dot(needs, before, preferred_element_type=F32)
    off_hi = jnp.floor(offset * (1.0 / 16.0))
    off_lo = offset - off_hi * 16.0
    shift = iota((seeds, per_owner), 1) - iota((seeds, per_owner), 0) * per_seed
    spread = ((shift >= 0) & (shift < per_seed)).astype(BF16)
    place = jnp.dot(iota((8, seeds), 1).astype(BF16), spread, preferred_element_type=F32)
    t = iota((owners, per_owner), 1).astype(F32) - place[0:1, :] * per_seed
    of_row = jnp.dot(counts.astype(BF16), spread, preferred_element_type=F32)
    row_hi = jnp.dot(off_hi.astype(BF16), spread, preferred_element_type=F32)
    row_lo = jnp.dot(off_lo.astype(BF16), spread, preferred_element_type=F32)
    slot = row_hi * 16.0 + row_lo + t
    used = (t <= of_row) & (slot < CAP)
    key = jnp.where(used, count_one[...], 0)
    slot = slot.astype(I32)
    kinds = [
        (iota((16, per_owner), 0) == jnp.broadcast_to(key[c : c + 1, :], (16, per_owner)))
        for c in range(owners)
    ]
    stacked = jnp.concatenate([k.astype(F32).astype(BF16) for k in kinds], axis=0)
    left = (iota((per_owner, per_owner), 0) < iota((per_owner, per_owner), 1)).astype(BF16)
    prefix = jnp.dot(stacked, left, preferred_element_type=F32)
    total = jnp.dot(stacked, jnp.ones((per_owner, LANES), BF16), preferred_element_type=F32)
    for h in range(2):
        carry = jnp.zeros((16, LANES), F32)
        carries = []
        for c in range(h * half, (h + 1) * half):
            carries.append(carry)
            carry = carry + total[c * 16 : (c + 1) * 16, :]
        sizes = jnp.floor((carry + (UNROLL - 1)) * (1.0 / UNROLL)) * UNROLL
        bases = [jnp.zeros((1, LANES), F32)]
        for v in range(1, 16):
            bases.append(bases[-1] + sizes[v : v + 1, :])
        first = jnp.concatenate([bases[0]] + bases[:15], axis=0)
        gathered = jnp.zeros((64, LANES), F32)
        for i, c in enumerate(range(h * half, (h + 1) * half)):
            begin = (first + carries[i])[:, 0:1]
            spot = jnp.where(kinds[c], prefix[c * 16 : (c + 1) * 16, :] + begin, 0.0)
            spot = jnp.sum(spot, axis=0, keepdims=True).astype(I32)
            spot = jnp.where(key[c : c + 1, :] > 0, spot, -1)
            spot_lo = jnp.bitwise_and(spot, LANES - 1)
            spot_hi = jnp.right_shift(spot, 7)
            lane = (iota((LANES, per_owner), 0) == spot_lo).astype(F32).astype(BF16)
            row = iota((1, per_owner), 1) + c * per_owner
            back = half * CAP - (slot[c : c + 1, :] + i * CAP)
            at_hi = iota((16, per_owner), 0) == spot_hi
            values = jnp.concatenate(
                [
                    jnp.where(at_hi, jnp.broadcast_to(x, (16, per_owner)).astype(F32), 0.0)
                    for x in (
                        jnp.right_shift(row, 8),
                        jnp.bitwise_and(row, 255),
                        jnp.right_shift(back, 8),
                        jnp.bitwise_and(back, 255),
                    )
                ],
                axis=0,
            ).astype(BF16)
            gathered = gathered + lax.dot_general(
                values, lane, (((1,), (1,)), ((), ())), preferred_element_type=F32
            )
        lists[h, 0:16, :] = (gathered[0:16, :] * 256.0 + gathered[16:32, :]).astype(I32)
        lists[h, 16:32, :] = half * CAP - (
            gathered[32:48, :] * 256.0 + gathered[48:64, :]
        ).astype(I32)
        lists[h, 32:48, :] = jnp.concatenate(bases, axis=0).astype(I32)


def look_up(fanout, table, ids, lists, self_rows, mean_rows):
    def entry(kind, at):
        return lists[kind + jnp.right_shift(at, 7), jnp.bitwise_and(at, LANES - 1)]

    for v in range(1, fanout + 1):
        begin = lists[32 + v - 1, 0]
        end = lists[32 + v, 0]

        def body(i, carry, v=v, begin=begin):
            for u in range(UNROLL):
                at = begin + i * UNROLL + u
                row = entry(0, at)
                to = entry(16, at)
                self_rows[pl.ds(to, 1), :] = table[pl.ds(ids[0][row], 1), :]
                total = tree_sum([table[pl.ds(ids[k][row], 1), :] for k in range(1, v + 1)])
                mean_rows[pl.ds(to, 1), :] = total * (1.0 / v)
            return carry

        lax.fori_loop(0, jnp.right_shift(end - begin, UNROLL.bit_length() - 1), body, 0)


def write_out(x, width, self_rows, mean_rows, keep, send):
    valid = iota((CAP, LANES), 1) < width
    for z in range(2):
        for ref, side in ((keep, x), (send, 1 - x)):
            at = pl.multiple_of((z * 2 + side) * CAP, CAP)
            for part, rows in enumerate((self_rows, mean_rows)):
                block = jnp.where(valid, rows[pl.ds(at, CAP), :], 0.0).astype(BF16)
                ref[z, :, part * LANES : (part + 1) * LANES] = block


def first_kernel(
    fanout, me, lists_hbm, ids_hbm, table_in, other, table, keep, send, *scratch
):
    ids = scratch[: fanout + 1]
    lists, self_rows, mean_rows, staged, sems, small = scratch[fanout + 1 :]
    width = other.shape[0]
    length = other.shape[1]
    x, h, rep = me[0], me[1], me[2]
    copies = feature_copies(other, staged, sems)
    start_all(copies)
    rest = [pltpu.make_async_copy(lists_hbm.at[h], lists, small.at[1])]
    rest += [pltpu.make_async_copy(ids_hbm.at[k], ids[k], small.at[2 + k]) for k in range(fanout + 1)]
    start_all(rest)
    self_rows[...] = jnp.zeros_like(self_rows)
    mean_rows[...] = jnp.zeros_like(mean_rows)
    turn(copies, staged, table, pl.multiple_of((1 - rep) * length, length))
    for copy in rest:
        copy.wait()
    look_up(fanout, table, ids, lists, self_rows, mean_rows)
    write_out(x, width, self_rows, mean_rows, keep, send)


def second_kernel(fanout, width, me, lists_hbm, ids_hbm, table, keep, send, *scratch):
    ids = scratch[: fanout + 1]
    lists, self_rows, mean_rows, small = scratch[fanout + 1 :]
    x, h = me[0], 1 - me[1]
    rest = [pltpu.make_async_copy(lists_hbm.at[h], lists, small.at[1])]
    rest += [pltpu.make_async_copy(ids_hbm.at[k], ids[k], small.at[2 + k]) for k in range(fanout + 1)]
    start_all(rest)
    self_rows[...] = jnp.zeros_like(self_rows)
    mean_rows[...] = jnp.zeros_like(mean_rows)
    for copy in rest:
        copy.wait()
    look_up(fanout, table, ids, lists, self_rows, mean_rows)
    write_out(x, width, self_rows, mean_rows, keep, send)


def project_kernel(me, keep, got, weight, weight_got, out_0, out_1):
    zl = me[3]
    for which, out in ((zl, out_0), (1 - zl, out_1)):
        out[...] = (
            jnp.dot(keep[which], weight[...], preferred_element_type=F32)
            + jnp.dot(got[which], weight_got[...], preferred_element_type=F32)
        ).astype(out.dtype)


def last_kernel(
    mine, a, b, c, counts, bias_one, self_two, neigh_two, bias_two, out_weight, out_bias, out
):
    pre = mine[...] + a[...].astype(F32) + b[...].astype(F32) + c[...].astype(F32)
    hidden = jnp.maximum(pre + bias_one[...], 0.0).astype(BF16)
    seeds = counts.shape[0]
    count = counts[...]
    earlier = (iota((seeds, seeds), 0) > iota((seeds, seeds), 1)).astype(BF16)
    needs = jnp.broadcast_to((count + 1).astype(F32), (seeds, LANES)).astype(BF16)
    offset = jnp.dot(earlier, needs, preferred_element_type=F32)[:, 0:1].astype(I32)
    place = iota((seeds, CAP), 1) - offset
    is_self = (place == 0).astype(F32).astype(BF16)
    is_near = ((place >= 1) & (place <= count)).astype(F32).astype(BF16)
    own = jnp.dot(is_self, hidden, preferred_element_type=F32).astype(BF16)
    total = jnp.dot(is_near, hidden, preferred_element_type=F32)
    mean = (total / count.astype(F32)).astype(BF16)
    pre_two = (
        jnp.dot(own, self_two[...], preferred_element_type=F32)
        + jnp.dot(mean, neigh_two[...], preferred_element_type=F32)
        + bias_two[...]
    )
    hidden_two = jnp.maximum(pre_two, 0.0).astype(BF16)
    out[...] = jnp.dot(hidden_two, out_weight[...], preferred_element_type=F32) + out_bias[...]


def params(limit):
    return pltpu.CompilerParams(vmem_limit_bytes=limit * MIB)


def shape(dims, dtype):
    return jax.ShapeDtypeStruct(dims, dtype)


def own_rows_call(me, features):
    width, length = features.shape
    return pl.pallas_call(
        own_rows_kernel,
        out_shape=shape((2 * length, LANES), F32),
        in_specs=[SMEM, ANY],
        out_specs=HBM,
        scratch_shapes=[
            pltpu.VMEM((length, LANES), F32),
            pltpu.VMEM((4, width, length // 4), BF16),
            pltpu.SemaphoreType.DMA((4,)),
            pltpu.SemaphoreType.DMA((4,)),
        ],
        compiler_params=params(28),
        name="own_rows",
    )(me, features)


def order_call(fanout, per_seed, counts_rel, col, count_one):
    return pl.pallas_call(
        functools.partial(order_kernel, fanout, per_seed),
        out_shape=shape((2, 48, LANES), I32),
        in_specs=[VMEM, SMEM, VMEM],
        out_specs=VMEM,
        compiler_params=params(10),
        name="order",
    )(counts_rel, col, count_one)


def id_scratch(fanout, rows):
    return [pltpu.SMEM((rows,), I32) for _ in range(fanout + 1)] + [
        pltpu.SMEM((48, LANES), I32),
        pltpu.VMEM((4 * CAP + 8, LANES), F32),
        pltpu.VMEM((4 * CAP + 8, LANES), F32),
    ]


def first_call(me, lists, ids, own_rows, other):
    width, length = other.shape
    fanout = ids.shape[0] - 1
    halves = shape((2, CAP, 2 * LANES), BF16)
    return pl.pallas_call(
        functools.partial(first_kernel, fanout),
        out_shape=(shape((2 * length, LANES), F32), halves, halves),
        in_specs=[SMEM, ANY, ANY, VMEM, ANY],
        out_specs=(VMEM, VMEM, VMEM),
        scratch_shapes=id_scratch(fanout, ids.shape[1])
        + [
            pltpu.VMEM((4, width, length // 4), BF16),
            pltpu.SemaphoreType.DMA((4,)),
            pltpu.SemaphoreType.DMA((fanout + 3,)),
        ],
        input_output_aliases={3: 0},
        compiler_params=params(10),
        name="first_half",
    )(me, lists, ids, own_rows, other)


def second_call(width, me, lists, ids, table):
    fanout = ids.shape[0] - 1
    halves = shape((2, CAP, 2 * LANES), BF16)
    return pl.pallas_call(
        functools.partial(second_kernel, fanout, width),
        out_shape=(halves, halves),
        in_specs=[SMEM, ANY, ANY, VMEM],
        out_specs=(VMEM, VMEM),
        scratch_shapes=id_scratch(fanout, ids.shape[1])
        + [pltpu.SemaphoreType.DMA((fanout + 3,))],
        compiler_params=params(10),
        name="second_half",
    )(me, lists, ids, table)


def project_call(me, keep, got, weight, weight_got, kinds):
    hidden = weight.shape[1]
    return pl.pallas_call(
        project_kernel,
        out_shape=tuple(shape((CAP, hidden), kind) for kind in kinds),
        in_specs=[SMEM, VMEM, VMEM, VMEM, VMEM],
        out_specs=(VMEM, VMEM),
        compiler_params=params(10),
        name="project",
    )(me, keep, got, weight, weight_got)


def last_call(*args):
    seeds = args[4].shape[0]
    classes = args[-1].shape[1]
    return pl.pallas_call(
        last_kernel,
        out_shape=shape((seeds, classes), F32),
        in_specs=[VMEM] * len(args),
        out_specs=VMEM,
        compiler_params=params(10),
        name="layer_two",
    )(*args)


def main(
    features,
    self_ids,
    neighbour_ids,
    count_one,
    count_two,
    self_one,
    neigh_one,
    bias_one,
    self_two,
    neigh_two,
    bias_two,
    out_weight,
    out_bias,
):
    owners = lax.axis_size("col")
    seeds = count_two.shape[0]
    rows = self_ids.shape[0]
    per_owner = rows // owners
    per_seed = per_owner // seeds
    fanout = neighbour_ids.shape[0]
    width = features.shape[0]
    col = lax.axis_index("col")
    rep = lax.axis_index("rep")
    z = col // 2
    me = jnp.stack([col % 2, 1 - z // 2, rep, z % 2]).astype(I32)

    def across(value, bit):
        return lax.ppermute(value, "col", [(i, i ^ bit) for i in range(owners)])

    other = lax.ppermute(features, "rep", [(0, 1), (1, 0)])
    weight = jnp.concatenate(
        [jnp.pad(w, ((0, LANES - width), (0, 0))) for w in (self_one, neigh_one)], axis=0
    )
    counts = count_two[None, :]
    for bit in (1, 2, 4):
        counts = jnp.concatenate([counts, across(counts, bit)], axis=0)
    weight_got = across(weight, 1)
    own_rows = own_rows_call(me, features)
    ids = jnp.concatenate([self_ids[None, :], neighbour_ids], axis=0)
    lists = order_call(
        fanout, per_seed, counts, col.reshape(1).astype(I32), count_one.reshape(owners, per_owner)
    )
    lists, weight_got = lax.optimization_barrier((lists, weight_got))
    table, keep_far, send_far = first_call(me, lists, ids, own_rows, other)
    got_far = across(send_far, 1)
    keep_near, send_near = second_call(width, me, lists, ids, table)
    far = project_call(me, keep_far, got_far, weight, weight_got, (BF16, BF16))
    got_near = across(send_near, 1)
    got = [across(far[0], 4), across(far[1], 6)]
    near = project_call(me, keep_near, got_near, weight, weight_got, (F32, BF16))
    got.append(across(near[1], 2))
    fast = last_call(
        near[0],
        *got,
        count_two[:, None],
        bias_one[None, :],
        self_two,
        neigh_two,
        bias_two[None, :],
        out_weight,
        out_bias[None, :],
    )
    most = jnp.max(jnp.sum(counts + 1, axis=1)).reshape(1)
    most = jnp.maximum(most, lax.ppermute(most, "rep", [(0, 1), (1, 0)]))
    most = jnp.maximum(most, lax.ppermute(most, "groups", [(0, 1), (1, 0)]))
    return lax.cond(
        most[0] > CAP,
        lambda: general(
            features,
            self_ids,
            neighbour_ids,
            count_one,
            count_two,
            self_one,
            neigh_one,
            bias_one,
            self_two,
            neigh_two,
            bias_two,
            out_weight,
            out_bias,
        ),
        lambda: fast,
    )


def local(*args):
    features, self_ids, neighbour_ids = args[0], args[1], args[2]
    sizes = (lax.axis_size("groups"), lax.axis_size("col"), lax.axis_size("rep"))
    small = (
        sizes == (2, 8, 2)
        and features.shape[0] <= LANES
        and features.shape[1] <= 32768
        and self_ids.shape[0] * (neighbour_ids.shape[0] + 1) <= 2**17
        and neighbour_ids.shape[0] <= 15
    )
    return main(*args) if small else general(*args)


def solution(mesh):
    placed = (
        P("col", ("groups", "rep")),
        P(("groups", "rep")),
        P(None, ("groups", "rep")),
        P(("groups", "rep")),
        P(("groups", "col", "rep")),
        P("col", None),
        P("col", None),
        P(),
        P(),
        P(),
        P(),
        P(),
        P(),
    )
    return jax.shard_map(
        local,
        mesh=mesh,
        in_specs=placed,
        out_specs=P(("groups", "col", "rep"), None),
        check_vma=False,
    )
```

```python
import functools

import jax
import jax.numpy as jnp
import numpy as np
from jax import lax
from jax.experimental import pallas as pl
from jax.experimental.pallas import tpu as pltpu
from jax.sharding import PartitionSpec as P

CAP = 256
UNROLL = 8
POSITIONS = 9 * 128
FIRST_MIB = 20
LANES = 128
MIB = 2**20
BF16 = jnp.bfloat16
F32 = jnp.float32
I32 = jnp.int32


def gathered(value, axis):
    copies = jnp.broadcast_to(value[None], (lax.axis_size(axis),) + value.shape)
    pieces = lax.all_to_all(copies, axis, split_axis=0, concat_axis=0, tiled=True)
    return pieces.reshape((-1,) + value.shape[1:])


def general(
    other,
    features,
    self_ids,
    neighbour_ids,
    count_one,
    count_two,
    self_one,
    neigh_one,
    bias_one,
    self_two,
    neigh_two,
    bias_two,
    out_weight,
    out_bias,
):
    mine = jnp.where(lax.axis_index("rep") == 0, 0, 1)
    table_cols = jnp.where(
        mine == 0,
        jnp.concatenate([features, other], axis=1),
        jnp.concatenate([other, features], axis=1),
    )
    table_rows = table_cols.T
    blocks = lax.axis_size("col")
    total_rows = self_ids.shape[0]
    per_owner = total_rows // blocks
    fanout = neighbour_ids.shape[0]
    width = table_rows.shape[1]
    all_ids = jnp.concatenate([self_ids[None, :], neighbour_ids], axis=0)
    fetched = jnp.take(table_rows, all_ids, axis=0)
    self_x = fetched[0]
    mask = (jnp.arange(fanout)[:, None] < count_one[None, :]).astype(BF16)
    summed = jnp.einsum("kmc,km->mc", fetched[1:], mask, preferred_element_type=F32)
    mean_one = (summed / count_one[:, None].astype(F32)).astype(BF16)
    full_self, full_neigh = gathered(self_one, "col"), gathered(neigh_one, "col")
    stacked = jnp.stack([self_x, mean_one], axis=0).reshape(2, blocks, per_owner, width)
    pieces = lax.all_to_all(stacked, "col", split_axis=1, concat_axis=3, tiled=True)
    pre_one = jnp.dot(pieces[0, 0], full_self, preferred_element_type=F32) + jnp.dot(
        pieces[1, 0], full_neigh, preferred_element_type=F32
    )
    hidden_one = jax.nn.relu(pre_one + bias_one).astype(BF16)
    seeds = count_two.shape[0]
    hidden = hidden_one.shape[1]
    grouped = hidden_one.reshape(seeds, per_owner // seeds, hidden)
    mask_two = (jnp.arange(grouped.shape[1] - 1)[None, :] < count_two[:, None]).astype(BF16)
    summed_two = jnp.einsum("skh,sk->sh", grouped[:, 1:, :], mask_two, preferred_element_type=F32)
    mean_two = (summed_two / count_two[:, None].astype(F32)).astype(BF16)
    pre_two = jnp.dot(grouped[:, 0, :], self_two, preferred_element_type=F32) + jnp.dot(
        mean_two, neigh_two, preferred_element_type=F32
    )
    hidden_two = jax.nn.relu(pre_two + bias_two).astype(BF16)
    return jnp.dot(hidden_two, out_weight, preferred_element_type=F32) + out_bias


def iota(shape, dim):
    return lax.broadcasted_iota(I32, shape, dim)


def tree_sum(terms):
    while len(terms) > 1:
        odd = [terms[-1]] if len(terms) % 2 else []
        terms = [a + b for a, b in zip(terms[::2], terms[1::2])] + odd
    return terms[0]


VMEM = pl.BlockSpec(memory_space=pltpu.VMEM)
SMEM = pl.BlockSpec(memory_space=pltpu.SMEM)
HBM = pl.BlockSpec(memory_space=pltpu.HBM)
ANY = pl.BlockSpec(memory_space=pl.ANY)


def start_all(copies):
    for copy in copies:
        copy.start()


def turn(source, table, base):
    width, length = source.shape
    step = 512
    unroll = 4

    def body(i, carry):
        for u in range(unroll):
            off = pl.multiple_of((i * unroll + u) * step, step)
            rows = source[:, pl.ds(off, step)].T.astype(F32)
            table[pl.ds(pl.multiple_of(base + off, step), step), 0:width] = rows
        return carry

    lax.fori_loop(0, length // step // unroll, body, 0)


def order_kernel(per_seed, counts_rel, me, self_ids, neighbour_ids, count_one, lists):
    owners, seeds = counts_rel.shape
    fanout = neighbour_ids.shape[0]
    per_owner = count_one.shape[1] // owners
    half = owners // 2
    mine = me[0]
    counts = jnp.concatenate(
        [counts_rel[pl.ds(jnp.bitwise_xor(mine, c), 1), :] for c in range(owners)], axis=0
    ).astype(F32)
    needs = (counts + 1.0).astype(BF16)
    before = (iota((seeds, seeds), 0) < iota((seeds, seeds), 1)).astype(BF16)
    offset = jnp.dot(needs, before, preferred_element_type=F32)
    off_hi = jnp.floor(offset * (1.0 / 16.0))
    off_lo = offset - off_hi * 16.0
    shift = iota((seeds, per_owner), 1) - iota((seeds, per_owner), 0) * per_seed
    spread = ((shift >= 0) & (shift < per_seed)).astype(BF16)
    place = jnp.dot(iota((8, seeds), 1).astype(BF16), spread, preferred_element_type=F32)
    t = iota((owners, per_owner), 1).astype(F32) - place[0:1, :] * per_seed
    of_row = jnp.dot(counts.astype(BF16), spread, preferred_element_type=F32)
    row_hi = jnp.dot(off_hi.astype(BF16), spread, preferred_element_type=F32)
    row_lo = jnp.dot(off_lo.astype(BF16), spread, preferred_element_type=F32)
    slot = row_hi * 16.0 + row_lo + t
    used = (t <= of_row) & (slot < CAP)
    slot = slot.astype(I32)
    keys = [
        jnp.where(used[c : c + 1, :], count_one[:, c * per_owner : (c + 1) * per_owner], 0)
        for c in range(owners)
    ]
    kinds = [
        iota((16, per_owner), 0) == jnp.broadcast_to(key, (16, per_owner)) for key in keys
    ]
    stacked = jnp.concatenate([k.astype(F32).astype(BF16) for k in kinds], axis=0)
    left = (iota((per_owner, per_owner), 0) < iota((per_owner, per_owner), 1)).astype(BF16)
    prefix = jnp.dot(stacked, left, preferred_element_type=F32)
    total = jnp.dot(stacked, jnp.ones((per_owner, LANES), BF16), preferred_element_type=F32)
    for h in range(2):
        carry = jnp.zeros((16, LANES), F32)
        carries = []
        for c in range(h * half, (h + 1) * half):
            carries.append(carry)
            carry = carry + total[c * 16 : (c + 1) * 16, :]
        sizes = jnp.floor((carry + (UNROLL - 1)) * (1.0 / UNROLL)) * UNROLL
        bases = [jnp.zeros((1, LANES), F32)]
        for v in range(1, 16):
            bases.append(bases[-1] + sizes[v : v + 1, :])
        first = jnp.concatenate([bases[0]] + bases[:15], axis=0)
        sums = jnp.zeros((2 * (fanout + 2) * 16, LANES), F32)
        for i, c in enumerate(range(h * half, (h + 1) * half)):
            begin = (first + carries[i])[:, 0:1]
            spot = jnp.where(kinds[c], prefix[c * 16 : (c + 1) * 16, :] + begin, 0.0)
            spot = jnp.sum(spot, axis=0, keepdims=True).astype(I32)
            spot = jnp.where(keys[c] > 0, spot, -1)
            spot_lo = jnp.bitwise_and(spot, LANES - 1)
            spot_hi = jnp.right_shift(spot, 7)
            lane = (iota((LANES, per_owner), 0) == spot_lo).astype(F32).astype(BF16)
            at_hi = (iota((16, per_owner), 0) == spot_hi).astype(F32)
            columns = slice(c * per_owner, (c + 1) * per_owner)
            rows = [self_ids[:, columns]]
            rows += [neighbour_ids[k : k + 1, columns] for k in range(fanout)]
            rows += [half * CAP - (slot[c : c + 1, :] + i * CAP)]
            parts = []
            for row in rows:
                for byte in (jnp.right_shift(row, 8), jnp.bitwise_and(row, 255)):
                    value = jnp.broadcast_to(byte.astype(F32), (16, per_owner))
                    parts.append((at_hi * value).astype(BF16))
            sums = sums + lax.dot_general(
                jnp.concatenate(parts, axis=0),
                lane,
                (((1,), (1,)), ((), ())),
                preferred_element_type=F32,
            )
        for k in range(fanout + 2):
            hi = sums[32 * k : 32 * k + 16, :]
            lo = sums[32 * k + 16 : 32 * k + 32, :]
            value = (hi * 256.0 + lo).astype(I32)
            lists[h, k, :, :] = value if k <= fanout else half * CAP - value
        lane = iota((8, LANES), 1)
        begins = jnp.zeros((8, LANES), F32)
        for v in range(16):
            begins = begins + jnp.where(lane == v, bases[v], 0.0)
        lists[h, fanout + 2, 0:8, :] = begins.astype(I32)
        lists[h, fanout + 2, 8:16, :] = jnp.zeros((8, LANES), I32)


def list_copies(fanout, h, lists, ids, places, begins, sems):
    block = 16 * LANES

    def piece(k, length):
        at = pl.multiple_of((h * (fanout + 3) + k) * block, block)
        return lists.at[pl.ds(at, length)]

    copies = [
        pltpu.make_async_copy(piece(k, POSITIONS), ref, sems.at[k])
        for k, ref in enumerate(list(ids) + [places])
    ]
    last = fanout + 2
    return copies + [pltpu.make_async_copy(piece(last, LANES), begins, sems.at[last])]


def look_up(fanout, table, ids, places, begins, self_rows, mean_rows):
    for v in range(1, fanout + 1):
        begin = begins[v - 1]
        end = begins[v]

        def body(i, carry, v=v, begin=begin):
            for u in range(UNROLL):
                at = begin + i * UNROLL + u
                to = places[at]
                self_rows[pl.ds(to, 1), :] = table[pl.ds(ids[0][at], 1), :]
                total = tree_sum([table[pl.ds(ids[k][at], 1), :] for k in range(1, v + 1)])
                mean_rows[pl.ds(to, 1), :] = total * (1.0 / v)
            return carry

        lax.fori_loop(0, jnp.right_shift(end - begin, UNROLL.bit_length() - 1), body, 0)


def write_out(x, width, self_rows, mean_rows, keep, send):
    valid = iota((CAP, LANES), 1) < width
    for z in range(2):
        for ref, side in ((keep, x), (send, 1 - x)):
            at = pl.multiple_of((z * 2 + side) * CAP, CAP)
            for part, rows in enumerate((self_rows, mean_rows)):
                block = jnp.where(valid, rows[pl.ds(at, CAP), :], 0.0).astype(BF16)
                ref[z, :, part * LANES : (part + 1) * LANES] = block


def first_kernel(
    fanout, me, lists, features, other, weight, table, keep, send, *scratch
):
    ids = scratch[: fanout + 1]
    places, begins, self_rows, mean_rows, sems, staged, staged_sems = scratch[fanout + 1 :]
    width, length = other.shape
    x, h, rep = me[0], me[1], me[2]
    blocks, _, part = staged.shape
    stages = [
        pltpu.make_async_copy(
            features.at[:, pl.ds(b * part, part)], staged.at[b], staged_sems.at[b]
        )
        for b in range(blocks)
    ]
    start_all(stages)
    copies = list_copies(fanout, h, lists, ids, places, begins, sems)
    start_all(copies)
    self_rows[...] = jnp.zeros_like(self_rows)
    mean_rows[...] = jnp.zeros_like(mean_rows)
    turn(other, table, pl.multiple_of((1 - rep) * length, length))
    for b, stage in enumerate(stages):
        stage.wait()
        turn(staged.at[b], table, pl.multiple_of(rep * length + b * part, part))
    for copy in copies:
        copy.wait()
    look_up(fanout, table, ids, places, begins, self_rows, mean_rows)
    write_out(x, width, self_rows, mean_rows, keep, send)
    send[2, :, :] = weight[...]


def second_kernel(fanout, width, me, lists, table, keep_hbm, send_hbm, *scratch):
    ids = scratch[: fanout + 1]
    places, begins, self_rows, mean_rows, sems, keep, send, out_sems = scratch[fanout + 1 :]
    x, h = me[0], 1 - me[1]
    copies = list_copies(fanout, h, lists, ids, places, begins, sems)
    start_all(copies)
    self_rows[...] = jnp.zeros_like(self_rows)
    mean_rows[...] = jnp.zeros_like(mean_rows)
    for copy in copies:
        copy.wait()
    look_up(fanout, table, ids, places, begins, self_rows, mean_rows)
    write_out(x, width, self_rows, mean_rows, keep, send)
    outs = [
        pltpu.make_async_copy(send, send_hbm, out_sems.at[0]),
        pltpu.make_async_copy(keep, keep_hbm, out_sems.at[1]),
    ]
    start_all(outs)
    for copy in outs:
        copy.wait()


def project_kernel(me, keep, got, weight, weight_got, out_0, out_1):
    zl = me[3]
    theirs = weight_got[2]
    for which, out in ((zl, out_0), (1 - zl, out_1)):
        out[...] = (
            jnp.dot(keep[which], weight[...], preferred_element_type=F32)
            + jnp.dot(got[which], theirs, preferred_element_type=F32)
        ).astype(out.dtype)


def last_kernel(
    mine, a, b, c, counts, bias_one, self_two, neigh_two, bias_two, out_weight, out_bias, out
):
    pre = mine[...] + a[...].astype(F32) + b[...].astype(F32) + c[...].astype(F32)
    hidden = jnp.maximum(pre + bias_one[...], 0.0).astype(BF16)
    seeds = counts.shape[0]
    count = counts[...]
    earlier = (iota((seeds, seeds), 0) > iota((seeds, seeds), 1)).astype(BF16)
    needs = jnp.broadcast_to((count + 1).astype(F32), (seeds, LANES)).astype(BF16)
    offset = jnp.dot(earlier, needs, preferred_element_type=F32)[:, 0:1].astype(I32)
    place = iota((seeds, CAP), 1) - offset
    is_self = (place == 0).astype(F32).astype(BF16)
    is_near = ((place >= 1) & (place <= count)).astype(F32).astype(BF16)
    own = jnp.dot(is_self, hidden, preferred_element_type=F32).astype(BF16)
    total = jnp.dot(is_near, hidden, preferred_element_type=F32)
    mean = (total / count.astype(F32)).astype(BF16)
    pre_two = (
        jnp.dot(own, self_two[...], preferred_element_type=F32)
        + jnp.dot(mean, neigh_two[...], preferred_element_type=F32)
        + bias_two[...]
    )
    hidden_two = jnp.maximum(pre_two, 0.0).astype(BF16)
    out[...] = jnp.dot(hidden_two, out_weight[...], preferred_element_type=F32) + out_bias[...]


def params(limit):
    return pltpu.CompilerParams(vmem_limit_bytes=limit * MIB)


def shape(dims, dtype):
    return jax.ShapeDtypeStruct(dims, dtype)


def order_call(per_seed, counts_rel, col, self_ids, neighbour_ids, count_one):
    lists = pl.pallas_call(
        functools.partial(order_kernel, per_seed),
        out_shape=shape((2, neighbour_ids.shape[0] + 3, 16, LANES), I32),
        in_specs=[VMEM, SMEM, VMEM, VMEM, VMEM],
        out_specs=VMEM,
        compiler_params=params(10),
        name="order",
    )(counts_rel, col, self_ids, neighbour_ids, count_one)
    return lists.reshape(-1)


def list_scratch(fanout):
    return (
        [pltpu.SMEM((POSITIONS,), I32) for _ in range(fanout + 2)]
        + [pltpu.SMEM((LANES,), I32)]
        + [pltpu.VMEM((4 * CAP + 8, LANES), F32) for _ in range(2)]
        + [pltpu.SemaphoreType.DMA((fanout + 3,))]
    )


def first_call(fanout, me, lists, features, other, weight):
    return pl.pallas_call(
        functools.partial(first_kernel, fanout),
        out_shape=(
            shape((2 * features.shape[1], LANES), F32),
            shape((2, CAP, 2 * LANES), BF16),
            shape((3, CAP, 2 * LANES), BF16),
        ),
        in_specs=[SMEM, ANY, ANY, VMEM, VMEM],
        out_specs=(VMEM, VMEM, VMEM),
        scratch_shapes=list_scratch(fanout)
        + [
            pltpu.VMEM((4, features.shape[0], features.shape[1] // 4), BF16),
            pltpu.SemaphoreType.DMA((4,)),
        ],
        compiler_params=params(FIRST_MIB),
        name="first_half",
    )(me, lists, features, other, weight)


def second_call(fanout, width, me, lists, table):
    dims = (2, CAP, 2 * LANES)
    halves = pltpu.HBM(dims, BF16)
    return pl.pallas_call(
        functools.partial(second_kernel, fanout, width),
        out_shape=(halves, halves),
        in_specs=[SMEM, ANY, VMEM],
        out_specs=(HBM, HBM),
        scratch_shapes=list_scratch(fanout)
        + [pltpu.VMEM(dims, BF16) for _ in range(2)]
        + [pltpu.SemaphoreType.DMA((2,))],
        compiler_params=params(10),
        name="second_half",
    )(me, lists, table)


def project_call(me, keep, got, weight, weight_got, kinds):
    hidden = weight.shape[1]
    return pl.pallas_call(
        project_kernel,
        out_shape=tuple(shape((CAP, hidden), kind) for kind in kinds),
        in_specs=[SMEM, VMEM, VMEM, VMEM, VMEM],
        out_specs=(VMEM, VMEM),
        compiler_params=params(10),
        name="project",
    )(me, keep, got, weight, weight_got)


def last_call(*args):
    seeds = args[4].shape[0]
    classes = args[-1].shape[1]
    return pl.pallas_call(
        last_kernel,
        out_shape=shape((seeds, classes), F32),
        in_specs=[VMEM] * len(args),
        out_specs=VMEM,
        compiler_params=params(10),
        name="layer_two",
    )(*args)


def main(
    features,
    self_ids,
    neighbour_ids,
    count_one,
    count_two,
    self_one,
    neigh_one,
    bias_one,
    self_two,
    neigh_two,
    bias_two,
    out_weight,
    out_bias,
):
    owners = lax.axis_size("col")
    seeds = count_two.shape[0]
    per_owner = self_ids.shape[0] // owners
    per_seed = per_owner // seeds
    fanout = neighbour_ids.shape[0]
    width = features.shape[0]
    col = lax.axis_index("col")
    rep = lax.axis_index("rep")
    z = col // 2
    me = jnp.stack([col % 2, 1 - z // 2, rep, z % 2]).astype(I32)

    def across(value, bit):
        return lax.ppermute(value, "col", [(i, i ^ bit) for i in range(owners)])

    def swapped(value):
        return lax.ppermute(value, "rep", [(0, 1), (1, 0)])

    other = swapped(features)
    weight = jnp.concatenate(
        [jnp.pad(w, ((0, LANES - width), (0, 0))) for w in (self_one, neigh_one)], axis=0
    )
    counts = count_two[None, :]
    for bit in (1, 2, 4):
        counts = jnp.concatenate([counts, across(counts, bit)], axis=0)
    lists = order_call(
        per_seed,
        counts,
        col.reshape(1).astype(I32),
        self_ids[None, :],
        neighbour_ids,
        count_one[None, :],
    )
    table, keep_far, send_far = first_call(fanout, me, lists, features, other, weight)
    got_far = across(send_far, 1)
    keep_near, send_near = second_call(fanout, width, me, lists, table)
    far = project_call(me, keep_far, got_far, weight, got_far, (BF16, BF16))
    got_near = across(send_near, 1)
    got = [across(far[0], 4), across(far[1], 6)]
    near = project_call(me, keep_near, got_near, weight, got_far, (F32, BF16))
    got.append(across(near[1], 2))
    fast = last_call(
        near[0],
        *got,
        count_two[:, None],
        bias_one[None, :],
        self_two,
        neigh_two,
        bias_two[None, :],
        out_weight,
        out_bias[None, :],
    )
    most = jnp.max(jnp.sum(counts + 1, axis=1)).reshape(1)
    most = jnp.maximum(most, swapped(most))
    most = jnp.maximum(most, lax.ppermute(most, "groups", [(0, 1), (1, 0)]))
    return lax.cond(
        most[0] > CAP,
        lambda: general(
            other,
            features,
            self_ids,
            neighbour_ids,
            count_one,
            count_two,
            self_one,
            neigh_one,
            bias_one,
            self_two,
            neigh_two,
            bias_two,
            out_weight,
            out_bias,
        ),
        lambda: fast,
    )


def local(*args):
    features, self_ids, neighbour_ids = args[0], args[1], args[2]
    sizes = (lax.axis_size("groups"), lax.axis_size("col"), lax.axis_size("rep"))
    small = (
        sizes == (2, 8, 2)
        and features.shape[0] <= LANES
        and features.shape[1] <= 32768
        and self_ids.shape[0] * (neighbour_ids.shape[0] + 1) <= 2**17
        and neighbour_ids.shape[0] <= 15
    )
    if small:
        return main(*args)
    return general(lax.ppermute(features, "rep", [(0, 1), (1, 0)]), *args)


def solution(mesh):
    placed = (
        P("col", ("groups", "rep")),
        P(("groups", "rep")),
        P(None, ("groups", "rep")),
        P(("groups", "rep")),
        P(("groups", "col", "rep")),
        P("col", None),
        P("col", None),
        P(),
        P(),
        P(),
        P(),
        P(),
        P(),
    )
    return jax.shard_map(
        local,
        mesh=mesh,
        in_specs=placed,
        out_specs=P(("groups", "col", "rep"), None),
        check_vma=False,
    )
```

```python
import functools

import jax
import jax.numpy as jnp
import numpy as np
from jax import lax
from jax.experimental import pallas as pl
from jax.experimental.pallas import tpu as pltpu
from jax.sharding import PartitionSpec as P

CAP = 272
UNROLL = 8
POSITIONS = 10 * 128
FIRST_MIB = 18
LANES = 128
MIB = 2**20
BF16 = jnp.bfloat16
F32 = jnp.float32
I32 = jnp.int32


def gathered(value, axis):
    copies = jnp.broadcast_to(value[None], (lax.axis_size(axis),) + value.shape)
    pieces = lax.all_to_all(copies, axis, split_axis=0, concat_axis=0, tiled=True)
    return pieces.reshape((-1,) + value.shape[1:])


def general(
    other,
    features,
    self_ids,
    neighbour_ids,
    count_one,
    count_two,
    self_one,
    neigh_one,
    bias_one,
    self_two,
    neigh_two,
    bias_two,
    out_weight,
    out_bias,
):
    mine = jnp.where(lax.axis_index("rep") == 0, 0, 1)
    table_cols = jnp.where(
        mine == 0,
        jnp.concatenate([features, other], axis=1),
        jnp.concatenate([other, features], axis=1),
    )
    table_rows = table_cols.T
    blocks = lax.axis_size("col")
    total_rows = self_ids.shape[0]
    per_owner = total_rows // blocks
    fanout = neighbour_ids.shape[0]
    width = table_rows.shape[1]
    all_ids = jnp.concatenate([self_ids[None, :], neighbour_ids], axis=0)
    fetched = jnp.take(table_rows, all_ids, axis=0)
    self_x = fetched[0]
    mask = (jnp.arange(fanout)[:, None] < count_one[None, :]).astype(BF16)
    summed = jnp.einsum("kmc,km->mc", fetched[1:], mask, preferred_element_type=F32)
    mean_one = (summed / count_one[:, None].astype(F32)).astype(BF16)
    full_self, full_neigh = gathered(self_one, "col"), gathered(neigh_one, "col")
    stacked = jnp.stack([self_x, mean_one], axis=0).reshape(2, blocks, per_owner, width)
    pieces = lax.all_to_all(stacked, "col", split_axis=1, concat_axis=3, tiled=True)
    pre_one = jnp.dot(pieces[0, 0], full_self, preferred_element_type=F32) + jnp.dot(
        pieces[1, 0], full_neigh, preferred_element_type=F32
    )
    hidden_one = jax.nn.relu(pre_one + bias_one).astype(BF16)
    seeds = count_two.shape[0]
    hidden = hidden_one.shape[1]
    grouped = hidden_one.reshape(seeds, per_owner // seeds, hidden)
    mask_two = (jnp.arange(grouped.shape[1] - 1)[None, :] < count_two[:, None]).astype(BF16)
    summed_two = jnp.einsum("skh,sk->sh", grouped[:, 1:, :], mask_two, preferred_element_type=F32)
    mean_two = (summed_two / count_two[:, None].astype(F32)).astype(BF16)
    pre_two = jnp.dot(grouped[:, 0, :], self_two, preferred_element_type=F32) + jnp.dot(
        mean_two, neigh_two, preferred_element_type=F32
    )
    hidden_two = jax.nn.relu(pre_two + bias_two).astype(BF16)
    return jnp.dot(hidden_two, out_weight, preferred_element_type=F32) + out_bias


def iota(shape, dim):
    return lax.broadcasted_iota(I32, shape, dim)


def tree_sum(terms):
    while len(terms) > 1:
        odd = [terms[-1]] if len(terms) % 2 else []
        terms = [a + b for a, b in zip(terms[::2], terms[1::2])] + odd
    return terms[0]


VMEM = pl.BlockSpec(memory_space=pltpu.VMEM)
SMEM = pl.BlockSpec(memory_space=pltpu.SMEM)
HBM = pl.BlockSpec(memory_space=pltpu.HBM)
ANY = pl.BlockSpec(memory_space=pl.ANY)


def start_all(copies):
    for copy in copies:
        copy.start()


def turn(source, table, base):
    width, length = source.shape
    step = 512
    unroll = 4

    def body(i, carry):
        for u in range(unroll):
            off = pl.multiple_of((i * unroll + u) * step, step)
            rows = source[:, pl.ds(off, step)].T.astype(F32)
            table[pl.ds(pl.multiple_of(base + off, step), step), 0:width] = rows
        return carry

    lax.fori_loop(0, length // step // unroll, body, 0)


def order_kernel(
    per_seed, me, own, got_1, got_2, got_4, self_ids, neighbour_ids, count_one, lists, counts_rel
):
    owners, seeds = counts_rel.shape
    fanout = neighbour_ids.shape[0]
    per_owner = count_one.shape[0] // owners
    half = owners // 2
    mine = me[4]
    counts_rel[0:1, :] = own[...]
    counts_rel[1:2, :] = got_1[...]
    counts_rel[2:4, :] = got_2[...]
    counts_rel[4:8, :] = got_4[...]
    own_ids = self_ids[...].reshape(1, owners * per_owner)
    ones = count_one[...].reshape(1, owners * per_owner)
    counts = jnp.concatenate(
        [counts_rel[pl.ds(jnp.bitwise_xor(mine, c), 1), :] for c in range(owners)], axis=0
    ).astype(F32)
    needs = (counts + 1.0).astype(BF16)
    before = (iota((seeds, seeds), 0) < iota((seeds, seeds), 1)).astype(BF16)
    offset = jnp.dot(needs, before, preferred_element_type=F32)
    off_hi = jnp.floor(offset * (1.0 / 16.0))
    off_lo = offset - off_hi * 16.0
    shift = iota((seeds, per_owner), 1) - iota((seeds, per_owner), 0) * per_seed
    spread = ((shift >= 0) & (shift < per_seed)).astype(BF16)
    place = jnp.dot(iota((8, seeds), 1).astype(BF16), spread, preferred_element_type=F32)
    t = iota((owners, per_owner), 1).astype(F32) - place[0:1, :] * per_seed
    of_row = jnp.dot(counts.astype(BF16), spread, preferred_element_type=F32)
    row_hi = jnp.dot(off_hi.astype(BF16), spread, preferred_element_type=F32)
    row_lo = jnp.dot(off_lo.astype(BF16), spread, preferred_element_type=F32)
    slot = row_hi * 16.0 + row_lo + t
    used = (t <= of_row) & (slot < CAP)
    slot = slot.astype(I32)
    keys = [
        jnp.where(used[c : c + 1, :], ones[:, c * per_owner : (c + 1) * per_owner], 0)
        for c in range(owners)
    ]
    kinds = [
        iota((16, per_owner), 0) == jnp.broadcast_to(key, (16, per_owner)) for key in keys
    ]
    stacked = jnp.concatenate([k.astype(F32).astype(BF16) for k in kinds], axis=0)
    left = (iota((per_owner, per_owner), 0) < iota((per_owner, per_owner), 1)).astype(BF16)
    prefix = jnp.dot(stacked, left, preferred_element_type=F32)
    total = jnp.dot(stacked, jnp.ones((per_owner, LANES), BF16), preferred_element_type=F32)
    for h in range(2):
        carry = jnp.zeros((16, LANES), F32)
        carries = []
        for c in range(h * half, (h + 1) * half):
            carries.append(carry)
            carry = carry + total[c * 16 : (c + 1) * 16, :]
        sizes = jnp.floor((carry + (UNROLL - 1)) * (1.0 / UNROLL)) * UNROLL
        bases = [jnp.zeros((1, LANES), F32)]
        for v in range(1, 16):
            bases.append(bases[-1] + sizes[v : v + 1, :])
        first = jnp.concatenate([bases[0]] + bases[:15], axis=0)
        sums = jnp.zeros((2 * (fanout + 2) * 16, LANES), F32)
        for i, c in enumerate(range(h * half, (h + 1) * half)):
            begin = (first + carries[i])[:, 0:1]
            spot = jnp.where(kinds[c], prefix[c * 16 : (c + 1) * 16, :] + begin, 0.0)
            spot = jnp.sum(spot, axis=0, keepdims=True).astype(I32)
            spot = jnp.where(keys[c] > 0, spot, -1)
            spot_lo = jnp.bitwise_and(spot, LANES - 1)
            spot_hi = jnp.right_shift(spot, 7)
            lane = (iota((LANES, per_owner), 0) == spot_lo).astype(F32).astype(BF16)
            at_hi = (iota((16, per_owner), 0) == spot_hi).astype(F32)
            columns = slice(c * per_owner, (c + 1) * per_owner)
            rows = [own_ids[:, columns]]
            rows += [neighbour_ids[k : k + 1, columns] for k in range(fanout)]
            rows += [half * CAP - (slot[c : c + 1, :] + i * CAP)]
            parts = []
            for row in rows:
                for byte in (jnp.right_shift(row, 8), jnp.bitwise_and(row, 255)):
                    value = jnp.broadcast_to(byte.astype(F32), (16, per_owner))
                    parts.append((at_hi * value).astype(BF16))
            sums = sums + lax.dot_general(
                jnp.concatenate(parts, axis=0),
                lane,
                (((1,), (1,)), ((), ())),
                preferred_element_type=F32,
            )
        for k in range(fanout + 2):
            hi = sums[32 * k : 32 * k + 16, :]
            lo = sums[32 * k + 16 : 32 * k + 32, :]
            value = (hi * 256.0 + lo).astype(I32)
            lists[h, k, :, :] = value if k <= fanout else half * CAP - value
        lane = iota((8, LANES), 1)
        begins = jnp.zeros((8, LANES), F32)
        for v in range(16):
            begins = begins + jnp.where(lane == v, bases[v], 0.0)
        lists[h, fanout + 2, 0:8, :] = begins.astype(I32)
        lists[h, fanout + 2, 8:16, :] = jnp.zeros((8, LANES), I32)


def list_copies(fanout, h, lists, ids, places, begins, sems):
    block = 16 * LANES

    def piece(k, length):
        at = pl.multiple_of((h * (fanout + 3) + k) * block, block)
        return lists.at[pl.ds(at, length)]

    last = fanout + 2
    copies = [
        pltpu.make_async_copy(piece(k, POSITIONS), ref, sems.at[k])
        for k, ref in enumerate(list(ids) + [places])
    ]
    copies.append(pltpu.make_async_copy(piece(last, LANES), begins, sems.at[last]))
    start_all(copies[fanout + 1 :] + copies[: fanout + 1])
    return copies


def look_up(fanout, copies, table, ids, places, begins, self_rows, mean_rows):
    for copy in [copies[0]] + copies[fanout + 1 :]:
        copy.wait()
    for v in range(1, fanout + 1):
        copies[v].wait()
        begin = begins[v - 1]
        end = begins[v]

        def body(i, carry, v=v, begin=begin):
            for u in range(UNROLL):
                at = begin + i * UNROLL + u
                to = places[at]
                self_rows[pl.ds(to, 1), :] = table[pl.ds(ids[0][at], 1), :]
                total = tree_sum([table[pl.ds(ids[k][at], 1), :] for k in range(1, v + 1)])
                mean_rows[pl.ds(to, 1), :] = total * (1.0 / v)
            return carry

        lax.fori_loop(0, jnp.right_shift(end - begin, UNROLL.bit_length() - 1), body, 0)


def write_out(x, width, self_rows, mean_rows, keep, send):
    valid = iota((CAP, LANES), 1) < width
    for z in range(2):
        for ref, side in ((keep, x), (send, 1 - x)):
            at = pl.multiple_of((z * 2 + side) * CAP, CAP)
            for part, rows in enumerate((self_rows, mean_rows)):
                block = jnp.where(valid, rows[pl.ds(at, CAP), :], 0.0).astype(BF16)
                ref[z, :, part * LANES : (part + 1) * LANES] = block


def stage(source, staged, sems):
    blocks, _, part = staged.shape
    copies = [
        pltpu.make_async_copy(source.at[:, pl.ds(b * part, part)], staged.at[b], sems.at[b])
        for b in range(blocks)
    ]
    start_all(copies)
    return copies


def first_kernel(
    fanout, me, lists, features, other, self_one, neigh_one, table, keep, send, *scratch
):
    ids = scratch[: fanout + 1]
    places, begins, self_rows, mean_rows, sems = scratch[fanout + 1 : -4]
    staged_0, sems_0, staged_1, sems_1 = scratch[-4:]
    width, length = other.shape
    x, h, rep = me[0], me[1], me[2]
    stages = [
        (stage(features, staged_0, sems_0), staged_0, rep * length),
        (stage(other, staged_1, sems_1), staged_1, (1 - rep) * length),
    ]
    copies = list_copies(fanout, h, lists, ids, places, begins, sems)
    self_rows[...] = jnp.zeros_like(self_rows)
    mean_rows[...] = jnp.zeros_like(mean_rows)
    send[2, :, :] = jnp.zeros(send.shape[1:], BF16)
    send[2, 0:width, :] = self_one[...]
    send[2, LANES : LANES + width, :] = neigh_one[...]
    for parts, staged, base in stages:
        length_of = staged.shape[2]
        for b, part in enumerate(parts):
            part.wait()
            turn(staged.at[b], table, pl.multiple_of(base + b * length_of, length_of))
    look_up(fanout, copies, table, ids, places, begins, self_rows, mean_rows)
    write_out(x, width, self_rows, mean_rows, keep, send)


def second_kernel(fanout, width, me, lists, table, keep_hbm, send_hbm, *scratch):
    ids = scratch[: fanout + 1]
    places, begins, self_rows, mean_rows, sems, keep, send, out_sems = scratch[fanout + 1 :]
    x, h = me[0], 1 - me[1]
    copies = list_copies(fanout, h, lists, ids, places, begins, sems)
    self_rows[...] = jnp.zeros_like(self_rows)
    mean_rows[...] = jnp.zeros_like(mean_rows)
    look_up(fanout, copies, table, ids, places, begins, self_rows, mean_rows)
    write_out(x, width, self_rows, mean_rows, keep, send)
    outs = [
        pltpu.make_async_copy(send, send_hbm, out_sems.at[0]),
        pltpu.make_async_copy(keep, keep_hbm, out_sems.at[1]),
    ]
    start_all(outs)
    for copy in outs:
        copy.wait()


def project(zl, keep, got, weight, weight_got, outs):
    for which, out in ((zl, outs[0]), (1 - zl, outs[1])):
        out[...] = (
            jnp.dot(keep[which], weight[2, 0 : 2 * LANES, :], preferred_element_type=F32)
            + jnp.dot(got[which], weight_got[2, 0 : 2 * LANES, :], preferred_element_type=F32)
        ).astype(out.dtype)


def project_far_kernel(me, keep, got, sent, later, out_0, out_1, loaded, sem):
    copy = pltpu.make_async_copy(later, loaded, sem)
    copy.start()
    project(me[3], keep, got, sent, got, (out_0, out_1))
    copy.wait()


def project_near_kernel(me, keep, got, weight, weight_got, out_0, out_1):
    project(me[3], keep, got, weight, weight_got, (out_0, out_1))


def last_kernel(
    mine, a, b, c, counts, bias_one, self_two, neigh_two, bias_two, out_weight, out_bias, out
):
    pre = mine[...] + a[...].astype(F32) + b[...].astype(F32) + c[...].astype(F32)
    hidden = jnp.maximum(pre + bias_one[...], 0.0).astype(BF16)
    seeds = counts.shape[0]
    count = counts[...]
    earlier = (iota((seeds, seeds), 0) > iota((seeds, seeds), 1)).astype(BF16)
    needs = jnp.broadcast_to((count + 1).astype(F32), (seeds, LANES)).astype(BF16)
    offset = jnp.dot(earlier, needs, preferred_element_type=F32)[:, 0:1].astype(I32)
    place = iota((seeds, CAP), 1) - offset
    is_self = (place == 0).astype(F32).astype(BF16)
    is_near = ((place >= 1) & (place <= count)).astype(F32).astype(BF16)
    own = jnp.dot(is_self, hidden, preferred_element_type=F32).astype(BF16)
    total = jnp.dot(is_near, hidden, preferred_element_type=F32)
    mean = (total / count.astype(F32)).astype(BF16)
    pre_two = (
        jnp.dot(own, self_two[...], preferred_element_type=F32)
        + jnp.dot(mean, neigh_two[...], preferred_element_type=F32)
        + bias_two[...]
    )
    hidden_two = jnp.maximum(pre_two, 0.0).astype(BF16)
    out[...] = jnp.dot(hidden_two, out_weight[...], preferred_element_type=F32) + out_bias[...]


def params(limit):
    return pltpu.CompilerParams(vmem_limit_bytes=limit * MIB)


def shape(dims, dtype):
    return jax.ShapeDtypeStruct(dims, dtype)


def order_call(per_seed, me, own, got, self_ids, neighbour_ids, count_one):
    owners = sum(x.shape[0] for x in (own, *got))
    lists = pl.pallas_call(
        functools.partial(order_kernel, per_seed),
        out_shape=shape((2, neighbour_ids.shape[0] + 3, 16, LANES), I32),
        in_specs=[SMEM] + [VMEM] * 7,
        out_specs=VMEM,
        scratch_shapes=[pltpu.VMEM((owners, own.shape[1]), I32)],
        compiler_params=params(10),
        name="order",
    )(me, own, *got, self_ids, neighbour_ids, count_one)
    return lists.reshape(-1)


def list_scratch(fanout):
    return (
        [pltpu.SMEM((POSITIONS,), I32) for _ in range(fanout + 2)]
        + [pltpu.SMEM((LANES,), I32)]
        + [pltpu.VMEM((4 * CAP + 8, LANES), F32) for _ in range(2)]
        + [pltpu.SemaphoreType.DMA((fanout + 3,))]
    )


def first_call(fanout, me, lists, features, other, self_one, neigh_one):
    width, length = features.shape
    staging = [pltpu.VMEM((4, width, length // 4), BF16), pltpu.SemaphoreType.DMA((4,))]
    return pl.pallas_call(
        functools.partial(first_kernel, fanout),
        out_shape=(
            shape((2 * length, LANES), F32),
            shape((2, CAP, 2 * LANES), BF16),
            shape((3, CAP, 2 * LANES), BF16),
        ),
        in_specs=[SMEM, ANY, ANY, ANY, VMEM, VMEM],
        out_specs=(VMEM, VMEM, VMEM),
        scratch_shapes=list_scratch(fanout) + staging + staging,
        compiler_params=params(FIRST_MIB),
        name="first_half",
    )(me, lists, features, other, self_one, neigh_one)


def second_call(fanout, width, me, lists, table):
    dims = (2, CAP, 2 * LANES)
    halves = pltpu.HBM(dims, BF16)
    return pl.pallas_call(
        functools.partial(second_kernel, fanout, width),
        out_shape=(halves, halves),
        in_specs=[SMEM, ANY, VMEM],
        out_specs=(HBM, HBM),
        scratch_shapes=list_scratch(fanout)
        + [pltpu.VMEM(dims, BF16) for _ in range(2)]
        + [pltpu.SemaphoreType.DMA((2,))],
        compiler_params=params(10),
        name="second_half",
    )(me, lists, table)


def project_far_call(me, keep, got, sent, later):
    part = shape((CAP, sent.shape[2]), BF16)
    return pl.pallas_call(
        project_far_kernel,
        out_shape=(part, part, shape(later.shape, BF16)),
        in_specs=[SMEM, VMEM, VMEM, VMEM, ANY],
        out_specs=(VMEM, VMEM, VMEM),
        scratch_shapes=[pltpu.SemaphoreType.DMA],
        compiler_params=params(10),
        name="project_far",
    )(me, keep, got, sent, later)


def project_near_call(me, keep, got, weight, weight_got):
    dims = (CAP, weight.shape[2])
    return pl.pallas_call(
        project_near_kernel,
        out_shape=(shape(dims, F32), shape(dims, BF16)),
        in_specs=[SMEM, VMEM, VMEM, VMEM, VMEM],
        out_specs=(VMEM, VMEM),
        compiler_params=params(10),
        name="project_near",
    )(me, keep, got, weight, weight_got)


def last_call(*args):
    seeds = args[4].shape[0]
    classes = args[-1].shape[1]
    return pl.pallas_call(
        last_kernel,
        out_shape=shape((seeds, classes), F32),
        in_specs=[VMEM] * len(args),
        out_specs=VMEM,
        compiler_params=params(10),
        name="layer_two",
    )(*args)


def main(
    features,
    self_ids,
    neighbour_ids,
    count_one,
    count_two,
    self_one,
    neigh_one,
    bias_one,
    self_two,
    neigh_two,
    bias_two,
    out_weight,
    out_bias,
):
    owners = lax.axis_size("col")
    seeds = count_two.shape[0]
    per_owner = self_ids.shape[0] // owners
    per_seed = per_owner // seeds
    fanout = neighbour_ids.shape[0]
    width = features.shape[0]
    col = lax.axis_index("col")
    rep = lax.axis_index("rep")
    z = col // 2
    me = jnp.stack([col % 2, 1 - z // 2, rep, z % 2, col]).astype(I32)

    def across(value, bit):
        return lax.ppermute(value, "col", [(i, i ^ bit) for i in range(owners)])

    other = lax.ppermute(features, "rep", [(0, 1), (1, 0)])
    own = count_two[None, :]
    got_1 = across(own, 1)
    got_2 = across(jnp.concatenate([own, got_1], axis=0), 2)
    got_4 = across(jnp.concatenate([own, got_1, got_2], axis=0), 4)
    got = (got_1, got_2, got_4)
    lists = order_call(per_seed, me, own, got, self_ids, neighbour_ids, count_one)
    table, keep_far, send_far = first_call(
        fanout, me, lists, features, other, self_one, neigh_one
    )
    got_far = across(send_far, 1)
    keep_near, send_near = second_call(fanout, width, me, lists, table)
    got_near = across(send_near, 1)
    far_0, far_1, keep_near = project_far_call(me, keep_far, got_far, send_far, keep_near)
    far = [across(far_0, 4), across(far_1, 6)]
    near_0, near_1 = project_near_call(me, keep_near, got_near, send_far, got_far)
    far.append(across(near_1, 2))
    fast = last_call(
        near_0,
        *far,
        count_two[:, None],
        bias_one[None, :],
        self_two,
        neigh_two,
        bias_two[None, :],
        out_weight,
        out_bias[None, :],
    )
    most = functools.reduce(jnp.maximum, [jnp.max(jnp.sum(x + 1, axis=1)) for x in (own, *got)])
    return lax.cond(
        most > CAP,
        lambda: general(
            other,
            features,
            self_ids,
            neighbour_ids,
            count_one,
            count_two,
            self_one,
            neigh_one,
            bias_one,
            self_two,
            neigh_two,
            bias_two,
            out_weight,
            out_bias,
        ),
        lambda: fast,
    )


def local(*args):
    features, self_ids, neighbour_ids = args[0], args[1], args[2]
    sizes = (lax.axis_size("groups"), lax.axis_size("col"), lax.axis_size("rep"))
    small = (
        sizes == (2, 8, 2)
        and features.shape[0] <= LANES
        and features.shape[1] <= 32768
        and self_ids.shape[0] * (neighbour_ids.shape[0] + 1) <= 2**17
        and neighbour_ids.shape[0] <= 15
    )
    if small:
        return main(*args)
    return general(lax.ppermute(features, "rep", [(0, 1), (1, 0)]), *args)


def solution(mesh):
    placed = (
        P("col", ("groups", "rep")),
        P(("groups", "rep")),
        P(None, ("groups", "rep")),
        P(("groups", "rep")),
        P(("groups", "col", "rep")),
        P("col", None),
        P("col", None),
        P(),
        P(),
        P(),
        P(),
        P(),
        P(),
    )
    return jax.shard_map(
        local,
        mesh=mesh,
        in_specs=placed,
        out_specs=P(("groups", "col", "rep"), None),
        check_vma=False,
    )
```

```python
import functools

import jax
import jax.numpy as jnp
import numpy as np
from jax import lax
from jax.experimental import pallas as pl
from jax.experimental.pallas import tpu as pltpu
from jax.sharding import PartitionSpec as P

CAP = 272
UNROLL = 8
POSITIONS = 10 * 128
FIRST_MIB = 12
LANES = 128
MIB = 2**20
BF16 = jnp.bfloat16
F32 = jnp.float32
I32 = jnp.int32


def gathered(value, axis):
    copies = jnp.broadcast_to(value[None], (lax.axis_size(axis),) + value.shape)
    pieces = lax.all_to_all(copies, axis, split_axis=0, concat_axis=0, tiled=True)
    return pieces.reshape((-1,) + value.shape[1:])


def general(
    other,
    features,
    self_ids,
    neighbour_ids,
    count_one,
    count_two,
    self_one,
    neigh_one,
    bias_one,
    self_two,
    neigh_two,
    bias_two,
    out_weight,
    out_bias,
):
    mine = jnp.where(lax.axis_index("rep") == 0, 0, 1)
    table_cols = jnp.where(
        mine == 0,
        jnp.concatenate([features, other], axis=1),
        jnp.concatenate([other, features], axis=1),
    )
    table_rows = table_cols.T
    blocks = lax.axis_size("col")
    total_rows = self_ids.shape[0]
    per_owner = total_rows // blocks
    fanout = neighbour_ids.shape[0]
    width = table_rows.shape[1]
    all_ids = jnp.concatenate([self_ids[None, :], neighbour_ids], axis=0)
    fetched = jnp.take(table_rows, all_ids, axis=0)
    self_x = fetched[0]
    mask = (jnp.arange(fanout)[:, None] < count_one[None, :]).astype(BF16)
    summed = jnp.einsum("kmc,km->mc", fetched[1:], mask, preferred_element_type=F32)
    mean_one = (summed / count_one[:, None].astype(F32)).astype(BF16)
    full_self, full_neigh = gathered(self_one, "col"), gathered(neigh_one, "col")
    stacked = jnp.stack([self_x, mean_one], axis=0).reshape(2, blocks, per_owner, width)
    pieces = lax.all_to_all(stacked, "col", split_axis=1, concat_axis=3, tiled=True)
    pre_one = jnp.dot(pieces[0, 0], full_self, preferred_element_type=F32) + jnp.dot(
        pieces[1, 0], full_neigh, preferred_element_type=F32
    )
    hidden_one = jax.nn.relu(pre_one + bias_one).astype(BF16)
    seeds = count_two.shape[0]
    hidden = hidden_one.shape[1]
    grouped = hidden_one.reshape(seeds, per_owner // seeds, hidden)
    mask_two = (jnp.arange(grouped.shape[1] - 1)[None, :] < count_two[:, None]).astype(BF16)
    summed_two = jnp.einsum("skh,sk->sh", grouped[:, 1:, :], mask_two, preferred_element_type=F32)
    mean_two = (summed_two / count_two[:, None].astype(F32)).astype(BF16)
    pre_two = jnp.dot(grouped[:, 0, :], self_two, preferred_element_type=F32) + jnp.dot(
        mean_two, neigh_two, preferred_element_type=F32
    )
    hidden_two = jax.nn.relu(pre_two + bias_two).astype(BF16)
    return jnp.dot(hidden_two, out_weight, preferred_element_type=F32) + out_bias


def iota(shape, dim):
    return lax.broadcasted_iota(I32, shape, dim)


def tree_sum(terms):
    while len(terms) > 1:
        odd = [terms[-1]] if len(terms) % 2 else []
        terms = [a + b for a, b in zip(terms[::2], terms[1::2])] + odd
    return terms[0]


VMEM = pl.BlockSpec(memory_space=pltpu.VMEM)
SMEM = pl.BlockSpec(memory_space=pltpu.SMEM)
HBM = pl.BlockSpec(memory_space=pltpu.HBM)
ANY = pl.BlockSpec(memory_space=pl.ANY)


def start_all(copies):
    for copy in copies:
        copy.start()


def turn(source, table, base):
    width, length = source.shape
    step = 512
    unroll = 4

    def body(i, carry):
        for u in range(unroll):
            off = pl.multiple_of((i * unroll + u) * step, step)
            rows = source[:, pl.ds(off, step)].T.astype(F32)
            table[pl.ds(pl.multiple_of(base + off, step), step), 0:width] = rows
        return carry

    lax.fori_loop(0, length // step // unroll, body, 0)


def order_kernel(
    per_seed, me, own, got_1, got_2, got_4, self_ids, neighbour_ids, count_one, lists, most, counts_rel
):
    owners, seeds = counts_rel.shape
    fanout = neighbour_ids.shape[0]
    per_owner = count_one.shape[0] // owners
    half = owners // 2
    mine = me[4]
    counts_rel[0:1, :] = own[...]
    counts_rel[1:2, :] = got_1[...]
    counts_rel[2:4, :] = got_2[...]
    counts_rel[4:8, :] = got_4[...]
    own_ids = self_ids[...].reshape(1, owners * per_owner)
    ones = count_one[...].reshape(1, owners * per_owner)
    counts = jnp.concatenate(
        [counts_rel[pl.ds(jnp.bitwise_xor(mine, c), 1), :] for c in range(owners)], axis=0
    ).astype(F32)
    needs = (counts + 1.0).astype(BF16)
    most[0] = jnp.max(jnp.sum(counts + 1.0, axis=1, keepdims=True)).astype(I32)
    before = (iota((seeds, seeds), 0) < iota((seeds, seeds), 1)).astype(BF16)
    offset = jnp.dot(needs, before, preferred_element_type=F32)
    off_hi = jnp.floor(offset * (1.0 / 16.0))
    off_lo = offset - off_hi * 16.0
    shift = iota((seeds, per_owner), 1) - iota((seeds, per_owner), 0) * per_seed
    spread = ((shift >= 0) & (shift < per_seed)).astype(BF16)
    place = jnp.dot(iota((8, seeds), 1).astype(BF16), spread, preferred_element_type=F32)
    t = iota((owners, per_owner), 1).astype(F32) - place[0:1, :] * per_seed
    of_row = jnp.dot(counts.astype(BF16), spread, preferred_element_type=F32)
    row_hi = jnp.dot(off_hi.astype(BF16), spread, preferred_element_type=F32)
    row_lo = jnp.dot(off_lo.astype(BF16), spread, preferred_element_type=F32)
    slot = row_hi * 16.0 + row_lo + t
    used = (t <= of_row) & (slot < CAP)
    slot = slot.astype(I32)
    keys = [
        jnp.where(used[c : c + 1, :], ones[:, c * per_owner : (c + 1) * per_owner], 0)
        for c in range(owners)
    ]
    kinds = [
        iota((16, per_owner), 0) == jnp.broadcast_to(key, (16, per_owner)) for key in keys
    ]
    stacked = jnp.concatenate([k.astype(F32).astype(BF16) for k in kinds], axis=0)
    left = (iota((per_owner, per_owner), 0) < iota((per_owner, per_owner), 1)).astype(BF16)
    prefix = jnp.dot(stacked, left, preferred_element_type=F32)
    total = jnp.dot(stacked, jnp.ones((per_owner, LANES), BF16), preferred_element_type=F32)
    for h in range(2):
        carry = jnp.zeros((16, LANES), F32)
        carries = []
        for c in range(h * half, (h + 1) * half):
            carries.append(carry)
            carry = carry + total[c * 16 : (c + 1) * 16, :]
        sizes = jnp.floor((carry + (UNROLL - 1)) * (1.0 / UNROLL)) * UNROLL
        bases = [jnp.zeros((1, LANES), F32)]
        for v in range(1, 16):
            bases.append(bases[-1] + sizes[v : v + 1, :])
        first = jnp.concatenate([bases[0]] + bases[:15], axis=0)
        sums = jnp.zeros((2 * (fanout + 2) * 16, LANES), F32)
        for i, c in enumerate(range(h * half, (h + 1) * half)):
            begin = (first + carries[i])[:, 0:1]
            spot = jnp.where(kinds[c], prefix[c * 16 : (c + 1) * 16, :] + begin, 0.0)
            spot = jnp.sum(spot, axis=0, keepdims=True).astype(I32)
            spot = jnp.where(keys[c] > 0, spot, -1)
            spot_lo = jnp.bitwise_and(spot, LANES - 1)
            spot_hi = jnp.right_shift(spot, 7)
            lane = (iota((LANES, per_owner), 0) == spot_lo).astype(F32).astype(BF16)
            at_hi = (iota((16, per_owner), 0) == spot_hi).astype(F32)
            columns = slice(c * per_owner, (c + 1) * per_owner)
            rows = [own_ids[:, columns]]
            rows += [neighbour_ids[k : k + 1, columns] for k in range(fanout)]
            rows += [half * CAP - (slot[c : c + 1, :] + i * CAP)]
            parts = []
            for row in rows:
                for byte in (jnp.right_shift(row, 8), jnp.bitwise_and(row, 255)):
                    value = jnp.broadcast_to(byte.astype(F32), (16, per_owner))
                    parts.append((at_hi * value).astype(BF16))
            sums = sums + lax.dot_general(
                jnp.concatenate(parts, axis=0),
                lane,
                (((1,), (1,)), ((), ())),
                preferred_element_type=F32,
            )
        for k in range(fanout + 2):
            hi = sums[32 * k : 32 * k + 16, :]
            lo = sums[32 * k + 16 : 32 * k + 32, :]
            value = (hi * 256.0 + lo).astype(I32)
            lists[h, k, :, :] = value if k <= fanout else half * CAP - value
        lane = iota((8, LANES), 1)
        begins = jnp.zeros((8, LANES), F32)
        for v in range(16):
            begins = begins + jnp.where(lane == v, bases[v], 0.0)
        lists[h, fanout + 2, 0:8, :] = begins.astype(I32)
        lists[h, fanout + 2, 8:16, :] = jnp.zeros((8, LANES), I32)


def list_copies(fanout, h, lists, ids, places, begins, sems):
    block = 16 * LANES

    def piece(k, length):
        at = pl.multiple_of((h * (fanout + 3) + k) * block, block)
        return lists.at[pl.ds(at, length)]

    last = fanout + 2
    copies = [
        pltpu.make_async_copy(piece(k, POSITIONS), ref, sems.at[k])
        for k, ref in enumerate(list(ids) + [places])
    ]
    copies.append(pltpu.make_async_copy(piece(last, LANES), begins, sems.at[last]))
    start_all(copies[fanout + 1 :] + copies[: fanout + 1])
    return copies


def look_up(fanout, copies, table, ids, places, begins, self_rows, mean_rows):
    for copy in [copies[0]] + copies[fanout + 1 :]:
        copy.wait()
    for v in range(1, fanout + 1):
        copies[v].wait()
        begin = begins[v - 1]
        end = begins[v]

        def body(i, carry, v=v, begin=begin):
            for u in range(UNROLL):
                at = begin + i * UNROLL + u
                to = places[at]
                self_rows[pl.ds(to, 1), :] = table[pl.ds(ids[0][at], 1), :]
                total = tree_sum([table[pl.ds(ids[k][at], 1), :] for k in range(1, v + 1)])
                mean_rows[pl.ds(to, 1), :] = total * (1.0 / v)
            return carry

        lax.fori_loop(0, jnp.right_shift(end - begin, UNROLL.bit_length() - 1), body, 0)


def write_out(x, width, self_rows, mean_rows, keep, send):
    valid = iota((CAP, LANES), 1) < width
    for z in range(2):
        for ref, side in ((keep, x), (send, 1 - x)):
            at = pl.multiple_of((z * 2 + side) * CAP, CAP)
            for part, rows in enumerate((self_rows, mean_rows)):
                block = jnp.where(valid, rows[pl.ds(at, CAP), :], 0.0).astype(BF16)
                ref[z, :, part * LANES : (part + 1) * LANES] = block


def stage(source, staged, sems):
    blocks, _, part = staged.shape
    copies = [
        pltpu.make_async_copy(source.at[:, pl.ds(b * part, part)], staged.at[b], sems.at[b])
        for b in range(blocks)
    ]
    start_all(copies)
    return copies


def turn_staged(copies, staged, table, base):
    part = staged.shape[2]
    for b, copy in enumerate(copies):
        copy.wait()
        turn(staged.at[b], table, pl.multiple_of(base + b * part, part))


def own_kernel(which, halves, me, features, *refs):
    table, staged, sems = refs[-3:]
    length = features.shape[1]
    half = length // halves
    copies = stage(features.at[:, pl.ds(which * half, half)], staged, sems)
    turn_staged(copies, staged, table, me[2] * length + which * half)


def join_kernel(*refs):
    *parts, out = refs
    at = 0
    for part in parts:
        out[at : at + part.shape[0], :] = part[...]
        at += part.shape[0]


def hand_out(keep, send, keep_hbm, send_hbm, sems):
    copies = [
        pltpu.make_async_copy(send, send_hbm, sems.at[0]),
        pltpu.make_async_copy(keep, keep_hbm, sems.at[1]),
    ]
    start_all(copies)
    for copy in copies:
        copy.wait()


def first_kernel(
    fanout, me, lists, table_in, other, self_one, neigh_one, table, keep_hbm, send_hbm, *scratch
):
    del table_in
    ids = scratch[: fanout + 1]
    places, begins, self_rows, mean_rows, sems = scratch[fanout + 1 : fanout + 6]
    staged, staged_sems, keep, send, out_sems = scratch[fanout + 6 :]
    width, length = other.shape
    x, h, rep = me[0], me[1], me[2]
    staging = stage(other, staged, staged_sems)
    copies = list_copies(fanout, h, lists, ids, places, begins, sems)
    self_rows[...] = jnp.zeros_like(self_rows)
    mean_rows[...] = jnp.zeros_like(mean_rows)
    send[2, :, :] = jnp.zeros(send.shape[1:], BF16)
    send[2, 0:width, :] = self_one[...]
    send[2, LANES : LANES + width, :] = neigh_one[...]
    turn_staged(staging, staged, table, (1 - rep) * length)
    look_up(fanout, copies, table, ids, places, begins, self_rows, mean_rows)
    write_out(x, width, self_rows, mean_rows, keep, send)
    hand_out(keep, send, keep_hbm, send_hbm, out_sems)


def second_kernel(fanout, width, me, lists, table, keep_hbm, send_hbm, *scratch):
    ids = scratch[: fanout + 1]
    places, begins, self_rows, mean_rows, sems, keep, send, out_sems = scratch[fanout + 1 :]
    x, h = me[0], 1 - me[1]
    copies = list_copies(fanout, h, lists, ids, places, begins, sems)
    self_rows[...] = jnp.zeros_like(self_rows)
    mean_rows[...] = jnp.zeros_like(mean_rows)
    look_up(fanout, copies, table, ids, places, begins, self_rows, mean_rows)
    write_out(x, width, self_rows, mean_rows, keep, send)
    hand_out(keep, send, keep_hbm, send_hbm, out_sems)


def project(zl, keep, got, weight, weight_got, outs):
    for which, out in ((zl, outs[0]), (1 - zl, outs[1])):
        out[...] = (
            jnp.dot(keep[which], weight[2, 0 : 2 * LANES, :], preferred_element_type=F32)
            + jnp.dot(got[which], weight_got[2, 0 : 2 * LANES, :], preferred_element_type=F32)
        ).astype(out.dtype)


def project_far_kernel(me, keep, got, sent, out_0, out_1):
    project(me[3], keep, got, sent, got, (out_0, out_1))


def project_near_kernel(me, keep_hbm, got, weight, weight_got, out_0, out_1, keep, sem):
    copy = pltpu.make_async_copy(keep_hbm, keep, sem)
    copy.start()
    copy.wait()
    project(me[3], keep, got, weight, weight_got, (out_0, out_1))


def last_kernel(
    mine, a, b, c, counts, bias_one, self_two, neigh_two, bias_two, out_weight, out_bias, out
):
    pre = mine[...] + a[...].astype(F32) + b[...].astype(F32) + c[...].astype(F32)
    hidden = jnp.maximum(pre + bias_one[...], 0.0).astype(BF16)
    seeds = counts.shape[1]
    same = iota((seeds, seeds), 0) == iota((seeds, seeds), 1)
    count = jnp.sum(jnp.where(same, counts[...].astype(F32), 0.0), axis=1, keepdims=True)
    count = count.astype(I32)
    earlier = (iota((seeds, seeds), 0) > iota((seeds, seeds), 1)).astype(BF16)
    needs = jnp.broadcast_to((count + 1).astype(F32), (seeds, LANES)).astype(BF16)
    offset = jnp.dot(earlier, needs, preferred_element_type=F32)[:, 0:1].astype(I32)
    place = iota((seeds, CAP), 1) - offset
    is_self = (place == 0).astype(F32).astype(BF16)
    is_near = ((place >= 1) & (place <= count)).astype(F32).astype(BF16)
    own = jnp.dot(is_self, hidden, preferred_element_type=F32).astype(BF16)
    total = jnp.dot(is_near, hidden, preferred_element_type=F32)
    mean = (total / count.astype(F32)).astype(BF16)
    pre_two = (
        jnp.dot(own, self_two[...], preferred_element_type=F32)
        + jnp.dot(mean, neigh_two[...], preferred_element_type=F32)
        + bias_two[...]
    )
    hidden_two = jnp.maximum(pre_two, 0.0).astype(BF16)
    logits = lax.dot_general(
        hidden_two, out_weight[...], (((1,), (1,)), ((), ())), preferred_element_type=F32
    )
    out[...] = logits + out_bias[...]


def params(limit):
    return pltpu.CompilerParams(vmem_limit_bytes=limit * MIB)


def shape(dims, dtype):
    return jax.ShapeDtypeStruct(dims, dtype)


def order_call(per_seed, me, own, got, self_ids, neighbour_ids, count_one):
    owners = sum(x.shape[0] for x in (own, *got))
    lists, most = pl.pallas_call(
        functools.partial(order_kernel, per_seed),
        out_shape=(shape((2, neighbour_ids.shape[0] + 3, 16, LANES), I32), shape((1,), I32)),
        in_specs=[SMEM] + [VMEM] * 7,
        out_specs=(VMEM, SMEM),
        scratch_shapes=[pltpu.VMEM((owners, own.shape[1]), I32)],
        compiler_params=params(10),
        name="order",
    )(me, own, *got, self_ids, neighbour_ids, count_one)
    return lists.reshape(-1), most[0]


def list_scratch(fanout):
    return (
        [pltpu.SMEM((POSITIONS,), I32) for _ in range(fanout + 2)]
        + [pltpu.SMEM((LANES,), I32)]
        + [pltpu.VMEM((4 * CAP + 8, LANES), F32) for _ in range(2)]
        + [pltpu.SemaphoreType.DMA((fanout + 3,))]
    )


def own_call(which, halves, me, features, *table):
    width, length = features.shape
    parts = 4 // halves
    return pl.pallas_call(
        functools.partial(own_kernel, which, halves),
        out_shape=shape((2 * length, LANES), F32),
        in_specs=[SMEM, HBM] + [VMEM] * len(table),
        out_specs=VMEM,
        scratch_shapes=[
            pltpu.VMEM((parts, width, length // 4), BF16),
            pltpu.SemaphoreType.DMA((parts,)),
        ],
        input_output_aliases={2: 0} if table else {},
        compiler_params=params(FIRST_MIB),
        name="own_rows",
    )(me, features, *table)


def join_call(*parts):
    rows = sum(part.shape[0] for part in parts)
    return pl.pallas_call(
        join_kernel,
        out_shape=shape((rows, parts[0].shape[1]), parts[0].dtype),
        in_specs=[VMEM] * len(parts),
        out_specs=VMEM,
        compiler_params=params(1),
        name="join",
    )(*parts)


def first_call(fanout, me, lists, table, other, self_one, neigh_one):
    width, length = other.shape
    keep, send = (2, CAP, 2 * LANES), (3, CAP, 2 * LANES)
    return pl.pallas_call(
        functools.partial(first_kernel, fanout),
        out_shape=(shape((2 * length, LANES), F32), pltpu.HBM(keep, BF16), pltpu.HBM(send, BF16)),
        in_specs=[SMEM, ANY, VMEM, HBM, VMEM, VMEM],
        out_specs=(VMEM, HBM, HBM),
        scratch_shapes=list_scratch(fanout)
        + [
            pltpu.VMEM((4, width, length // 4), BF16),
            pltpu.SemaphoreType.DMA((4,)),
            pltpu.VMEM(keep, BF16),
            pltpu.VMEM(send, BF16),
            pltpu.SemaphoreType.DMA((2,)),
        ],
        input_output_aliases={2: 0},
        compiler_params=params(FIRST_MIB),
        name="first_half",
    )(me, lists, table, other, self_one, neigh_one)


def second_call(fanout, width, me, lists, table):
    dims = (2, CAP, 2 * LANES)
    halves = pltpu.HBM(dims, BF16)
    return pl.pallas_call(
        functools.partial(second_kernel, fanout, width),
        out_shape=(halves, halves),
        in_specs=[SMEM, ANY, VMEM],
        out_specs=(HBM, HBM),
        scratch_shapes=list_scratch(fanout)
        + [pltpu.VMEM(dims, BF16) for _ in range(2)]
        + [pltpu.SemaphoreType.DMA((2,))],
        compiler_params=params(10),
        name="second_half",
    )(me, lists, table)


def project_far_call(me, keep, got, sent):
    part = shape((CAP, sent.shape[2]), BF16)
    return pl.pallas_call(
        project_far_kernel,
        out_shape=(part, part),
        in_specs=[SMEM, VMEM, VMEM, VMEM],
        out_specs=(VMEM, VMEM),
        compiler_params=params(10),
        name="project_far",
    )(me, keep, got, sent)


def project_near_call(me, keep, got, weight, weight_got):
    dims = (CAP, weight.shape[2])
    return pl.pallas_call(
        project_near_kernel,
        out_shape=(shape(dims, F32), shape(dims, BF16)),
        in_specs=[SMEM, HBM, VMEM, VMEM, VMEM],
        out_specs=(VMEM, VMEM),
        scratch_shapes=[pltpu.VMEM(keep.shape, BF16), pltpu.SemaphoreType.DMA],
        compiler_params=params(10),
        name="project_near",
    )(me, keep, got, weight, weight_got)


def last_call(*args):
    seeds = args[4].shape[1]
    classes = args[-1].shape[1]
    return pl.pallas_call(
        last_kernel,
        out_shape=shape((seeds, classes), F32),
        in_specs=[VMEM] * len(args),
        out_specs=VMEM,
        compiler_params=params(10),
        name="layer_two",
    )(*args)


def main(
    features,
    self_ids,
    neighbour_ids,
    count_one,
    count_two,
    self_one,
    neigh_one,
    bias_one,
    self_two,
    neigh_two,
    bias_two,
    out_weight,
    out_bias,
):
    owners = lax.axis_size("col")
    seeds = count_two.shape[0]
    per_owner = self_ids.shape[0] // owners
    per_seed = per_owner // seeds
    fanout = neighbour_ids.shape[0]
    width = features.shape[0]
    col = lax.axis_index("col")
    rep = lax.axis_index("rep")
    z = col // 2
    me = jnp.stack([col % 2, 1 - z // 2, rep, z % 2, col]).astype(I32)

    def across(value, bit):
        return lax.ppermute(value, "col", [(i, i ^ bit) for i in range(owners)])

    other = lax.ppermute(features, "rep", [(0, 1), (1, 0)])
    held = pltpu.with_memory_space_constraint(features, pltpu.HBM)
    own = count_two[None, :]
    got_1 = across(own, 1)
    table, got_1 = lax.optimization_barrier((own_call(0, 1, me, held), got_1))
    got_2 = across(join_call(own, got_1), 2)
    got_4 = across(join_call(own, got_1, got_2), 4)
    got = (got_1, got_2, got_4)
    lists, most = order_call(per_seed, me, own, got, self_ids, neighbour_ids, count_one)
    table, keep_far, send_far = first_call(
        fanout, me, lists, table, other, self_one, neigh_one
    )
    got_far = across(send_far, 1)
    keep_near, send_near = second_call(fanout, width, me, lists, table)
    got_near = across(send_near, 1)
    far_0, far_1 = project_far_call(me, keep_far, got_far, send_far)
    far = [across(far_0, 4), across(far_1, 6)]
    near_0, near_1 = project_near_call(me, keep_near, got_near, send_far, got_far)
    far.append(across(near_1, 2))
    fast = last_call(
        near_0,
        *far,
        own,
        bias_one[None, :],
        self_two,
        neigh_two,
        bias_two[None, :],
        out_weight.T,
        out_bias[None, :],
    )
    return lax.cond(
        most > CAP,
        lambda: general(
            other,
            features,
            self_ids,
            neighbour_ids,
            count_one,
            count_two,
            self_one,
            neigh_one,
            bias_one,
            self_two,
            neigh_two,
            bias_two,
            out_weight,
            out_bias,
        ),
        lambda: fast,
    )


def local(*args):
    features, self_ids, neighbour_ids = args[0], args[1], args[2]
    sizes = (lax.axis_size("groups"), lax.axis_size("col"), lax.axis_size("rep"))
    small = (
        sizes == (2, 8, 2)
        and features.shape[0] <= LANES
        and features.shape[1] <= 32768
        and self_ids.shape[0] * (neighbour_ids.shape[0] + 1) <= 2**17
        and neighbour_ids.shape[0] <= 15
    )
    if small:
        return main(*args)
    return general(lax.ppermute(features, "rep", [(0, 1), (1, 0)]), *args)


def solution(mesh):
    placed = (
        P("col", ("groups", "rep")),
        P(("groups", "rep")),
        P(None, ("groups", "rep")),
        P(("groups", "rep")),
        P(("groups", "col", "rep")),
        P("col", None),
        P("col", None),
        P(),
        P(),
        P(),
        P(),
        P(),
        P(),
    )
    return jax.shard_map(
        local,
        mesh=mesh,
        in_specs=placed,
        out_specs=P(("groups", "col", "rep"), None),
        check_vma=False,
    )
```

```python
import functools

import jax
import jax.numpy as jnp
import numpy as np
from jax import lax
from jax.experimental import pallas as pl
from jax.experimental.pallas import tpu as pltpu
from jax.sharding import PartitionSpec as P

CAP = 272
UNROLL = 8
POSITIONS = 10 * 128
FIRST_MIB = 12
OWN_MIB = 18
LANES = 128
MIB = 2**20
BF16 = jnp.bfloat16
F32 = jnp.float32
I32 = jnp.int32


def gathered(value, axis):
    copies = jnp.broadcast_to(value[None], (lax.axis_size(axis),) + value.shape)
    pieces = lax.all_to_all(copies, axis, split_axis=0, concat_axis=0, tiled=True)
    return pieces.reshape((-1,) + value.shape[1:])


def general(
    other,
    features,
    self_ids,
    neighbour_ids,
    count_one,
    count_two,
    self_one,
    neigh_one,
    bias_one,
    self_two,
    neigh_two,
    bias_two,
    out_weight,
    out_bias,
):
    mine = jnp.where(lax.axis_index("rep") == 0, 0, 1)
    table_cols = jnp.where(
        mine == 0,
        jnp.concatenate([features, other], axis=1),
        jnp.concatenate([other, features], axis=1),
    )
    table_rows = table_cols.T
    blocks = lax.axis_size("col")
    total_rows = self_ids.shape[0]
    per_owner = total_rows // blocks
    fanout = neighbour_ids.shape[0]
    width = table_rows.shape[1]
    all_ids = jnp.concatenate([self_ids[None, :], neighbour_ids], axis=0)
    fetched = jnp.take(table_rows, all_ids, axis=0)
    self_x = fetched[0]
    mask = (jnp.arange(fanout)[:, None] < count_one[None, :]).astype(BF16)
    summed = jnp.einsum("kmc,km->mc", fetched[1:], mask, preferred_element_type=F32)
    mean_one = (summed / count_one[:, None].astype(F32)).astype(BF16)
    full_self, full_neigh = gathered(self_one, "col"), gathered(neigh_one, "col")
    stacked = jnp.stack([self_x, mean_one], axis=0).reshape(2, blocks, per_owner, width)
    pieces = lax.all_to_all(stacked, "col", split_axis=1, concat_axis=3, tiled=True)
    pre_one = jnp.dot(pieces[0, 0], full_self, preferred_element_type=F32) + jnp.dot(
        pieces[1, 0], full_neigh, preferred_element_type=F32
    )
    hidden_one = jax.nn.relu(pre_one + bias_one).astype(BF16)
    seeds = count_two.shape[0]
    hidden = hidden_one.shape[1]
    grouped = hidden_one.reshape(seeds, per_owner // seeds, hidden)
    mask_two = (jnp.arange(grouped.shape[1] - 1)[None, :] < count_two[:, None]).astype(BF16)
    summed_two = jnp.einsum("skh,sk->sh", grouped[:, 1:, :], mask_two, preferred_element_type=F32)
    mean_two = (summed_two / count_two[:, None].astype(F32)).astype(BF16)
    pre_two = jnp.dot(grouped[:, 0, :], self_two, preferred_element_type=F32) + jnp.dot(
        mean_two, neigh_two, preferred_element_type=F32
    )
    hidden_two = jax.nn.relu(pre_two + bias_two).astype(BF16)
    return jnp.dot(hidden_two, out_weight, preferred_element_type=F32) + out_bias


def iota(shape, dim):
    return lax.broadcasted_iota(I32, shape, dim)


def tree_sum(terms):
    while len(terms) > 1:
        odd = [terms[-1]] if len(terms) % 2 else []
        terms = [a + b for a, b in zip(terms[::2], terms[1::2])] + odd
    return terms[0]


VMEM = pl.BlockSpec(memory_space=pltpu.VMEM)
SMEM = pl.BlockSpec(memory_space=pltpu.SMEM)
HBM = pl.BlockSpec(memory_space=pltpu.HBM)
ANY = pl.BlockSpec(memory_space=pl.ANY)


def start_all(copies):
    for copy in copies:
        copy.start()


def turn(source, table, base):
    width, length = source.shape
    step = 512
    unroll = 4

    def body(i, carry):
        for u in range(unroll):
            off = pl.multiple_of((i * unroll + u) * step, step)
            rows = source[:, pl.ds(off, step)].T.astype(F32)
            table[pl.ds(pl.multiple_of(base + off, step), step), 0:width] = rows
        return carry

    lax.fori_loop(0, length // step // unroll, body, 0)


def order_kernel(
    per_seed, me, own, got_1, got_2, got_4, self_ids, neighbour_ids, count_one, lists, most, counts_rel
):
    owners, seeds = counts_rel.shape
    fanout = neighbour_ids.shape[0]
    per_owner = count_one.shape[0] // owners
    half = owners // 2
    mine = me[4]
    counts_rel[0:1, :] = own[...]
    counts_rel[1:2, :] = got_1[...]
    counts_rel[2:4, :] = got_2[...]
    counts_rel[4:8, :] = got_4[...]
    own_ids = self_ids[...].reshape(1, owners * per_owner)
    ones = count_one[...].reshape(1, owners * per_owner)
    counts = jnp.concatenate(
        [counts_rel[pl.ds(jnp.bitwise_xor(mine, c), 1), :] for c in range(owners)], axis=0
    ).astype(F32)
    needs = (counts + 1.0).astype(BF16)
    most[0] = jnp.max(jnp.sum(counts + 1.0, axis=1, keepdims=True)).astype(I32)
    column = iota((seeds, per_owner), 1).astype(F32)
    seed_of = jnp.floor((column + 0.5) * (1.0 / per_seed))
    seed = iota((seeds, per_owner), 0).astype(F32)
    t = column[0:1, :] - seed_of[0:1, :] * per_seed
    of_row = jnp.dot(
        counts.astype(BF16), (seed == seed_of).astype(BF16), preferred_element_type=F32
    )
    slot = t + jnp.dot(needs, (seed < seed_of).astype(BF16), preferred_element_type=F32)
    used = (t <= of_row) & (slot < CAP)
    slot = slot.astype(I32)
    keys = [
        jnp.where(used[c : c + 1, :], ones[:, c * per_owner : (c + 1) * per_owner], 0)
        for c in range(owners)
    ]
    kinds = [
        iota((16, per_owner), 0) == jnp.broadcast_to(key, (16, per_owner)) for key in keys
    ]
    stacked = jnp.concatenate([k.astype(F32).astype(BF16) for k in kinds], axis=0)
    left = (iota((per_owner, per_owner), 0) < iota((per_owner, per_owner), 1)).astype(BF16)
    prefix = jnp.dot(stacked, left, preferred_element_type=F32)
    total = jnp.dot(stacked, jnp.ones((per_owner, LANES), BF16), preferred_element_type=F32)
    for h in range(2):
        carry = jnp.zeros((16, LANES), F32)
        carries = []
        for c in range(h * half, (h + 1) * half):
            carries.append(carry)
            carry = carry + total[c * 16 : (c + 1) * 16, :]
        sizes = jnp.floor((carry + (UNROLL - 1)) * (1.0 / UNROLL)) * UNROLL
        bases = [jnp.zeros((1, LANES), F32)]
        for v in range(1, 16):
            bases.append(bases[-1] + sizes[v : v + 1, :])
        first = jnp.concatenate([bases[0]] + bases[:15], axis=0)
        sums = jnp.zeros((2 * (fanout + 2) * 16, LANES), F32)
        for i, c in enumerate(range(h * half, (h + 1) * half)):
            begin = (first + carries[i])[:, 0:1]
            spot = jnp.where(kinds[c], prefix[c * 16 : (c + 1) * 16, :] + begin, 0.0)
            spot = jnp.sum(spot, axis=0, keepdims=True).astype(I32)
            spot = jnp.where(keys[c] > 0, spot, -1)
            spot_lo = jnp.bitwise_and(spot, LANES - 1)
            spot_hi = jnp.right_shift(spot, 7)
            lane = (iota((LANES, per_owner), 0) == spot_lo).astype(F32).astype(BF16)
            at_hi = (iota((16, per_owner), 0) == spot_hi).astype(F32)
            columns = slice(c * per_owner, (c + 1) * per_owner)
            rows = [own_ids[:, columns]]
            rows += [neighbour_ids[k : k + 1, columns] for k in range(fanout)]
            rows += [half * CAP - (slot[c : c + 1, :] + i * CAP)]
            parts = []
            for row in rows:
                for byte in (jnp.right_shift(row, 8), jnp.bitwise_and(row, 255)):
                    value = jnp.broadcast_to(byte.astype(F32), (16, per_owner))
                    parts.append((at_hi * value).astype(BF16))
            sums = sums + lax.dot_general(
                jnp.concatenate(parts, axis=0),
                lane,
                (((1,), (1,)), ((), ())),
                preferred_element_type=F32,
            )
        for k in range(fanout + 2):
            hi = sums[32 * k : 32 * k + 16, :]
            lo = sums[32 * k + 16 : 32 * k + 32, :]
            value = (hi * 256.0 + lo).astype(I32)
            lists[h, k, :, :] = value if k <= fanout else half * CAP - value
        lane = iota((8, LANES), 1)
        begins = jnp.zeros((8, LANES), F32)
        for v in range(16):
            begins = begins + jnp.where(lane == v, bases[v], 0.0)
        lists[h, fanout + 2, 0:8, :] = begins.astype(I32)
        lists[h, fanout + 2, 8:16, :] = jnp.zeros((8, LANES), I32)


def list_copies(fanout, h, lists, ids, places, begins, sems):
    block = 16 * LANES

    def piece(k, length):
        at = pl.multiple_of((h * (fanout + 3) + k) * block, block)
        return lists.at[pl.ds(at, length)]

    last = fanout + 2
    copies = [
        pltpu.make_async_copy(piece(k, POSITIONS), ref, sems.at[k])
        for k, ref in enumerate(list(ids) + [places])
    ]
    copies.append(pltpu.make_async_copy(piece(last, LANES), begins, sems.at[last]))
    start_all(copies[fanout + 1 :] + copies[: fanout + 1])
    return copies


def look_up(fanout, copies, table, ids, places, begins, self_rows, mean_rows):
    for copy in [copies[0]] + copies[fanout + 1 :]:
        copy.wait()
    for v in range(1, fanout + 1):
        copies[v].wait()
        begin = begins[v - 1]
        end = begins[v]

        def body(i, carry, v=v, begin=begin):
            for u in range(UNROLL):
                at = begin + i * UNROLL + u
                to = places[at]
                self_rows[pl.ds(to, 1), :] = table[pl.ds(ids[0][at], 1), :]
                total = tree_sum([table[pl.ds(ids[k][at], 1), :] for k in range(1, v + 1)])
                mean_rows[pl.ds(to, 1), :] = total * (1.0 / v)
            return carry

        lax.fori_loop(0, jnp.right_shift(end - begin, UNROLL.bit_length() - 1), body, 0)


def write_out(x, width, self_rows, mean_rows, keep, send):
    valid = iota((CAP, LANES), 1) < width
    for z in range(2):
        for ref, side in ((keep, x), (send, 1 - x)):
            at = pl.multiple_of((z * 2 + side) * CAP, CAP)
            for part, rows in enumerate((self_rows, mean_rows)):
                block = jnp.where(valid, rows[pl.ds(at, CAP), :], 0.0).astype(BF16)
                ref[z, :, part * LANES : (part + 1) * LANES] = block


def stage(source, staged, sems):
    blocks, _, part = staged.shape
    copies = [
        pltpu.make_async_copy(source.at[:, pl.ds(b * part, part)], staged.at[b], sems.at[b])
        for b in range(blocks)
    ]
    start_all(copies)
    return copies


def turn_staged(copies, staged, table, base):
    part = staged.shape[2]
    for b, copy in enumerate(copies):
        copy.wait()
        turn(staged.at[b], table, pl.multiple_of(base + b * part, part))


def own_kernel(which, halves, me, features, *refs):
    table, staged, sems = refs[-3:]
    length = features.shape[1]
    half = length // halves
    copies = stage(features.at[:, pl.ds(which * half, half)], staged, sems)
    turn_staged(copies, staged, table, me[2] * length + which * half)


def join_kernel(*refs):
    *parts, out = refs
    at = 0
    for part in parts:
        out[at : at + part.shape[0], :] = part[...]
        at += part.shape[0]


def hand_out(keep, send, keep_hbm, send_hbm, sems):
    copies = [
        pltpu.make_async_copy(send, send_hbm, sems.at[0]),
        pltpu.make_async_copy(keep, keep_hbm, sems.at[1]),
    ]
    start_all(copies)
    for copy in copies:
        copy.wait()


def first_kernel(
    fanout, me, lists, table_in, other, self_one, neigh_one, table, keep_hbm, send_hbm, *scratch
):
    del table_in
    ids = scratch[: fanout + 1]
    places, begins, self_rows, mean_rows, sems = scratch[fanout + 1 : fanout + 6]
    staged, staged_sems, keep, send, out_sems = scratch[fanout + 6 :]
    width, length = other.shape
    x, h, rep = me[0], me[1], me[2]
    staging = stage(other, staged, staged_sems)
    copies = list_copies(fanout, h, lists, ids, places, begins, sems)
    self_rows[...] = jnp.zeros_like(self_rows)
    mean_rows[...] = jnp.zeros_like(mean_rows)
    send[2, :, :] = jnp.zeros(send.shape[1:], BF16)
    send[2, 0:width, :] = self_one[...]
    send[2, LANES : LANES + width, :] = neigh_one[...]
    turn_staged(staging, staged, table, (1 - rep) * length)
    look_up(fanout, copies, table, ids, places, begins, self_rows, mean_rows)
    write_out(x, width, self_rows, mean_rows, keep, send)
    hand_out(keep, send, keep_hbm, send_hbm, out_sems)


def second_kernel(fanout, width, me, lists, table, keep_hbm, send_hbm, *scratch):
    ids = scratch[: fanout + 1]
    places, begins, self_rows, mean_rows, sems, keep, send, out_sems = scratch[fanout + 1 :]
    x, h = me[0], 1 - me[1]
    copies = list_copies(fanout, h, lists, ids, places, begins, sems)
    self_rows[...] = jnp.zeros_like(self_rows)
    mean_rows[...] = jnp.zeros_like(mean_rows)
    look_up(fanout, copies, table, ids, places, begins, self_rows, mean_rows)
    write_out(x, width, self_rows, mean_rows, keep, send)
    hand_out(keep, send, keep_hbm, send_hbm, out_sems)


def project(zl, keep, got, weight, weight_got, outs):
    for which, out in ((zl, outs[0]), (1 - zl, outs[1])):
        out[...] = (
            jnp.dot(keep[which], weight[2, 0 : 2 * LANES, :], preferred_element_type=F32)
            + jnp.dot(got[which], weight_got[2, 0 : 2 * LANES, :], preferred_element_type=F32)
        ).astype(out.dtype)


def project_far_kernel(me, keep, got, sent, later, out_0, out_1, loaded, sem):
    copy = pltpu.make_async_copy(later, loaded, sem)
    copy.start()
    project(me[3], keep, got, sent, got, (out_0, out_1))
    copy.wait()


def project_near_kernel(me, keep, got, weight, weight_got, out_0, out_1):
    project(me[3], keep, got, weight, weight_got, (out_0, out_1))


def last_kernel(
    mine, a, b, c, counts, bias_one, self_two, neigh_two, bias_two, out_weight, out_bias, out
):
    pre = mine[...] + a[...].astype(F32) + b[...].astype(F32) + c[...].astype(F32)
    hidden = jnp.maximum(pre + bias_one[...], 0.0).astype(BF16)
    seeds = counts.shape[1]
    same = iota((seeds, seeds), 0) == iota((seeds, seeds), 1)
    count = jnp.sum(jnp.where(same, counts[...].astype(F32), 0.0), axis=1, keepdims=True)
    count = count.astype(I32)
    earlier = (iota((seeds, seeds), 0) > iota((seeds, seeds), 1)).astype(BF16)
    needs = jnp.broadcast_to((count + 1).astype(F32), (seeds, LANES)).astype(BF16)
    offset = jnp.dot(earlier, needs, preferred_element_type=F32)[:, 0:1].astype(I32)
    place = iota((seeds, CAP), 1) - offset
    is_self = (place == 0).astype(F32).astype(BF16)
    is_near = ((place >= 1) & (place <= count)).astype(F32).astype(BF16)
    own = jnp.dot(is_self, hidden, preferred_element_type=F32).astype(BF16)
    total = jnp.dot(is_near, hidden, preferred_element_type=F32)
    mean = (total / count.astype(F32)).astype(BF16)
    pre_two = (
        jnp.dot(own, self_two[...], preferred_element_type=F32)
        + jnp.dot(mean, neigh_two[...], preferred_element_type=F32)
        + bias_two[...]
    )
    hidden_two = jnp.maximum(pre_two, 0.0).astype(BF16)
    logits = lax.dot_general(
        hidden_two, out_weight[...], (((1,), (1,)), ((), ())), preferred_element_type=F32
    )
    out[...] = logits + out_bias[...]


def params(limit):
    return pltpu.CompilerParams(vmem_limit_bytes=limit * MIB)


def shape(dims, dtype):
    return jax.ShapeDtypeStruct(dims, dtype)


def order_call(per_seed, me, own, got, self_ids, neighbour_ids, count_one):
    owners = sum(x.shape[0] for x in (own, *got))
    lists, most = pl.pallas_call(
        functools.partial(order_kernel, per_seed),
        out_shape=(shape((2, neighbour_ids.shape[0] + 3, 16, LANES), I32), shape((1,), I32)),
        in_specs=[SMEM] + [VMEM] * 7,
        out_specs=(VMEM, SMEM),
        scratch_shapes=[pltpu.VMEM((owners, own.shape[1]), I32)],
        compiler_params=params(10),
        name="order",
    )(me, own, *got, self_ids, neighbour_ids, count_one)
    return lists.reshape(-1), most[0]


def list_scratch(fanout):
    return (
        [pltpu.SMEM((POSITIONS,), I32) for _ in range(fanout + 2)]
        + [pltpu.SMEM((LANES,), I32)]
        + [pltpu.VMEM((4 * CAP + 8, LANES), F32) for _ in range(2)]
        + [pltpu.SemaphoreType.DMA((fanout + 3,))]
    )


def own_call(which, halves, me, features, *table):
    width, length = features.shape
    parts = 8 // halves
    return pl.pallas_call(
        functools.partial(own_kernel, which, halves),
        out_shape=shape((2 * length, LANES), F32),
        in_specs=[SMEM, HBM] + [VMEM] * len(table),
        out_specs=VMEM,
        scratch_shapes=[
            pltpu.VMEM((parts, width, length // 8), BF16),
            pltpu.SemaphoreType.DMA((parts,)),
        ],
        input_output_aliases={2: 0} if table else {},
        compiler_params=params(FIRST_MIB if table else OWN_MIB),
        name="own_rows",
    )(me, features, *table)


def join_call(*parts):
    rows = sum(part.shape[0] for part in parts)
    return pl.pallas_call(
        join_kernel,
        out_shape=shape((rows, parts[0].shape[1]), parts[0].dtype),
        in_specs=[VMEM] * len(parts),
        out_specs=VMEM,
        compiler_params=params(1),
        name="join",
    )(*parts)


def first_call(fanout, me, lists, table, other, self_one, neigh_one):
    width, length = other.shape
    keep, send = (2, CAP, 2 * LANES), (3, CAP, 2 * LANES)
    return pl.pallas_call(
        functools.partial(first_kernel, fanout),
        out_shape=(shape((2 * length, LANES), F32), pltpu.HBM(keep, BF16), pltpu.HBM(send, BF16)),
        in_specs=[SMEM, ANY, VMEM, HBM, VMEM, VMEM],
        out_specs=(VMEM, HBM, HBM),
        scratch_shapes=list_scratch(fanout)
        + [
            pltpu.VMEM((8, width, length // 8), BF16),
            pltpu.SemaphoreType.DMA((8,)),
            pltpu.VMEM(keep, BF16),
            pltpu.VMEM(send, BF16),
            pltpu.SemaphoreType.DMA((2,)),
        ],
        input_output_aliases={2: 0},
        compiler_params=params(FIRST_MIB),
        name="first_half",
    )(me, lists, table, other, self_one, neigh_one)


def second_call(fanout, width, me, lists, table):
    dims = (2, CAP, 2 * LANES)
    halves = pltpu.HBM(dims, BF16)
    return pl.pallas_call(
        functools.partial(second_kernel, fanout, width),
        out_shape=(halves, halves),
        in_specs=[SMEM, ANY, VMEM],
        out_specs=(HBM, HBM),
        scratch_shapes=list_scratch(fanout)
        + [pltpu.VMEM(dims, BF16) for _ in range(2)]
        + [pltpu.SemaphoreType.DMA((2,))],
        compiler_params=params(10),
        name="second_half",
    )(me, lists, table)


def project_far_call(me, keep, got, sent, later):
    part = shape((CAP, sent.shape[2]), BF16)
    return pl.pallas_call(
        project_far_kernel,
        out_shape=(part, part, shape(later.shape, BF16)),
        in_specs=[SMEM, VMEM, VMEM, VMEM, HBM],
        out_specs=(VMEM, VMEM, VMEM),
        scratch_shapes=[pltpu.SemaphoreType.DMA],
        compiler_params=params(10),
        name="project_far",
    )(me, keep, got, sent, pltpu.with_memory_space_constraint(later, pltpu.HBM))


def project_near_call(me, keep, got, weight, weight_got):
    dims = (CAP, weight.shape[2])
    return pl.pallas_call(
        project_near_kernel,
        out_shape=(shape(dims, F32), shape(dims, BF16)),
        in_specs=[SMEM, VMEM, VMEM, VMEM, VMEM],
        out_specs=(VMEM, VMEM),
        compiler_params=params(10),
        name="project_near",
    )(me, keep, got, weight, weight_got)


def last_call(*args):
    seeds = args[4].shape[1]
    classes = args[-1].shape[1]
    return pl.pallas_call(
        last_kernel,
        out_shape=shape((seeds, classes), F32),
        in_specs=[VMEM] * len(args),
        out_specs=VMEM,
        compiler_params=params(10),
        name="layer_two",
    )(*args)


def main(
    features,
    self_ids,
    neighbour_ids,
    count_one,
    count_two,
    self_one,
    neigh_one,
    bias_one,
    self_two,
    neigh_two,
    bias_two,
    out_weight,
    out_bias,
):
    owners = lax.axis_size("col")
    seeds = count_two.shape[0]
    per_owner = self_ids.shape[0] // owners
    per_seed = per_owner // seeds
    fanout = neighbour_ids.shape[0]
    width = features.shape[0]
    col = lax.axis_index("col")
    rep = lax.axis_index("rep")
    z = col // 2
    me = jnp.stack([col % 2, 1 - z // 2, rep, z % 2, col]).astype(I32)

    def across(value, bit):
        return lax.ppermute(value, "col", [(i, i ^ bit) for i in range(owners)])

    other = lax.ppermute(features, "rep", [(0, 1), (1, 0)])
    held = pltpu.with_memory_space_constraint(features, pltpu.HBM)
    own = count_two[None, :]
    got_1 = across(own, 1)
    table, got_1 = lax.optimization_barrier((own_call(0, 2, me, held), got_1))
    got_2 = across(join_call(own, got_1), 2)
    table, got_2 = lax.optimization_barrier((own_call(1, 2, me, held, table), got_2))
    got_4 = across(join_call(own, got_1, got_2), 4)
    got = (got_1, got_2, got_4)
    lists, most = order_call(per_seed, me, own, got, self_ids, neighbour_ids, count_one)
    table, keep_far, send_far = first_call(
        fanout, me, lists, table, other, self_one, neigh_one
    )
    got_far = across(send_far, 1)
    keep_near, send_near = second_call(fanout, width, me, lists, table)
    got_near = across(send_near, 1)
    far_0, far_1, keep_near = project_far_call(me, keep_far, got_far, send_far, keep_near)
    far = [across(far_0, 4), across(far_1, 6)]
    near_0, near_1 = project_near_call(me, keep_near, got_near, send_far, got_far)
    far.append(across(near_1, 2))
    fast = last_call(
        near_0,
        *far,
        own,
        bias_one[None, :],
        self_two,
        neigh_two,
        bias_two[None, :],
        out_weight.T,
        out_bias[None, :],
    )
    return lax.cond(
        most > CAP,
        lambda: general(
            other,
            features,
            self_ids,
            neighbour_ids,
            count_one,
            count_two,
            self_one,
            neigh_one,
            bias_one,
            self_two,
            neigh_two,
            bias_two,
            out_weight,
            out_bias,
        ),
        lambda: fast,
    )


def local(*args):
    features, self_ids, neighbour_ids = args[0], args[1], args[2]
    sizes = (lax.axis_size("groups"), lax.axis_size("col"), lax.axis_size("rep"))
    small = (
        sizes == (2, 8, 2)
        and features.shape[0] <= LANES
        and features.shape[1] <= 32768
        and self_ids.shape[0] * (neighbour_ids.shape[0] + 1) <= 2**17
        and neighbour_ids.shape[0] <= 15
    )
    if small:
        return main(*args)
    return general(lax.ppermute(features, "rep", [(0, 1), (1, 0)]), *args)


def solution(mesh):
    placed = (
        P("col", ("groups", "rep")),
        P(("groups", "rep")),
        P(None, ("groups", "rep")),
        P(("groups", "rep")),
        P(("groups", "col", "rep")),
        P("col", None),
        P("col", None),
        P(),
        P(),
        P(),
        P(),
        P(),
        P(),
    )
    return jax.shard_map(
        local,
        mesh=mesh,
        in_specs=placed,
        out_specs=P(("groups", "col", "rep"), None),
        check_vma=False,
    )
```

```python
import functools

import jax
import jax.numpy as jnp
import numpy as np
from jax import lax
from jax.experimental import pallas as pl
from jax.experimental.pallas import tpu as pltpu
from jax.sharding import PartitionSpec as P

CAP = 272
UNROLL = 8
POSITIONS = 10 * 128
FIRST_MIB = 12
OWN_MIB = 18
LANES = 128
MIB = 2**20
BF16 = jnp.bfloat16
F32 = jnp.float32
I32 = jnp.int32


def gathered(value, axis):
    copies = jnp.broadcast_to(value[None], (lax.axis_size(axis),) + value.shape)
    pieces = lax.all_to_all(copies, axis, split_axis=0, concat_axis=0, tiled=True)
    return pieces.reshape((-1,) + value.shape[1:])


def general(
    other,
    features,
    self_ids,
    neighbour_ids,
    count_one,
    count_two,
    self_one,
    neigh_one,
    bias_one,
    self_two,
    neigh_two,
    bias_two,
    out_weight,
    out_bias,
):
    mine = jnp.where(lax.axis_index("rep") == 0, 0, 1)
    table_cols = jnp.where(
        mine == 0,
        jnp.concatenate([features, other], axis=1),
        jnp.concatenate([other, features], axis=1),
    )
    table_rows = table_cols.T
    blocks = lax.axis_size("col")
    total_rows = self_ids.shape[0]
    per_owner = total_rows // blocks
    fanout = neighbour_ids.shape[0]
    width = table_rows.shape[1]
    all_ids = jnp.concatenate([self_ids[None, :], neighbour_ids], axis=0)
    fetched = jnp.take(table_rows, all_ids, axis=0)
    self_x = fetched[0]
    mask = (jnp.arange(fanout)[:, None] < count_one[None, :]).astype(BF16)
    summed = jnp.einsum("kmc,km->mc", fetched[1:], mask, preferred_element_type=F32)
    mean_one = (summed / count_one[:, None].astype(F32)).astype(BF16)
    full_self, full_neigh = gathered(self_one, "col"), gathered(neigh_one, "col")
    stacked = jnp.stack([self_x, mean_one], axis=0).reshape(2, blocks, per_owner, width)
    pieces = lax.all_to_all(stacked, "col", split_axis=1, concat_axis=3, tiled=True)
    pre_one = jnp.dot(pieces[0, 0], full_self, preferred_element_type=F32) + jnp.dot(
        pieces[1, 0], full_neigh, preferred_element_type=F32
    )
    hidden_one = jax.nn.relu(pre_one + bias_one).astype(BF16)
    seeds = count_two.shape[0]
    hidden = hidden_one.shape[1]
    grouped = hidden_one.reshape(seeds, per_owner // seeds, hidden)
    mask_two = (jnp.arange(grouped.shape[1] - 1)[None, :] < count_two[:, None]).astype(BF16)
    summed_two = jnp.einsum("skh,sk->sh", grouped[:, 1:, :], mask_two, preferred_element_type=F32)
    mean_two = (summed_two / count_two[:, None].astype(F32)).astype(BF16)
    pre_two = jnp.dot(grouped[:, 0, :], self_two, preferred_element_type=F32) + jnp.dot(
        mean_two, neigh_two, preferred_element_type=F32
    )
    hidden_two = jax.nn.relu(pre_two + bias_two).astype(BF16)
    return jnp.dot(hidden_two, out_weight, preferred_element_type=F32) + out_bias


def iota(shape, dim):
    return lax.broadcasted_iota(I32, shape, dim)


def tree_sum(terms):
    while len(terms) > 1:
        odd = [terms[-1]] if len(terms) % 2 else []
        terms = [a + b for a, b in zip(terms[::2], terms[1::2])] + odd
    return terms[0]


VMEM = pl.BlockSpec(memory_space=pltpu.VMEM)
SMEM = pl.BlockSpec(memory_space=pltpu.SMEM)
HBM = pl.BlockSpec(memory_space=pltpu.HBM)
ANY = pl.BlockSpec(memory_space=pl.ANY)


def start_all(copies):
    for copy in copies:
        copy.start()


def turn(source, table, base):
    width, length = source.shape
    step = 512
    unroll = 4

    def body(i, carry):
        for u in range(unroll):
            off = pl.multiple_of((i * unroll + u) * step, step)
            rows = source[:, pl.ds(off, step)].T.astype(F32)
            table[pl.ds(pl.multiple_of(base + off, step), step), 0:width] = rows
        return carry

    lax.fori_loop(0, length // step // unroll, body, 0)


def order_kernel(
    per_seed, me, own, got_1, got_2, got_4, got_6, self_ids, neighbour_ids, count_one, lists, most, counts_rel
):
    owners, seeds = counts_rel.shape
    fanout = neighbour_ids.shape[0]
    per_owner = count_one.shape[0] // owners
    half = owners // 2
    mine = me[4]
    counts_rel[0:1, :] = own[...]
    counts_rel[1:2, :] = got_1[...]
    counts_rel[2:4, :] = got_2[...]
    counts_rel[4:6, :] = got_4[...]
    counts_rel[6:8, :] = got_6[...]
    own_ids = self_ids[...].reshape(1, owners * per_owner)
    ones = count_one[...].reshape(1, owners * per_owner)
    counts = jnp.concatenate(
        [counts_rel[pl.ds(jnp.bitwise_xor(mine, c), 1), :] for c in range(owners)], axis=0
    ).astype(F32)
    needs = (counts + 1.0).astype(BF16)
    most[0] = jnp.max(jnp.sum(counts + 1.0, axis=1, keepdims=True)).astype(I32)
    column = iota((seeds, per_owner), 1).astype(F32)
    seed_of = jnp.floor((column + 0.5) * (1.0 / per_seed))
    seed = iota((seeds, per_owner), 0).astype(F32)
    t = column[0:1, :] - seed_of[0:1, :] * per_seed
    of_row = jnp.dot(
        counts.astype(BF16), (seed == seed_of).astype(BF16), preferred_element_type=F32
    )
    slot = t + jnp.dot(needs, (seed < seed_of).astype(BF16), preferred_element_type=F32)
    used = (t <= of_row) & (slot < CAP)
    slot = slot.astype(I32)
    keys = [
        jnp.where(used[c : c + 1, :], ones[:, c * per_owner : (c + 1) * per_owner], 0)
        for c in range(owners)
    ]
    kinds = [
        iota((16, per_owner), 0) == jnp.broadcast_to(key, (16, per_owner)) for key in keys
    ]
    stacked = jnp.concatenate([k.astype(F32).astype(BF16) for k in kinds], axis=0)
    left = (iota((per_owner, per_owner), 0) < iota((per_owner, per_owner), 1)).astype(BF16)
    prefix = jnp.dot(stacked, left, preferred_element_type=F32)
    total = jnp.dot(stacked, jnp.ones((per_owner, LANES), BF16), preferred_element_type=F32)
    for h in range(2):
        carry = jnp.zeros((16, LANES), F32)
        carries = []
        for c in range(h * half, (h + 1) * half):
            carries.append(carry)
            carry = carry + total[c * 16 : (c + 1) * 16, :]
        sizes = jnp.floor((carry + (UNROLL - 1)) * (1.0 / UNROLL)) * UNROLL
        bases = [jnp.zeros((1, LANES), F32)]
        for v in range(1, 16):
            bases.append(bases[-1] + sizes[v : v + 1, :])
        first = jnp.concatenate([bases[0]] + bases[:15], axis=0)
        sums = jnp.zeros((2 * (fanout + 2) * 16, LANES), F32)
        for i, c in enumerate(range(h * half, (h + 1) * half)):
            begin = (first + carries[i])[:, 0:1]
            spot = jnp.where(kinds[c], prefix[c * 16 : (c + 1) * 16, :] + begin, 0.0)
            spot = jnp.sum(spot, axis=0, keepdims=True).astype(I32)
            spot = jnp.where(keys[c] > 0, spot, -1)
            spot_lo = jnp.bitwise_and(spot, LANES - 1)
            spot_hi = jnp.right_shift(spot, 7)
            lane = (iota((LANES, per_owner), 0) == spot_lo).astype(F32).astype(BF16)
            at_hi = (iota((16, per_owner), 0) == spot_hi).astype(F32)
            columns = slice(c * per_owner, (c + 1) * per_owner)
            rows = [own_ids[:, columns]]
            rows += [neighbour_ids[k : k + 1, columns] for k in range(fanout)]
            rows += [half * CAP - (slot[c : c + 1, :] + i * CAP)]
            parts = []
            for row in rows:
                for byte in (jnp.right_shift(row, 8), jnp.bitwise_and(row, 255)):
                    value = jnp.broadcast_to(byte.astype(F32), (16, per_owner))
                    parts.append((at_hi * value).astype(BF16))
            sums = sums + lax.dot_general(
                jnp.concatenate(parts, axis=0),
                lane,
                (((1,), (1,)), ((), ())),
                preferred_element_type=F32,
            )
        for k in range(fanout + 2):
            hi = sums[32 * k : 32 * k + 16, :]
            lo = sums[32 * k + 16 : 32 * k + 32, :]
            value = (hi * 256.0 + lo).astype(I32)
            lists[h, k, :, :] = value if k <= fanout else half * CAP - value
        lane = iota((8, LANES), 1)
        begins = jnp.zeros((8, LANES), F32)
        for v in range(16):
            begins = begins + jnp.where(lane == v, bases[v], 0.0)
        lists[h, fanout + 2, 0:8, :] = begins.astype(I32)
        lists[h, fanout + 2, 8:16, :] = jnp.zeros((8, LANES), I32)


def list_copies(fanout, h, lists, ids, places, begins, sems):
    block = 16 * LANES

    def piece(k, length):
        at = pl.multiple_of((h * (fanout + 3) + k) * block, block)
        return lists.at[pl.ds(at, length)]

    last = fanout + 2
    copies = [
        pltpu.make_async_copy(piece(k, POSITIONS), ref, sems.at[k])
        for k, ref in enumerate(list(ids) + [places])
    ]
    copies.append(pltpu.make_async_copy(piece(last, LANES), begins, sems.at[last]))
    start_all(copies[fanout + 1 :] + copies[: fanout + 1])
    return copies


def look_up(fanout, copies, table, ids, places, begins, self_rows, mean_rows):
    for copy in [copies[0]] + copies[fanout + 1 :]:
        copy.wait()
    for v in range(1, fanout + 1):
        copies[v].wait()
        begin = begins[v - 1]
        end = begins[v]

        def body(i, carry, v=v, begin=begin):
            for u in range(UNROLL):
                at = begin + i * UNROLL + u
                to = places[at]
                self_rows[pl.ds(to, 1), :] = table[pl.ds(ids[0][at], 1), :]
                total = tree_sum([table[pl.ds(ids[k][at], 1), :] for k in range(1, v + 1)])
                mean_rows[pl.ds(to, 1), :] = total * (1.0 / v)
            return carry

        lax.fori_loop(0, jnp.right_shift(end - begin, UNROLL.bit_length() - 1), body, 0)


def write_out(x, width, self_rows, mean_rows, keep, send):
    valid = iota((CAP, LANES), 1) < width
    for z in range(2):
        for ref, side in ((keep, x), (send, 1 - x)):
            at = pl.multiple_of((z * 2 + side) * CAP, CAP)
            for part, rows in enumerate((self_rows, mean_rows)):
                block = jnp.where(valid, rows[pl.ds(at, CAP), :], 0.0).astype(BF16)
                ref[z, :, part * LANES : (part + 1) * LANES] = block


def stage(source, staged, sems):
    blocks, _, part = staged.shape
    copies = [
        pltpu.make_async_copy(source.at[:, pl.ds(b * part, part)], staged.at[b], sems.at[b])
        for b in range(blocks)
    ]
    start_all(copies)
    return copies


def turn_staged(copies, staged, table, base):
    part = staged.shape[2]
    for b, copy in enumerate(copies):
        copy.wait()
        turn(staged.at[b], table, pl.multiple_of(base + b * part, part))


def own_kernel(which, halves, me, features, *refs):
    table, staged, sems = refs[-3:]
    length = features.shape[1]
    half = length // halves
    copies = stage(features.at[:, pl.ds(which * half, half)], staged, sems)
    turn_staged(copies, staged, table, me[2] * length + which * half)


def join_kernel(*refs):
    *parts, out = refs
    at = 0
    for part in parts:
        out[at : at + part.shape[0], :] = part[...]
        at += part.shape[0]


def hand_out(keep, send, keep_hbm, send_hbm, sems):
    copies = [
        pltpu.make_async_copy(send, send_hbm, sems.at[0]),
        pltpu.make_async_copy(keep, keep_hbm, sems.at[1]),
    ]
    start_all(copies)
    for copy in copies:
        copy.wait()


def first_kernel(
    fanout, me, lists, table_in, other, self_one, neigh_one, table, keep_hbm, send_hbm, *scratch
):
    del table_in
    ids = scratch[: fanout + 1]
    places, begins, self_rows, mean_rows, sems = scratch[fanout + 1 : fanout + 6]
    staged, staged_sems, keep, send, out_sems = scratch[fanout + 6 :]
    width, length = other.shape
    x, h, rep = me[0], me[1], me[2]
    staging = stage(other, staged, staged_sems)
    copies = list_copies(fanout, h, lists, ids, places, begins, sems)
    self_rows[...] = jnp.zeros_like(self_rows)
    mean_rows[...] = jnp.zeros_like(mean_rows)
    send[2, :, :] = jnp.zeros(send.shape[1:], BF16)
    send[2, 0:width, :] = self_one[...]
    send[2, LANES : LANES + width, :] = neigh_one[...]
    turn_staged(staging, staged, table, (1 - rep) * length)
    look_up(fanout, copies, table, ids, places, begins, self_rows, mean_rows)
    write_out(x, width, self_rows, mean_rows, keep, send)
    hand_out(keep, send, keep_hbm, send_hbm, out_sems)


def second_kernel(fanout, width, me, lists, table, keep_hbm, send_hbm, *scratch):
    ids = scratch[: fanout + 1]
    places, begins, self_rows, mean_rows, sems, keep, send, out_sems = scratch[fanout + 1 :]
    x, h = me[0], 1 - me[1]
    copies = list_copies(fanout, h, lists, ids, places, begins, sems)
    self_rows[...] = jnp.zeros_like(self_rows)
    mean_rows[...] = jnp.zeros_like(mean_rows)
    look_up(fanout, copies, table, ids, places, begins, self_rows, mean_rows)
    write_out(x, width, self_rows, mean_rows, keep, send)
    hand_out(keep, send, keep_hbm, send_hbm, out_sems)


def project(zl, keep, got, weight, weight_got, outs):
    for which, out in ((zl, outs[0]), (1 - zl, outs[1])):
        out[...] = (
            jnp.dot(keep[which], weight[2, 0 : 2 * LANES, :], preferred_element_type=F32)
            + jnp.dot(got[which], weight_got[2, 0 : 2 * LANES, :], preferred_element_type=F32)
        ).astype(out.dtype)


def project_far_kernel(me, keep, got, sent, out_0, out_1):
    project(me[3], keep, got, sent, got, (out_0, out_1))


def project_near_kernel(me, keep_hbm, got, weight, weight_got, out_0, out_1, keep, sem):
    copy = pltpu.make_async_copy(keep_hbm, keep, sem)
    copy.start()
    copy.wait()
    project(me[3], keep, got, weight, weight_got, (out_0, out_1))


def last_kernel(
    mine, a, b, c, counts, bias_one, self_two, neigh_two, bias_two, out_weight, out_bias, out
):
    pre = mine[...] + a[...].astype(F32) + b[...].astype(F32) + c[...].astype(F32)
    hidden = jnp.maximum(pre + bias_one[...], 0.0).astype(BF16)
    seeds = counts.shape[1]
    same = iota((seeds, seeds), 0) == iota((seeds, seeds), 1)
    count = jnp.sum(jnp.where(same, counts[...].astype(F32), 0.0), axis=1, keepdims=True)
    count = count.astype(I32)
    earlier = (iota((seeds, seeds), 0) > iota((seeds, seeds), 1)).astype(BF16)
    needs = jnp.broadcast_to((count + 1).astype(F32), (seeds, LANES)).astype(BF16)
    offset = jnp.dot(earlier, needs, preferred_element_type=F32)[:, 0:1].astype(I32)
    place = iota((seeds, CAP), 1) - offset
    is_self = (place == 0).astype(F32).astype(BF16)
    is_near = ((place >= 1) & (place <= count)).astype(F32).astype(BF16)
    own = jnp.dot(is_self, hidden, preferred_element_type=F32).astype(BF16)
    total = jnp.dot(is_near, hidden, preferred_element_type=F32)
    mean = (total / count.astype(F32)).astype(BF16)
    pre_two = (
        jnp.dot(own, self_two[...], preferred_element_type=F32)
        + jnp.dot(mean, neigh_two[...], preferred_element_type=F32)
        + bias_two[...]
    )
    hidden_two = jnp.maximum(pre_two, 0.0).astype(BF16)
    logits = lax.dot_general(
        hidden_two, out_weight[...], (((1,), (1,)), ((), ())), preferred_element_type=F32
    )
    out[...] = logits + out_bias[...]


def params(limit):
    return pltpu.CompilerParams(vmem_limit_bytes=limit * MIB)


def shape(dims, dtype):
    return jax.ShapeDtypeStruct(dims, dtype)


def order_call(per_seed, me, own, got, self_ids, neighbour_ids, count_one):
    owners = sum(x.shape[0] for x in (own, *got))
    lists, most = pl.pallas_call(
        functools.partial(order_kernel, per_seed),
        out_shape=(shape((2, neighbour_ids.shape[0] + 3, 16, LANES), I32), shape((1,), I32)),
        in_specs=[SMEM] + [VMEM] * 8,
        out_specs=(VMEM, SMEM),
        scratch_shapes=[pltpu.VMEM((owners, own.shape[1]), I32)],
        compiler_params=params(10),
        name="order",
    )(me, own, *got, self_ids, neighbour_ids, count_one)
    return lists.reshape(-1), most[0]


def list_scratch(fanout):
    return (
        [pltpu.SMEM((POSITIONS,), I32) for _ in range(fanout + 2)]
        + [pltpu.SMEM((LANES,), I32)]
        + [pltpu.VMEM((4 * CAP + 8, LANES), F32) for _ in range(2)]
        + [pltpu.SemaphoreType.DMA((fanout + 3,))]
    )


def own_call(which, halves, me, features, *table):
    width, length = features.shape
    parts = 8 // halves
    return pl.pallas_call(
        functools.partial(own_kernel, which, halves),
        out_shape=shape((2 * length, LANES), F32),
        in_specs=[SMEM, HBM] + [VMEM] * len(table),
        out_specs=VMEM,
        scratch_shapes=[
            pltpu.VMEM((parts, width, length // 8), BF16),
            pltpu.SemaphoreType.DMA((parts,)),
        ],
        input_output_aliases={2: 0} if table else {},
        compiler_params=params(FIRST_MIB if table else OWN_MIB),
        name="own_rows",
    )(me, features, *table)


def join_call(*parts):
    rows = sum(part.shape[0] for part in parts)
    return pl.pallas_call(
        join_kernel,
        out_shape=shape((rows, parts[0].shape[1]), parts[0].dtype),
        in_specs=[VMEM] * len(parts),
        out_specs=VMEM,
        compiler_params=params(1),
        name="join",
    )(*parts)


def first_call(fanout, me, lists, table, other, self_one, neigh_one):
    width, length = other.shape
    keep, send = (2, CAP, 2 * LANES), (3, CAP, 2 * LANES)
    return pl.pallas_call(
        functools.partial(first_kernel, fanout),
        out_shape=(shape((2 * length, LANES), F32), pltpu.HBM(keep, BF16), pltpu.HBM(send, BF16)),
        in_specs=[SMEM, ANY, VMEM, HBM, VMEM, VMEM],
        out_specs=(VMEM, HBM, HBM),
        scratch_shapes=list_scratch(fanout)
        + [
            pltpu.VMEM((8, width, length // 8), BF16),
            pltpu.SemaphoreType.DMA((8,)),
            pltpu.VMEM(keep, BF16),
            pltpu.VMEM(send, BF16),
            pltpu.SemaphoreType.DMA((2,)),
        ],
        input_output_aliases={2: 0},
        compiler_params=params(FIRST_MIB),
        name="first_half",
    )(me, lists, table, other, self_one, neigh_one)


def second_call(fanout, width, me, lists, table):
    dims = (2, CAP, 2 * LANES)
    halves = pltpu.HBM(dims, BF16)
    return pl.pallas_call(
        functools.partial(second_kernel, fanout, width),
        out_shape=(halves, halves),
        in_specs=[SMEM, ANY, VMEM],
        out_specs=(HBM, HBM),
        scratch_shapes=list_scratch(fanout)
        + [pltpu.VMEM(dims, BF16) for _ in range(2)]
        + [pltpu.SemaphoreType.DMA((2,))],
        compiler_params=params(10),
        name="second_half",
    )(me, lists, table)


def project_far_call(me, keep, got, sent):
    part = shape((CAP, sent.shape[2]), BF16)
    return pl.pallas_call(
        project_far_kernel,
        out_shape=(part, part),
        in_specs=[SMEM, VMEM, VMEM, VMEM],
        out_specs=(VMEM, VMEM),
        compiler_params=params(10),
        name="project_far",
    )(me, keep, got, sent)


def project_near_call(me, keep, got, weight, weight_got):
    dims = (CAP, weight.shape[2])
    return pl.pallas_call(
        project_near_kernel,
        out_shape=(shape(dims, F32), shape(dims, BF16)),
        in_specs=[SMEM, HBM, VMEM, VMEM, VMEM],
        out_specs=(VMEM, VMEM),
        scratch_shapes=[pltpu.VMEM(keep.shape, BF16), pltpu.SemaphoreType.DMA],
        compiler_params=params(10),
        name="project_near",
    )(me, keep, got, weight, weight_got)


def last_call(*args):
    seeds = args[4].shape[1]
    classes = args[-1].shape[1]
    return pl.pallas_call(
        last_kernel,
        out_shape=shape((seeds, classes), F32),
        in_specs=[VMEM] * len(args),
        out_specs=VMEM,
        compiler_params=params(10),
        name="layer_two",
    )(*args)


def main(
    features,
    self_ids,
    neighbour_ids,
    count_one,
    count_two,
    self_one,
    neigh_one,
    bias_one,
    self_two,
    neigh_two,
    bias_two,
    out_weight,
    out_bias,
):
    owners = lax.axis_size("col")
    seeds = count_two.shape[0]
    per_owner = self_ids.shape[0] // owners
    per_seed = per_owner // seeds
    fanout = neighbour_ids.shape[0]
    width = features.shape[0]
    col = lax.axis_index("col")
    rep = lax.axis_index("rep")
    z = col // 2
    me = jnp.stack([col % 2, 1 - z // 2, rep, z % 2, col]).astype(I32)

    def across(value, bit):
        return lax.ppermute(value, "col", [(i, i ^ bit) for i in range(owners)])

    other = lax.ppermute(features, "rep", [(0, 1), (1, 0)])
    held = pltpu.with_memory_space_constraint(features, pltpu.HBM)
    own = count_two[None, :]
    got_1 = across(own, 1)
    table, got_1 = lax.optimization_barrier((own_call(0, 2, me, held), got_1))
    pair = join_call(own, got_1)
    got = tuple(across(pair, bit) for bit in (4, 6, 2))
    table, *got = lax.optimization_barrier((own_call(1, 2, me, held, table), *got))
    got = (got_1, got[2], got[0], got[1])
    lists, most = order_call(per_seed, me, own, got, self_ids, neighbour_ids, count_one)
    table, keep_far, send_far = first_call(
        fanout, me, lists, table, other, self_one, neigh_one
    )
    got_far = across(send_far, 1)
    keep_near, send_near = second_call(fanout, width, me, lists, table)
    far_0, far_1 = project_far_call(me, keep_far, got_far, send_far)
    far_0, far_1, send_near = lax.optimization_barrier((far_0, far_1, send_near))
    far = [across(far_0, 4), across(far_1, 6)]
    got_near = across(send_near, 1)
    near_0, near_1 = project_near_call(me, keep_near, got_near, send_far, got_far)
    far.append(across(near_1, 2))
    fast = last_call(
        near_0,
        *far,
        own,
        bias_one[None, :],
        self_two,
        neigh_two,
        bias_two[None, :],
        out_weight.T,
        out_bias[None, :],
    )
    return lax.cond(
        most > CAP,
        lambda: general(
            other,
            features,
            self_ids,
            neighbour_ids,
            count_one,
            count_two,
            self_one,
            neigh_one,
            bias_one,
            self_two,
            neigh_two,
            bias_two,
            out_weight,
            out_bias,
        ),
        lambda: fast,
    )


def local(*args):
    features, self_ids, neighbour_ids = args[0], args[1], args[2]
    sizes = (lax.axis_size("groups"), lax.axis_size("col"), lax.axis_size("rep"))
    small = (
        sizes == (2, 8, 2)
        and features.shape[0] <= LANES
        and features.shape[1] <= 32768
        and self_ids.shape[0] * (neighbour_ids.shape[0] + 1) <= 2**17
        and neighbour_ids.shape[0] <= 15
    )
    if small:
        return main(*args)
    return general(lax.ppermute(features, "rep", [(0, 1), (1, 0)]), *args)


def solution(mesh):
    placed = (
        P("col", ("groups", "rep")),
        P(("groups", "rep")),
        P(None, ("groups", "rep")),
        P(("groups", "rep")),
        P(("groups", "col", "rep")),
        P("col", None),
        P("col", None),
        P(),
        P(),
        P(),
        P(),
        P(),
        P(),
    )
    return jax.shard_map(
        local,
        mesh=mesh,
        in_specs=placed,
        out_specs=P(("groups", "col", "rep"), None),
        check_vma=False,
    )
```

```python
import functools

import jax
import jax.numpy as jnp
import numpy as np
from jax import lax
from jax.experimental import pallas as pl
from jax.experimental.pallas import tpu as pltpu
from jax.sharding import PartitionSpec as P

CAP = 272
UNROLL = 8
POSITIONS = 10 * 128
FIRST_MIB = 12
OWN_MIB = 18
LANES = 128
MIB = 2**20
BF16 = jnp.bfloat16
F32 = jnp.float32
I32 = jnp.int32


def gathered(value, axis):
    copies = jnp.broadcast_to(value[None], (lax.axis_size(axis),) + value.shape)
    pieces = lax.all_to_all(copies, axis, split_axis=0, concat_axis=0, tiled=True)
    return pieces.reshape((-1,) + value.shape[1:])


def general(
    other,
    features,
    self_ids,
    neighbour_ids,
    count_one,
    count_two,
    self_one,
    neigh_one,
    bias_one,
    self_two,
    neigh_two,
    bias_two,
    out_weight,
    out_bias,
):
    mine = jnp.where(lax.axis_index("rep") == 0, 0, 1)
    table_cols = jnp.where(
        mine == 0,
        jnp.concatenate([features, other], axis=1),
        jnp.concatenate([other, features], axis=1),
    )
    table_rows = table_cols.T
    blocks = lax.axis_size("col")
    total_rows = self_ids.shape[0]
    per_owner = total_rows // blocks
    fanout = neighbour_ids.shape[0]
    width = table_rows.shape[1]
    all_ids = jnp.concatenate([self_ids[None, :], neighbour_ids], axis=0)
    fetched = jnp.take(table_rows, all_ids, axis=0)
    self_x = fetched[0]
    mask = (jnp.arange(fanout)[:, None] < count_one[None, :]).astype(BF16)
    summed = jnp.einsum("kmc,km->mc", fetched[1:], mask, preferred_element_type=F32)
    mean_one = (summed / count_one[:, None].astype(F32)).astype(BF16)
    full_self, full_neigh = gathered(self_one, "col"), gathered(neigh_one, "col")
    stacked = jnp.stack([self_x, mean_one], axis=0).reshape(2, blocks, per_owner, width)
    pieces = lax.all_to_all(stacked, "col", split_axis=1, concat_axis=3, tiled=True)
    pre_one = jnp.dot(pieces[0, 0], full_self, preferred_element_type=F32) + jnp.dot(
        pieces[1, 0], full_neigh, preferred_element_type=F32
    )
    hidden_one = jax.nn.relu(pre_one + bias_one).astype(BF16)
    seeds = count_two.shape[0]
    hidden = hidden_one.shape[1]
    grouped = hidden_one.reshape(seeds, per_owner // seeds, hidden)
    mask_two = (jnp.arange(grouped.shape[1] - 1)[None, :] < count_two[:, None]).astype(BF16)
    summed_two = jnp.einsum("skh,sk->sh", grouped[:, 1:, :], mask_two, preferred_element_type=F32)
    mean_two = (summed_two / count_two[:, None].astype(F32)).astype(BF16)
    pre_two = jnp.dot(grouped[:, 0, :], self_two, preferred_element_type=F32) + jnp.dot(
        mean_two, neigh_two, preferred_element_type=F32
    )
    hidden_two = jax.nn.relu(pre_two + bias_two).astype(BF16)
    return jnp.dot(hidden_two, out_weight, preferred_element_type=F32) + out_bias


def iota(shape, dim):
    return lax.broadcasted_iota(I32, shape, dim)


def tree_sum(terms):
    while len(terms) > 1:
        odd = [terms[-1]] if len(terms) % 2 else []
        terms = [a + b for a, b in zip(terms[::2], terms[1::2])] + odd
    return terms[0]


VMEM = pl.BlockSpec(memory_space=pltpu.VMEM)
SMEM = pl.BlockSpec(memory_space=pltpu.SMEM)
HBM = pl.BlockSpec(memory_space=pltpu.HBM)
ANY = pl.BlockSpec(memory_space=pl.ANY)


def start_all(copies):
    for copy in copies:
        copy.start()


def turn(source, table, base):
    width, length = source.shape
    step = 512
    unroll = 8

    def body(i, carry):
        for u in range(unroll):
            off = pl.multiple_of((i * unroll + u) * step, step)
            rows = source[:, pl.ds(off, step)].T.astype(F32)
            table[pl.ds(pl.multiple_of(base + off, step), step), 0:width] = rows
        return carry

    lax.fori_loop(0, length // step // unroll, body, 0)


def order_kernel(
    per_seed, me, own, got_1, got_2, got_4, got_6, self_ids, neighbour_ids, count_one, lists, most, counts_rel
):
    owners, seeds = counts_rel.shape
    fanout = neighbour_ids.shape[0]
    per_owner = count_one.shape[0] // owners
    half = owners // 2
    mine = me[4]
    counts_rel[0:1, :] = own[...]
    counts_rel[1:2, :] = got_1[...]
    counts_rel[2:4, :] = got_2[...]
    counts_rel[4:6, :] = got_4[...]
    counts_rel[6:8, :] = got_6[...]
    own_ids = self_ids[...].reshape(1, owners * per_owner)
    ones = count_one[...].reshape(1, owners * per_owner)
    counts = jnp.concatenate(
        [counts_rel[pl.ds(jnp.bitwise_xor(mine, c), 1), :] for c in range(owners)], axis=0
    ).astype(F32)
    needs = (counts + 1.0).astype(BF16)
    most[0] = jnp.max(jnp.sum(counts + 1.0, axis=1, keepdims=True)).astype(I32)
    column = iota((seeds, per_owner), 1).astype(F32)
    seed_of = jnp.floor((column + 0.5) * (1.0 / per_seed))
    seed = iota((seeds, per_owner), 0).astype(F32)
    t = column[0:1, :] - seed_of[0:1, :] * per_seed
    of_row = jnp.dot(
        counts.astype(BF16), (seed == seed_of).astype(BF16), preferred_element_type=F32
    )
    slot = t + jnp.dot(needs, (seed < seed_of).astype(BF16), preferred_element_type=F32)
    used = (t <= of_row) & (slot < CAP)
    slot = slot.astype(I32)
    keys = [
        jnp.where(used[c : c + 1, :], ones[:, c * per_owner : (c + 1) * per_owner], 0)
        for c in range(owners)
    ]
    kinds = [
        iota((16, per_owner), 0) == jnp.broadcast_to(key, (16, per_owner)) for key in keys
    ]
    stacked = jnp.concatenate([k.astype(F32).astype(BF16) for k in kinds], axis=0)
    left = (iota((per_owner, per_owner), 0) < iota((per_owner, per_owner), 1)).astype(BF16)
    prefix = jnp.dot(stacked, left, preferred_element_type=F32)
    total = jnp.dot(stacked, jnp.ones((per_owner, LANES), BF16), preferred_element_type=F32)
    for h in range(2):
        carry = jnp.zeros((16, LANES), F32)
        carries = []
        for c in range(h * half, (h + 1) * half):
            carries.append(carry)
            carry = carry + total[c * 16 : (c + 1) * 16, :]
        sizes = jnp.floor((carry + (UNROLL - 1)) * (1.0 / UNROLL)) * UNROLL
        bases = [jnp.zeros((1, LANES), F32)]
        for v in range(1, 16):
            bases.append(bases[-1] + sizes[v : v + 1, :])
        first = jnp.concatenate([bases[0]] + bases[:15], axis=0)
        sums = jnp.zeros((2 * (fanout + 2) * 16, LANES), F32)
        for i, c in enumerate(range(h * half, (h + 1) * half)):
            begin = (first + carries[i])[:, 0:1]
            spot = jnp.where(kinds[c], prefix[c * 16 : (c + 1) * 16, :] + begin, 0.0)
            spot = jnp.sum(spot, axis=0, keepdims=True).astype(I32)
            spot = jnp.where(keys[c] > 0, spot, -1)
            spot_lo = jnp.bitwise_and(spot, LANES - 1)
            spot_hi = jnp.right_shift(spot, 7)
            lane = (iota((LANES, per_owner), 0) == spot_lo).astype(F32).astype(BF16)
            at_hi = (iota((16, per_owner), 0) == spot_hi).astype(F32)
            columns = slice(c * per_owner, (c + 1) * per_owner)
            rows = [own_ids[:, columns]]
            rows += [neighbour_ids[k : k + 1, columns] for k in range(fanout)]
            rows += [half * CAP - (slot[c : c + 1, :] + i * CAP)]
            parts = []
            for row in rows:
                for byte in (jnp.right_shift(row, 8), jnp.bitwise_and(row, 255)):
                    value = jnp.broadcast_to(byte.astype(F32), (16, per_owner))
                    parts.append((at_hi * value).astype(BF16))
            sums = sums + lax.dot_general(
                jnp.concatenate(parts, axis=0),
                lane,
                (((1,), (1,)), ((), ())),
                preferred_element_type=F32,
            )
        for k in range(fanout + 2):
            hi = sums[32 * k : 32 * k + 16, :]
            lo = sums[32 * k + 16 : 32 * k + 32, :]
            value = (hi * 256.0 + lo).astype(I32)
            lists[h, k, :, :] = value if k <= fanout else half * CAP - value
        lane = iota((8, LANES), 1)
        begins = jnp.zeros((8, LANES), F32)
        for v in range(16):
            begins = begins + jnp.where(lane == v, bases[v], 0.0)
        lists[h, fanout + 2, 0:8, :] = begins.astype(I32)
        lists[h, fanout + 2, 8:16, :] = jnp.zeros((8, LANES), I32)


def list_copies(fanout, h, lists, ids, places, begins, sems):
    block = 16 * LANES

    def piece(k, length):
        at = pl.multiple_of((h * (fanout + 3) + k) * block, block)
        return lists.at[pl.ds(at, length)]

    last = fanout + 2
    copies = [
        pltpu.make_async_copy(piece(k, POSITIONS), ref, sems.at[k])
        for k, ref in enumerate(list(ids) + [places])
    ]
    copies.append(pltpu.make_async_copy(piece(last, LANES), begins, sems.at[last]))
    start_all(copies[fanout + 1 :] + copies[: fanout + 1])
    return copies


def look_up(fanout, copies, table, ids, places, begins, self_rows, mean_rows):
    for copy in [copies[0]] + copies[fanout + 1 :]:
        copy.wait()
    for v in range(1, fanout + 1):
        copies[v].wait()
        begin = begins[v - 1]
        end = begins[v]

        def body(i, carry, v=v, begin=begin):
            for u in range(UNROLL):
                at = begin + i * UNROLL + u
                to = places[at]
                self_rows[pl.ds(to, 1), :] = table[pl.ds(ids[0][at], 1), :]
                total = tree_sum([table[pl.ds(ids[k][at], 1), :] for k in range(1, v + 1)])
                mean_rows[pl.ds(to, 1), :] = total * (1.0 / v)
            return carry

        lax.fori_loop(0, jnp.right_shift(end - begin, UNROLL.bit_length() - 1), body, 0)


def write_out(x, width, self_rows, mean_rows, keep, send):
    valid = iota((CAP, LANES), 1) < width
    for z in range(2):
        for ref, side in ((keep, x), (send, 1 - x)):
            at = pl.multiple_of((z * 2 + side) * CAP, CAP)
            for part, rows in enumerate((self_rows, mean_rows)):
                block = jnp.where(valid, rows[pl.ds(at, CAP), :], 0.0).astype(BF16)
                ref[z, :, part * LANES : (part + 1) * LANES] = block


def stage(source, staged, sems):
    blocks, _, part = staged.shape
    copies = [
        pltpu.make_async_copy(source.at[:, pl.ds(b * part, part)], staged.at[b], sems.at[b])
        for b in range(blocks)
    ]
    start_all(copies)
    return copies


def turn_staged(copies, staged, table, base):
    part = staged.shape[2]
    for b, copy in enumerate(copies):
        copy.wait()
        turn(staged.at[b], table, pl.multiple_of(base + b * part, part))


def own_kernel(which, halves, me, features, *refs):
    table, staged, sems = refs[-3:]
    length = features.shape[1]
    half = length // halves
    copies = stage(features.at[:, pl.ds(which * half, half)], staged, sems)
    turn_staged(copies, staged, table, me[2] * length + which * half)


def join_kernel(*refs):
    *parts, out = refs
    at = 0
    for part in parts:
        out[at : at + part.shape[0], :] = part[...]
        at += part.shape[0]


def hand_out(keep, send, keep_hbm, send_hbm, sems):
    copies = [
        pltpu.make_async_copy(send, send_hbm, sems.at[0]),
        pltpu.make_async_copy(keep, keep_hbm, sems.at[1]),
    ]
    start_all(copies)
    for copy in copies:
        copy.wait()


def first_kernel(
    fanout, me, lists, table_in, other, table, keep_hbm, send_hbm, *scratch
):
    del table_in
    ids = scratch[: fanout + 1]
    places, begins, self_rows, mean_rows, sems = scratch[fanout + 1 : fanout + 6]
    staged, staged_sems, keep, send, out_sems = scratch[fanout + 6 :]
    width, length = other.shape
    x, h, rep = me[0], me[1], me[2]
    staging = stage(other, staged, staged_sems)
    copies = list_copies(fanout, h, lists, ids, places, begins, sems)
    self_rows[...] = jnp.zeros_like(self_rows)
    mean_rows[...] = jnp.zeros_like(mean_rows)
    turn_staged(staging, staged, table, (1 - rep) * length)
    look_up(fanout, copies, table, ids, places, begins, self_rows, mean_rows)
    write_out(x, width, self_rows, mean_rows, keep, send)
    hand_out(keep, send, keep_hbm, send_hbm, out_sems)


def second_kernel(fanout, width, me, lists, table, keep_hbm, send_hbm, *scratch):
    ids = scratch[: fanout + 1]
    places, begins, self_rows, mean_rows, sems, keep, send, out_sems = scratch[fanout + 1 :]
    x, h = me[0], 1 - me[1]
    copies = list_copies(fanout, h, lists, ids, places, begins, sems)
    self_rows[...] = jnp.zeros_like(self_rows)
    mean_rows[...] = jnp.zeros_like(mean_rows)
    look_up(fanout, copies, table, ids, places, begins, self_rows, mean_rows)
    write_out(x, width, self_rows, mean_rows, keep, send)
    hand_out(keep, send, keep_hbm, send_hbm, out_sems)


def partial(rows, self_one, neigh_one):
    width = self_one.shape[0]
    return jnp.dot(rows[:, 0:width], self_one[...], preferred_element_type=F32) + jnp.dot(
        rows[:, LANES : LANES + width], neigh_one[...], preferred_element_type=F32
    )


def far_kernel(me, keep, got, self_one, neigh_one, self_got, neigh_got, out_0, out_1):
    zl = me[3]
    for which, out in ((zl, out_0), (1 - zl, out_1)):
        total = partial(keep[which], self_one, neigh_one) + partial(got[which], self_got, neigh_got)
        out[...] = total.astype(BF16)


def own_near_kernel(keep, self_one, neigh_one, out):
    for z in range(2):
        out[z, :, :] = partial(keep[z], self_one, neigh_one)


def near_kernel(me, own, got, self_got, neigh_got, out_0, out_1):
    zl = me[3]
    out_0[...] = own[zl] + partial(got[zl], self_got, neigh_got)
    out_1[...] = (own[1 - zl] + partial(got[1 - zl], self_got, neigh_got)).astype(BF16)


def last_kernel(
    mine, a, b, c, counts, bias_one, self_two, neigh_two, bias_two, out_weight, out_bias, out
):
    pre = mine[...] + a[...].astype(F32) + b[...].astype(F32) + c[...].astype(F32)
    hidden = jnp.maximum(pre + bias_one[...], 0.0).astype(BF16)
    seeds = counts.shape[1]
    same = iota((seeds, seeds), 0) == iota((seeds, seeds), 1)
    count = jnp.sum(jnp.where(same, counts[...].astype(F32), 0.0), axis=1, keepdims=True)
    count = count.astype(I32)
    earlier = (iota((seeds, seeds), 0) > iota((seeds, seeds), 1)).astype(BF16)
    needs = jnp.broadcast_to((count + 1).astype(F32), (seeds, LANES)).astype(BF16)
    offset = jnp.dot(earlier, needs, preferred_element_type=F32)[:, 0:1].astype(I32)
    place = iota((seeds, CAP), 1) - offset
    is_self = (place == 0).astype(F32).astype(BF16)
    is_near = ((place >= 1) & (place <= count)).astype(F32).astype(BF16)
    own = jnp.dot(is_self, hidden, preferred_element_type=F32).astype(BF16)
    total = jnp.dot(is_near, hidden, preferred_element_type=F32)
    mean = (total / count.astype(F32)).astype(BF16)
    pre_two = (
        jnp.dot(own, self_two[...], preferred_element_type=F32)
        + jnp.dot(mean, neigh_two[...], preferred_element_type=F32)
        + bias_two[...]
    )
    hidden_two = jnp.maximum(pre_two, 0.0).astype(BF16)
    logits = lax.dot_general(
        hidden_two, out_weight[...], (((1,), (1,)), ((), ())), preferred_element_type=F32
    )
    out[...] = logits + out_bias[...]


def params(limit):
    return pltpu.CompilerParams(vmem_limit_bytes=limit * MIB)


def shape(dims, dtype):
    return jax.ShapeDtypeStruct(dims, dtype)


def order_call(per_seed, me, own, got, self_ids, neighbour_ids, count_one):
    owners = sum(x.shape[0] for x in (own, *got))
    lists, most = pl.pallas_call(
        functools.partial(order_kernel, per_seed),
        out_shape=(shape((2, neighbour_ids.shape[0] + 3, 16, LANES), I32), shape((1,), I32)),
        in_specs=[SMEM] + [VMEM] * 8,
        out_specs=(VMEM, SMEM),
        scratch_shapes=[pltpu.VMEM((owners, own.shape[1]), I32)],
        compiler_params=params(10),
        name="order",
    )(me, own, *got, self_ids, neighbour_ids, count_one)
    return lists.reshape(-1), most[0]


def list_scratch(fanout):
    return (
        [pltpu.SMEM((POSITIONS,), I32) for _ in range(fanout + 2)]
        + [pltpu.SMEM((LANES,), I32)]
        + [pltpu.VMEM((4 * CAP + 8, LANES), F32) for _ in range(2)]
        + [pltpu.SemaphoreType.DMA((fanout + 3,))]
    )


def own_call(which, halves, me, features, *table):
    width, length = features.shape
    parts = 8 // halves
    return pl.pallas_call(
        functools.partial(own_kernel, which, halves),
        out_shape=shape((2 * length, LANES), F32),
        in_specs=[SMEM, HBM] + [VMEM] * len(table),
        out_specs=VMEM,
        scratch_shapes=[
            pltpu.VMEM((parts, width, length // 8), BF16),
            pltpu.SemaphoreType.DMA((parts,)),
        ],
        input_output_aliases={2: 0} if table else {},
        compiler_params=params(FIRST_MIB if table else OWN_MIB),
        name="own_rows",
    )(me, features, *table)


def join_call(*parts):
    rows = sum(part.shape[0] for part in parts)
    return pl.pallas_call(
        join_kernel,
        out_shape=shape((rows, parts[0].shape[1]), parts[0].dtype),
        in_specs=[VMEM] * len(parts),
        out_specs=VMEM,
        compiler_params=params(1),
        name="join",
    )(*parts)


def first_call(fanout, me, lists, table, other):
    width, length = other.shape
    dims = (2, CAP, 2 * LANES)
    return pl.pallas_call(
        functools.partial(first_kernel, fanout),
        out_shape=(shape((2 * length, LANES), F32), pltpu.HBM(dims, BF16), pltpu.HBM(dims, BF16)),
        in_specs=[SMEM, ANY, VMEM, HBM],
        out_specs=(VMEM, HBM, HBM),
        scratch_shapes=list_scratch(fanout)
        + [
            pltpu.VMEM((8, width, length // 8), BF16),
            pltpu.SemaphoreType.DMA((8,)),
            pltpu.VMEM(dims, BF16),
            pltpu.VMEM(dims, BF16),
            pltpu.SemaphoreType.DMA((2,)),
        ],
        input_output_aliases={2: 0},
        compiler_params=params(FIRST_MIB),
        name="first_half",
    )(me, lists, table, other)


def second_call(fanout, width, me, lists, table):
    dims = (2, CAP, 2 * LANES)
    halves = pltpu.HBM(dims, BF16)
    return pl.pallas_call(
        functools.partial(second_kernel, fanout, width),
        out_shape=(halves, halves),
        in_specs=[SMEM, ANY, VMEM],
        out_specs=(HBM, HBM),
        scratch_shapes=list_scratch(fanout)
        + [pltpu.VMEM(dims, BF16) for _ in range(2)]
        + [pltpu.SemaphoreType.DMA((2,))],
        compiler_params=params(10),
        name="second_half",
    )(me, lists, table)


def far_call(me, keep, got, *weights):
    part = shape((CAP, weights[0].shape[1]), BF16)
    return pl.pallas_call(
        far_kernel,
        out_shape=(part, part),
        in_specs=[SMEM] + [VMEM] * 6,
        out_specs=(VMEM, VMEM),
        compiler_params=params(10),
        name="project_far",
    )(me, keep, got, *weights)


def own_near_call(keep, *weights):
    return pl.pallas_call(
        own_near_kernel,
        out_shape=shape((2, CAP, weights[0].shape[1]), F32),
        in_specs=[VMEM] * 3,
        out_specs=VMEM,
        compiler_params=params(10),
        name="project_own_near",
    )(keep, *weights)


def near_call(me, own, got, *weights):
    dims = (CAP, weights[0].shape[1])
    return pl.pallas_call(
        near_kernel,
        out_shape=(shape(dims, F32), shape(dims, BF16)),
        in_specs=[SMEM] + [VMEM] * 4,
        out_specs=(VMEM, VMEM),
        compiler_params=params(10),
        name="project_near",
    )(me, own, got, *weights)


def last_call(*args):
    seeds = args[4].shape[1]
    classes = args[-1].shape[1]
    return pl.pallas_call(
        last_kernel,
        out_shape=shape((seeds, classes), F32),
        in_specs=[VMEM] * len(args),
        out_specs=VMEM,
        compiler_params=params(10),
        name="layer_two",
    )(*args)


def main(
    features,
    self_ids,
    neighbour_ids,
    count_one,
    count_two,
    self_one,
    neigh_one,
    bias_one,
    self_two,
    neigh_two,
    bias_two,
    out_weight,
    out_bias,
):
    owners = lax.axis_size("col")
    seeds = count_two.shape[0]
    per_owner = self_ids.shape[0] // owners
    per_seed = per_owner // seeds
    fanout = neighbour_ids.shape[0]
    width = features.shape[0]
    col = lax.axis_index("col")
    rep = lax.axis_index("rep")
    z = col // 2
    me = jnp.stack([col % 2, 1 - z // 2, rep, z % 2, col]).astype(I32)

    def across(value, bit):
        return lax.ppermute(value, "col", [(i, i ^ bit) for i in range(owners)])

    other = lax.ppermute(features, "rep", [(0, 1), (1, 0)])
    held = pltpu.with_memory_space_constraint(features, pltpu.HBM)
    own = count_two[None, :]
    got_1 = across(own, 1)
    weights_got = (across(self_one, 1), across(neigh_one, 1))
    table, got_1, weights_got = lax.optimization_barrier(
        (own_call(0, 2, me, held), got_1, weights_got)
    )
    pair = join_call(own, got_1)
    got = tuple(across(pair, bit) for bit in (4, 6, 2))
    table, got = lax.optimization_barrier((own_call(1, 2, me, held, table), got))
    got = (got_1, got[2], got[0], got[1])
    lists, most = order_call(per_seed, me, own, got, self_ids, neighbour_ids, count_one)
    table, keep_far, send_far = first_call(fanout, me, lists, table, other)
    got_far = across(send_far, 1)
    keep_near, send_near = second_call(fanout, width, me, lists, table)
    far = far_call(me, keep_far, got_far, self_one, neigh_one, *weights_got)
    far, send_near, keep_near = lax.optimization_barrier((far, send_near, keep_near))
    far_got = [across(far[0], 4), across(far[1], 6)]
    got_near = across(send_near, 1)
    own_near = own_near_call(keep_near, self_one, neigh_one)
    near = near_call(me, own_near, got_near, *weights_got)
    far_got.append(across(near[1], 2))
    fast = last_call(
        near[0],
        *far_got,
        own,
        bias_one[None, :],
        self_two,
        neigh_two,
        bias_two[None, :],
        out_weight.T,
        out_bias[None, :],
    )
    return lax.cond(
        most > CAP,
        lambda: general(
            other,
            features,
            self_ids,
            neighbour_ids,
            count_one,
            count_two,
            self_one,
            neigh_one,
            bias_one,
            self_two,
            neigh_two,
            bias_two,
            out_weight,
            out_bias,
        ),
        lambda: fast,
    )


def local(*args):
    features, self_ids, neighbour_ids = args[0], args[1], args[2]
    sizes = (lax.axis_size("groups"), lax.axis_size("col"), lax.axis_size("rep"))
    small = (
        sizes == (2, 8, 2)
        and features.shape[0] <= LANES
        and features.shape[1] <= 32768
        and self_ids.shape[0] * (neighbour_ids.shape[0] + 1) <= 2**17
        and neighbour_ids.shape[0] <= 15
    )
    if small:
        return main(*args)
    return general(lax.ppermute(features, "rep", [(0, 1), (1, 0)]), *args)


def solution(mesh):
    placed = (
        P("col", ("groups", "rep")),
        P(("groups", "rep")),
        P(None, ("groups", "rep")),
        P(("groups", "rep")),
        P(("groups", "col", "rep")),
        P("col", None),
        P("col", None),
        P(),
        P(),
        P(),
        P(),
        P(),
        P(),
    )
    return jax.shard_map(
        local,
        mesh=mesh,
        in_specs=placed,
        out_specs=P(("groups", "col", "rep"), None),
        check_vma=False,
    )
```

```python
import functools

import jax
import jax.numpy as jnp
import numpy as np
from jax import lax
from jax.experimental import pallas as pl
from jax.experimental.pallas import tpu as pltpu
from jax.sharding import PartitionSpec as P

CAP = 272
UNROLL = 8
POSITIONS = 10 * 128
FIRST_MIB = 12
OWN_MIB = 18
LANES = 128
MIB = 2**20
BF16 = jnp.bfloat16
F32 = jnp.float32
I32 = jnp.int32


def gathered(value, axis):
    copies = jnp.broadcast_to(value[None], (lax.axis_size(axis),) + value.shape)
    pieces = lax.all_to_all(copies, axis, split_axis=0, concat_axis=0, tiled=True)
    return pieces.reshape((-1,) + value.shape[1:])


def general(
    other,
    features,
    self_ids,
    neighbour_ids,
    count_one,
    count_two,
    self_one,
    neigh_one,
    bias_one,
    self_two,
    neigh_two,
    bias_two,
    out_weight,
    out_bias,
):
    mine = jnp.where(lax.axis_index("rep") == 0, 0, 1)
    table_cols = jnp.where(
        mine == 0,
        jnp.concatenate([features, other], axis=1),
        jnp.concatenate([other, features], axis=1),
    )
    table_rows = table_cols.T
    blocks = lax.axis_size("col")
    total_rows = self_ids.shape[0]
    per_owner = total_rows // blocks
    fanout = neighbour_ids.shape[0]
    width = table_rows.shape[1]
    all_ids = jnp.concatenate([self_ids[None, :], neighbour_ids], axis=0)
    fetched = jnp.take(table_rows, all_ids, axis=0)
    self_x = fetched[0]
    mask = (jnp.arange(fanout)[:, None] < count_one[None, :]).astype(BF16)
    summed = jnp.einsum("kmc,km->mc", fetched[1:], mask, preferred_element_type=F32)
    mean_one = (summed / count_one[:, None].astype(F32)).astype(BF16)
    full_self, full_neigh = gathered(self_one, "col"), gathered(neigh_one, "col")
    stacked = jnp.stack([self_x, mean_one], axis=0).reshape(2, blocks, per_owner, width)
    pieces = lax.all_to_all(stacked, "col", split_axis=1, concat_axis=3, tiled=True)
    pre_one = jnp.dot(pieces[0, 0], full_self, preferred_element_type=F32) + jnp.dot(
        pieces[1, 0], full_neigh, preferred_element_type=F32
    )
    hidden_one = jax.nn.relu(pre_one + bias_one).astype(BF16)
    seeds = count_two.shape[0]
    hidden = hidden_one.shape[1]
    grouped = hidden_one.reshape(seeds, per_owner // seeds, hidden)
    mask_two = (jnp.arange(grouped.shape[1] - 1)[None, :] < count_two[:, None]).astype(BF16)
    summed_two = jnp.einsum("skh,sk->sh", grouped[:, 1:, :], mask_two, preferred_element_type=F32)
    mean_two = (summed_two / count_two[:, None].astype(F32)).astype(BF16)
    pre_two = jnp.dot(grouped[:, 0, :], self_two, preferred_element_type=F32) + jnp.dot(
        mean_two, neigh_two, preferred_element_type=F32
    )
    hidden_two = jax.nn.relu(pre_two + bias_two).astype(BF16)
    return jnp.dot(hidden_two, out_weight, preferred_element_type=F32) + out_bias


def iota(shape, dim):
    return lax.broadcasted_iota(I32, shape, dim)


def tree_sum(terms):
    while len(terms) > 1:
        odd = [terms[-1]] if len(terms) % 2 else []
        terms = [a + b for a, b in zip(terms[::2], terms[1::2])] + odd
    return terms[0]


VMEM = pl.BlockSpec(memory_space=pltpu.VMEM)
SMEM = pl.BlockSpec(memory_space=pltpu.SMEM)
HBM = pl.BlockSpec(memory_space=pltpu.HBM)
ANY = pl.BlockSpec(memory_space=pl.ANY)


def start_all(copies):
    for copy in copies:
        copy.start()


def turn(source, table, base):
    width, length = source.shape
    step = 512
    unroll = 8

    def body(i, carry):
        for u in range(unroll):
            off = pl.multiple_of((i * unroll + u) * step, step)
            rows = source[:, pl.ds(off, step)].T.astype(F32)
            table[pl.ds(pl.multiple_of(base + off, step), step), 0:width] = rows
        return carry

    lax.fori_loop(0, length // step // unroll, body, 0)


def order_kernel(
    per_seed, me, own, got_1, got_2, got_4, got_6, self_ids, neighbour_ids, count_one, lists, most, counts_rel
):
    owners, seeds = counts_rel.shape
    fanout = neighbour_ids.shape[0]
    per_owner = count_one.shape[0] // owners
    half = owners // 2
    mine = me[4]
    counts_rel[0:1, :] = own[...]
    counts_rel[1:2, :] = got_1[...]
    counts_rel[2:4, :] = got_2[...]
    counts_rel[4:6, :] = got_4[...]
    counts_rel[6:8, :] = got_6[...]
    own_ids = self_ids[...].reshape(1, owners * per_owner)
    ones = count_one[...].reshape(1, owners * per_owner)
    counts = jnp.concatenate(
        [counts_rel[pl.ds(jnp.bitwise_xor(mine, c), 1), :] for c in range(owners)], axis=0
    ).astype(F32)
    needs = (counts + 1.0).astype(BF16)
    most[0] = jnp.max(jnp.sum(counts + 1.0, axis=1, keepdims=True)).astype(I32)
    column = iota((seeds, per_owner), 1).astype(F32)
    seed_of = jnp.floor((column + 0.5) * (1.0 / per_seed))
    seed = iota((seeds, per_owner), 0).astype(F32)
    t = column[0:1, :] - seed_of[0:1, :] * per_seed
    of_row = jnp.dot(
        counts.astype(BF16), (seed == seed_of).astype(BF16), preferred_element_type=F32
    )
    slot = t + jnp.dot(needs, (seed < seed_of).astype(BF16), preferred_element_type=F32)
    used = (t <= of_row) & (slot < CAP)
    slot = slot.astype(I32)
    keys = [
        jnp.where(used[c : c + 1, :], ones[:, c * per_owner : (c + 1) * per_owner], 0)
        for c in range(owners)
    ]
    kinds = [
        iota((16, per_owner), 0) == jnp.broadcast_to(key, (16, per_owner)) for key in keys
    ]
    stacked = jnp.concatenate([k.astype(F32).astype(BF16) for k in kinds], axis=0)
    left = (iota((per_owner, per_owner), 0) < iota((per_owner, per_owner), 1)).astype(BF16)
    prefix = jnp.dot(stacked, left, preferred_element_type=F32)
    total = jnp.dot(stacked, jnp.ones((per_owner, LANES), BF16), preferred_element_type=F32)
    for h in range(2):
        carry = jnp.zeros((16, LANES), F32)
        carries = []
        for c in range(h * half, (h + 1) * half):
            carries.append(carry)
            carry = carry + total[c * 16 : (c + 1) * 16, :]
        sizes = jnp.floor((carry + (UNROLL - 1)) * (1.0 / UNROLL)) * UNROLL
        bases = [jnp.zeros((1, LANES), F32)]
        for v in range(1, 16):
            bases.append(bases[-1] + sizes[v : v + 1, :])
        first = jnp.concatenate([bases[0]] + bases[:15], axis=0)
        sums = jnp.zeros((2 * (fanout + 2) * 16, LANES), F32)
        for i, c in enumerate(range(h * half, (h + 1) * half)):
            begin = (first + carries[i])[:, 0:1]
            spot = jnp.where(kinds[c], prefix[c * 16 : (c + 1) * 16, :] + begin, 0.0)
            spot = jnp.sum(spot, axis=0, keepdims=True).astype(I32)
            spot = jnp.where(keys[c] > 0, spot, -1)
            spot_lo = jnp.bitwise_and(spot, LANES - 1)
            spot_hi = jnp.right_shift(spot, 7)
            lane = (iota((LANES, per_owner), 0) == spot_lo).astype(F32).astype(BF16)
            at_hi = (iota((16, per_owner), 0) == spot_hi).astype(F32)
            columns = slice(c * per_owner, (c + 1) * per_owner)
            rows = [own_ids[:, columns]]
            rows += [neighbour_ids[k : k + 1, columns] for k in range(fanout)]
            rows += [half * CAP - (slot[c : c + 1, :] + i * CAP)]
            parts = []
            for row in rows:
                for byte in (jnp.right_shift(row, 8), jnp.bitwise_and(row, 255)):
                    value = jnp.broadcast_to(byte.astype(F32), (16, per_owner))
                    parts.append((at_hi * value).astype(BF16))
            sums = sums + lax.dot_general(
                jnp.concatenate(parts, axis=0),
                lane,
                (((1,), (1,)), ((), ())),
                preferred_element_type=F32,
            )
        for k in range(fanout + 2):
            hi = sums[32 * k : 32 * k + 16, :]
            lo = sums[32 * k + 16 : 32 * k + 32, :]
            value = (hi * 256.0 + lo).astype(I32)
            lists[h, k, :, :] = value if k <= fanout else half * CAP - value
        lane = iota((8, LANES), 1)
        begins = jnp.zeros((8, LANES), F32)
        for v in range(16):
            begins = begins + jnp.where(lane == v, bases[v], 0.0)
        lists[h, fanout + 2, 0:8, :] = begins.astype(I32)
        lists[h, fanout + 2, 8:16, :] = jnp.zeros((8, LANES), I32)


def list_copies(fanout, h, lists, ids, places, begins, sems):
    block = 16 * LANES

    def piece(k, length):
        at = pl.multiple_of((h * (fanout + 3) + k) * block, block)
        return lists.at[pl.ds(at, length)]

    last = fanout + 2
    copies = [
        pltpu.make_async_copy(piece(k, POSITIONS), ref, sems.at[k])
        for k, ref in enumerate(list(ids) + [places])
    ]
    copies.append(pltpu.make_async_copy(piece(last, LANES), begins, sems.at[last]))
    start_all(copies[fanout + 1 :] + copies[: fanout + 1])
    return copies


def look_up(fanout, copies, table, ids, places, begins, self_rows, mean_rows):
    for copy in [copies[0]] + copies[fanout + 1 :]:
        copy.wait()
    for v in range(1, fanout + 1):
        copies[v].wait()
        begin = begins[v - 1]
        end = begins[v]

        def body(i, carry, v=v, begin=begin):
            for u in range(UNROLL):
                at = begin + i * UNROLL + u
                to = places[at]
                self_rows[pl.ds(to, 1), :] = table[pl.ds(ids[0][at], 1), :]
                total = tree_sum([table[pl.ds(ids[k][at], 1), :] for k in range(1, v + 1)])
                mean_rows[pl.ds(to, 1), :] = total * (1.0 / v)
            return carry

        lax.fori_loop(0, jnp.right_shift(end - begin, UNROLL.bit_length() - 1), body, 0)


def write_out(x, width, self_rows, mean_rows, keep, send):
    valid = iota((CAP, LANES), 1) < width
    for z in range(2):
        for ref, side in ((keep, x), (send, 1 - x)):
            at = pl.multiple_of((z * 2 + side) * CAP, CAP)
            for part, rows in enumerate((self_rows, mean_rows)):
                block = jnp.where(valid, rows[pl.ds(at, CAP), :], 0.0).astype(BF16)
                ref[z, :, part * LANES : (part + 1) * LANES] = block


def stage(source, staged, sems):
    blocks, _, part = staged.shape
    copies = [
        pltpu.make_async_copy(source.at[:, pl.ds(b * part, part)], staged.at[b], sems.at[b])
        for b in range(blocks)
    ]
    start_all(copies)
    return copies


def turn_staged(copies, staged, table, base):
    part = staged.shape[2]
    for b, copy in enumerate(copies):
        copy.wait()
        turn(staged.at[b], table, pl.multiple_of(base + b * part, part))


def own_kernel(which, halves, me, features, *refs):
    table, staged, sems = refs[-3:]
    length = features.shape[1]
    half = length // halves
    copies = stage(features.at[:, pl.ds(which * half, half)], staged, sems)
    turn_staged(copies, staged, table, me[2] * length + which * half)


def join_kernel(*refs):
    *parts, out = refs
    at = 0
    for part in parts:
        out[at : at + part.shape[0], :] = part[...]
        at += part.shape[0]


def hand_out(keep, send, keep_hbm, send_hbm, sems):
    copies = [
        pltpu.make_async_copy(send, send_hbm, sems.at[0]),
        pltpu.make_async_copy(keep, keep_hbm, sems.at[1]),
    ]
    start_all(copies)
    for copy in copies:
        copy.wait()


def first_kernel(
    fanout, me, lists, table_in, other, table, keep_hbm, send_hbm, *scratch
):
    del table_in
    ids = scratch[: fanout + 1]
    places, begins, self_rows, mean_rows, sems = scratch[fanout + 1 : fanout + 6]
    staged, staged_sems, keep, send, out_sems = scratch[fanout + 6 :]
    width, length = other.shape
    x, h, rep = me[0], me[1], me[2]
    staging = stage(other, staged, staged_sems)
    copies = list_copies(fanout, h, lists, ids, places, begins, sems)
    self_rows[...] = jnp.zeros_like(self_rows)
    mean_rows[...] = jnp.zeros_like(mean_rows)
    turn_staged(staging, staged, table, (1 - rep) * length)
    look_up(fanout, copies, table, ids, places, begins, self_rows, mean_rows)
    write_out(x, width, self_rows, mean_rows, keep, send)
    hand_out(keep, send, keep_hbm, send_hbm, out_sems)


def second_kernel(fanout, width, me, lists, table, keep_hbm, send_hbm, *scratch):
    ids = scratch[: fanout + 1]
    places, begins, self_rows, mean_rows, sems, keep, send, out_sems = scratch[fanout + 1 :]
    x, h = me[0], 1 - me[1]
    copies = list_copies(fanout, h, lists, ids, places, begins, sems)
    self_rows[...] = jnp.zeros_like(self_rows)
    mean_rows[...] = jnp.zeros_like(mean_rows)
    look_up(fanout, copies, table, ids, places, begins, self_rows, mean_rows)
    write_out(x, width, self_rows, mean_rows, keep, send)
    hand_out(keep, send, keep_hbm, send_hbm, out_sems)


def partial(rows, weights):
    width = weights.shape[0] // 2
    return jnp.dot(rows[:, 0:width], weights[0:width, :], preferred_element_type=F32) + jnp.dot(
        rows[:, LANES : LANES + width], weights[width:, :], preferred_element_type=F32
    )


def far_kernel(me, keep, got, weights, weights_got, out_0, out_1):
    zl = me[3]
    for which, out in ((zl, out_0), (1 - zl, out_1)):
        total = partial(keep[which], weights) + partial(got[which], weights_got)
        out[...] = total.astype(BF16)


def near_kernel(me, keep_hbm, got, weights, weights_got, out_0, out_1, keep, sem):
    copy = pltpu.make_async_copy(keep_hbm, keep, sem)
    copy.start()
    zl = me[3]
    theirs = partial(got[zl], weights_got), partial(got[1 - zl], weights_got)
    copy.wait()
    out_0[...] = partial(keep[zl], weights) + theirs[0]
    out_1[...] = (partial(keep[1 - zl], weights) + theirs[1]).astype(BF16)


def last_kernel(
    mine, a, b, c, counts, bias_one, self_two, neigh_two, bias_two, out_weight, out_bias, out
):
    pre = mine[...] + a[...].astype(F32) + b[...].astype(F32) + c[...].astype(F32)
    hidden = jnp.maximum(pre + bias_one[...], 0.0).astype(BF16)
    seeds = counts.shape[1]
    same = iota((seeds, seeds), 0) == iota((seeds, seeds), 1)
    count = jnp.sum(jnp.where(same, counts[...].astype(F32), 0.0), axis=1, keepdims=True)
    count = count.astype(I32)
    earlier = (iota((seeds, seeds), 0) > iota((seeds, seeds), 1)).astype(BF16)
    needs = jnp.broadcast_to((count + 1).astype(F32), (seeds, LANES)).astype(BF16)
    offset = jnp.dot(earlier, needs, preferred_element_type=F32)[:, 0:1].astype(I32)
    place = iota((seeds, CAP), 1) - offset
    is_self = (place == 0).astype(F32).astype(BF16)
    is_near = ((place >= 1) & (place <= count)).astype(F32).astype(BF16)
    own = jnp.dot(is_self, hidden, preferred_element_type=F32).astype(BF16)
    total = jnp.dot(is_near, hidden, preferred_element_type=F32)
    mean = (total / count.astype(F32)).astype(BF16)
    pre_two = (
        jnp.dot(own, self_two[...], preferred_element_type=F32)
        + jnp.dot(mean, neigh_two[...], preferred_element_type=F32)
        + bias_two[...]
    )
    hidden_two = jnp.maximum(pre_two, 0.0).astype(BF16)
    logits = lax.dot_general(
        hidden_two, out_weight[...], (((1,), (1,)), ((), ())), preferred_element_type=F32
    )
    out[...] = logits + out_bias[...]


def params(limit):
    return pltpu.CompilerParams(vmem_limit_bytes=limit * MIB)


def shape(dims, dtype):
    return jax.ShapeDtypeStruct(dims, dtype)


def order_call(per_seed, me, own, got, self_ids, neighbour_ids, count_one):
    owners = sum(x.shape[0] for x in (own, *got))
    lists, most = pl.pallas_call(
        functools.partial(order_kernel, per_seed),
        out_shape=(shape((2, neighbour_ids.shape[0] + 3, 16, LANES), I32), shape((1,), I32)),
        in_specs=[SMEM] + [VMEM] * 8,
        out_specs=(VMEM, SMEM),
        scratch_shapes=[pltpu.VMEM((owners, own.shape[1]), I32)],
        compiler_params=params(10),
        name="order",
    )(me, own, *got, self_ids, neighbour_ids, count_one)
    return lists.reshape(-1), most[0]


def list_scratch(fanout):
    return (
        [pltpu.SMEM((POSITIONS,), I32) for _ in range(fanout + 2)]
        + [pltpu.SMEM((LANES,), I32)]
        + [pltpu.VMEM((4 * CAP + 8, LANES), F32) for _ in range(2)]
        + [pltpu.SemaphoreType.DMA((fanout + 3,))]
    )


def own_call(which, halves, me, features, *table):
    width, length = features.shape
    parts = 8 // halves
    return pl.pallas_call(
        functools.partial(own_kernel, which, halves),
        out_shape=shape((2 * length, LANES), F32),
        in_specs=[SMEM, HBM] + [VMEM] * len(table),
        out_specs=VMEM,
        scratch_shapes=[
            pltpu.VMEM((parts, width, length // 8), BF16),
            pltpu.SemaphoreType.DMA((parts,)),
        ],
        input_output_aliases={2: 0} if table else {},
        compiler_params=params(FIRST_MIB if table else OWN_MIB),
        name="own_rows",
    )(me, features, *table)


def join_call(*parts):
    rows = sum(part.shape[0] for part in parts)
    return pl.pallas_call(
        join_kernel,
        out_shape=shape((rows, parts[0].shape[1]), parts[0].dtype),
        in_specs=[VMEM] * len(parts),
        out_specs=VMEM,
        compiler_params=params(1),
        name="join",
    )(*parts)


def first_call(fanout, me, lists, table, other):
    width, length = other.shape
    dims = (2, CAP, 2 * LANES)
    return pl.pallas_call(
        functools.partial(first_kernel, fanout),
        out_shape=(shape((2 * length, LANES), F32), pltpu.HBM(dims, BF16), pltpu.HBM(dims, BF16)),
        in_specs=[SMEM, ANY, VMEM, HBM],
        out_specs=(VMEM, HBM, HBM),
        scratch_shapes=list_scratch(fanout)
        + [
            pltpu.VMEM((8, width, length // 8), BF16),
            pltpu.SemaphoreType.DMA((8,)),
            pltpu.VMEM(dims, BF16),
            pltpu.VMEM(dims, BF16),
            pltpu.SemaphoreType.DMA((2,)),
        ],
        input_output_aliases={2: 0},
        compiler_params=params(FIRST_MIB),
        name="first_half",
    )(me, lists, table, other)


def second_call(fanout, width, me, lists, table):
    dims = (2, CAP, 2 * LANES)
    halves = pltpu.HBM(dims, BF16)
    return pl.pallas_call(
        functools.partial(second_kernel, fanout, width),
        out_shape=(halves, halves),
        in_specs=[SMEM, ANY, VMEM],
        out_specs=(HBM, HBM),
        scratch_shapes=list_scratch(fanout)
        + [pltpu.VMEM(dims, BF16) for _ in range(2)]
        + [pltpu.SemaphoreType.DMA((2,))],
        compiler_params=params(10),
        name="second_half",
    )(me, lists, table)


def far_call(me, keep, got, weights, weights_got):
    part = shape((CAP, weights.shape[1]), BF16)
    return pl.pallas_call(
        far_kernel,
        out_shape=(part, part),
        in_specs=[SMEM] + [VMEM] * 4,
        out_specs=(VMEM, VMEM),
        compiler_params=params(10),
        name="project_far",
    )(me, keep, got, weights, weights_got)


def near_call(me, keep, got, weights, weights_got):
    dims = (CAP, weights.shape[1])
    return pl.pallas_call(
        near_kernel,
        out_shape=(shape(dims, F32), shape(dims, BF16)),
        in_specs=[SMEM, HBM] + [VMEM] * 3,
        out_specs=(VMEM, VMEM),
        scratch_shapes=[pltpu.VMEM(keep.shape, BF16), pltpu.SemaphoreType.DMA],
        compiler_params=params(10),
        name="project_near",
    )(me, pltpu.with_memory_space_constraint(keep, pltpu.HBM), got, weights, weights_got)


def last_call(*args):
    seeds = args[4].shape[1]
    classes = args[-1].shape[1]
    return pl.pallas_call(
        last_kernel,
        out_shape=shape((seeds, classes), F32),
        in_specs=[VMEM] * len(args),
        out_specs=VMEM,
        compiler_params=params(10),
        name="layer_two",
    )(*args)


def main(
    features,
    self_ids,
    neighbour_ids,
    count_one,
    count_two,
    self_one,
    neigh_one,
    bias_one,
    self_two,
    neigh_two,
    bias_two,
    out_weight,
    out_bias,
):
    owners = lax.axis_size("col")
    seeds = count_two.shape[0]
    per_owner = self_ids.shape[0] // owners
    per_seed = per_owner // seeds
    fanout = neighbour_ids.shape[0]
    width = features.shape[0]
    col = lax.axis_index("col")
    rep = lax.axis_index("rep")
    z = col // 2
    me = jnp.stack([col % 2, 1 - z // 2, rep, z % 2, col]).astype(I32)

    def across(value, bit):
        return lax.ppermute(value, "col", [(i, i ^ bit) for i in range(owners)])

    other = lax.ppermute(features, "rep", [(0, 1), (1, 0)])
    held = pltpu.with_memory_space_constraint(features, pltpu.HBM)
    own = count_two[None, :]
    got_1 = across(own, 1)
    weights = join_call(self_one, neigh_one)
    table, got_1, weights = lax.optimization_barrier(
        (own_call(0, 2, me, held), got_1, weights)
    )
    pair = join_call(own, got_1)
    got = tuple(across(pair, bit) for bit in (4, 6, 2))
    weights_got = across(weights, 1)
    table, got, weights_got = lax.optimization_barrier(
        (own_call(1, 2, me, held, table), got, weights_got)
    )
    got = (got_1, got[2], got[0], got[1])
    lists, most = order_call(per_seed, me, own, got, self_ids, neighbour_ids, count_one)
    table, keep_far, send_far = first_call(fanout, me, lists, table, other)
    got_far = across(send_far, 1)
    keep_near, send_near = second_call(fanout, width, me, lists, table)
    far = far_call(me, keep_far, got_far, weights, weights_got)
    far, send_near = lax.optimization_barrier((far, send_near))
    far_got = [across(far[0], 4), across(far[1], 6)]
    got_near = across(send_near, 1)
    near = near_call(me, keep_near, got_near, weights, weights_got)
    far_got.append(across(near[1], 2))
    fast = last_call(
        near[0],
        *far_got,
        own,
        bias_one[None, :],
        self_two,
        neigh_two,
        bias_two[None, :],
        out_weight.T,
        out_bias[None, :],
    )
    return lax.cond(
        most > CAP,
        lambda: general(
            other,
            features,
            self_ids,
            neighbour_ids,
            count_one,
            count_two,
            self_one,
            neigh_one,
            bias_one,
            self_two,
            neigh_two,
            bias_two,
            out_weight,
            out_bias,
        ),
        lambda: fast,
    )


def local(*args):
    features, self_ids, neighbour_ids = args[0], args[1], args[2]
    sizes = (lax.axis_size("groups"), lax.axis_size("col"), lax.axis_size("rep"))
    small = (
        sizes == (2, 8, 2)
        and features.shape[0] <= LANES
        and features.shape[1] <= 32768
        and self_ids.shape[0] * (neighbour_ids.shape[0] + 1) <= 2**17
        and neighbour_ids.shape[0] <= 15
    )
    if small:
        return main(*args)
    return general(lax.ppermute(features, "rep", [(0, 1), (1, 0)]), *args)


def solution(mesh):
    placed = (
        P("col", ("groups", "rep")),
        P(("groups", "rep")),
        P(None, ("groups", "rep")),
        P(("groups", "rep")),
        P(("groups", "col", "rep")),
        P("col", None),
        P("col", None),
        P(),
        P(),
        P(),
        P(),
        P(),
        P(),
    )
    return jax.shard_map(
        local,
        mesh=mesh,
        in_specs=placed,
        out_specs=P(("groups", "col", "rep"), None),
        check_vma=False,
    )
```

```python
import functools

import jax
import jax.numpy as jnp
import numpy as np
from jax import lax
from jax.experimental import pallas as pl
from jax.experimental.pallas import tpu as pltpu
from jax.sharding import PartitionSpec as P

CAP = 272
UNROLL = 8
POSITIONS = 10 * 128
FIRST_MIB = 12
OWN_MIB = 18
LANES = 128
MIB = 2**20
BF16 = jnp.bfloat16
F32 = jnp.float32
I32 = jnp.int32


def gathered(value, axis):
    copies = jnp.broadcast_to(value[None], (lax.axis_size(axis),) + value.shape)
    pieces = lax.all_to_all(copies, axis, split_axis=0, concat_axis=0, tiled=True)
    return pieces.reshape((-1,) + value.shape[1:])


def general(
    other,
    features,
    self_ids,
    neighbour_ids,
    count_one,
    count_two,
    self_one,
    neigh_one,
    bias_one,
    self_two,
    neigh_two,
    bias_two,
    out_weight,
    out_bias,
):
    mine = jnp.where(lax.axis_index("rep") == 0, 0, 1)
    table_cols = jnp.where(
        mine == 0,
        jnp.concatenate([features, other], axis=1),
        jnp.concatenate([other, features], axis=1),
    )
    table_rows = table_cols.T
    blocks = lax.axis_size("col")
    total_rows = self_ids.shape[0]
    per_owner = total_rows // blocks
    fanout = neighbour_ids.shape[0]
    width = table_rows.shape[1]
    all_ids = jnp.concatenate([self_ids[None, :], neighbour_ids], axis=0)
    fetched = jnp.take(table_rows, all_ids, axis=0)
    self_x = fetched[0]
    mask = (jnp.arange(fanout)[:, None] < count_one[None, :]).astype(BF16)
    summed = jnp.einsum("kmc,km->mc", fetched[1:], mask, preferred_element_type=F32)
    mean_one = (summed / count_one[:, None].astype(F32)).astype(BF16)
    full_self, full_neigh = gathered(self_one, "col"), gathered(neigh_one, "col")
    stacked = jnp.stack([self_x, mean_one], axis=0).reshape(2, blocks, per_owner, width)
    pieces = lax.all_to_all(stacked, "col", split_axis=1, concat_axis=3, tiled=True)
    pre_one = jnp.dot(pieces[0, 0], full_self, preferred_element_type=F32) + jnp.dot(
        pieces[1, 0], full_neigh, preferred_element_type=F32
    )
    hidden_one = jax.nn.relu(pre_one + bias_one).astype(BF16)
    seeds = count_two.shape[0]
    hidden = hidden_one.shape[1]
    grouped = hidden_one.reshape(seeds, per_owner // seeds, hidden)
    mask_two = (jnp.arange(grouped.shape[1] - 1)[None, :] < count_two[:, None]).astype(BF16)
    summed_two = jnp.einsum("skh,sk->sh", grouped[:, 1:, :], mask_two, preferred_element_type=F32)
    mean_two = (summed_two / count_two[:, None].astype(F32)).astype(BF16)
    pre_two = jnp.dot(grouped[:, 0, :], self_two, preferred_element_type=F32) + jnp.dot(
        mean_two, neigh_two, preferred_element_type=F32
    )
    hidden_two = jax.nn.relu(pre_two + bias_two).astype(BF16)
    return jnp.dot(hidden_two, out_weight, preferred_element_type=F32) + out_bias


def iota(shape, dim):
    return lax.broadcasted_iota(I32, shape, dim)


def tree_sum(terms):
    while len(terms) > 1:
        odd = [terms[-1]] if len(terms) % 2 else []
        terms = [a + b for a, b in zip(terms[::2], terms[1::2])] + odd
    return terms[0]


VMEM = pl.BlockSpec(memory_space=pltpu.VMEM)
SMEM = pl.BlockSpec(memory_space=pltpu.SMEM)
HBM = pl.BlockSpec(memory_space=pltpu.HBM)
ANY = pl.BlockSpec(memory_space=pl.ANY)


def start_all(copies):
    for copy in copies:
        copy.start()


def turn(source, table, base):
    width, length = source.shape
    step = 512
    unroll = 8

    def body(i, carry):
        for u in range(unroll):
            off = pl.multiple_of((i * unroll + u) * step, step)
            rows = source[:, pl.ds(off, step)].T.astype(F32)
            table[pl.ds(pl.multiple_of(base + off, step), step), 0:width] = rows
        return carry

    lax.fori_loop(0, length // step // unroll, body, 0)


def order_kernel(
    per_seed, me, own, got_1, got_2, got_4, got_6, self_ids, neighbour_ids, count_one, lists, most, counts_rel
):
    owners, seeds = counts_rel.shape
    fanout = neighbour_ids.shape[0]
    per_owner = count_one.shape[0] // owners
    half = owners // 2
    mine = me[4]
    counts_rel[0:1, :] = own[...]
    counts_rel[1:2, :] = got_1[...]
    counts_rel[2:4, :] = got_2[...]
    counts_rel[4:6, :] = got_4[...]
    counts_rel[6:8, :] = got_6[...]
    own_ids = self_ids[...].reshape(1, owners * per_owner)
    ones = count_one[...].reshape(1, owners * per_owner)
    counts = jnp.concatenate(
        [counts_rel[pl.ds(jnp.bitwise_xor(mine, c), 1), :] for c in range(owners)], axis=0
    ).astype(F32)
    needs = (counts + 1.0).astype(BF16)
    most[0] = jnp.max(jnp.sum(counts + 1.0, axis=1, keepdims=True)).astype(I32)
    column = iota((seeds, per_owner), 1).astype(F32)
    seed_of = jnp.floor((column + 0.5) * (1.0 / per_seed))
    seed = iota((seeds, per_owner), 0).astype(F32)
    t = column[0:1, :] - seed_of[0:1, :] * per_seed
    of_row = jnp.dot(
        counts.astype(BF16), (seed == seed_of).astype(BF16), preferred_element_type=F32
    )
    slot = t + jnp.dot(needs, (seed < seed_of).astype(BF16), preferred_element_type=F32)
    used = (t <= of_row) & (slot < CAP)
    slot = slot.astype(I32)
    keys = [
        jnp.where(used[c : c + 1, :], ones[:, c * per_owner : (c + 1) * per_owner], 0)
        for c in range(owners)
    ]
    kinds = [
        iota((16, per_owner), 0) == jnp.broadcast_to(key, (16, per_owner)) for key in keys
    ]
    stacked = jnp.concatenate([k.astype(F32).astype(BF16) for k in kinds], axis=0)
    left = (iota((per_owner, per_owner), 0) < iota((per_owner, per_owner), 1)).astype(BF16)
    prefix = jnp.dot(stacked, left, preferred_element_type=F32)
    total = jnp.dot(stacked, jnp.ones((per_owner, LANES), BF16), preferred_element_type=F32)
    for h in range(2):
        carry = jnp.zeros((16, LANES), F32)
        carries = []
        for c in range(h * half, (h + 1) * half):
            carries.append(carry)
            carry = carry + total[c * 16 : (c + 1) * 16, :]
        sizes = jnp.floor((carry + (UNROLL - 1)) * (1.0 / UNROLL)) * UNROLL
        bases = [jnp.zeros((1, LANES), F32)]
        for v in range(1, 16):
            bases.append(bases[-1] + sizes[v : v + 1, :])
        first = jnp.concatenate([bases[0]] + bases[:15], axis=0)
        sums = jnp.zeros((2 * (fanout + 2) * 16, LANES), F32)
        for i, c in enumerate(range(h * half, (h + 1) * half)):
            begin = (first + carries[i])[:, 0:1]
            spot = jnp.where(kinds[c], prefix[c * 16 : (c + 1) * 16, :] + begin, 0.0)
            spot = jnp.sum(spot, axis=0, keepdims=True).astype(I32)
            spot = jnp.where(keys[c] > 0, spot, -1)
            spot_lo = jnp.bitwise_and(spot, LANES - 1)
            spot_hi = jnp.right_shift(spot, 7)
            lane = (iota((LANES, per_owner), 0) == spot_lo).astype(F32).astype(BF16)
            at_hi = (iota((16, per_owner), 0) == spot_hi).astype(F32)
            columns = slice(c * per_owner, (c + 1) * per_owner)
            rows = [own_ids[:, columns]]
            rows += [neighbour_ids[k : k + 1, columns] for k in range(fanout)]
            rows += [half * CAP - (slot[c : c + 1, :] + i * CAP)]
            parts = []
            for row in rows:
                for byte in (jnp.right_shift(row, 8), jnp.bitwise_and(row, 255)):
                    value = jnp.broadcast_to(byte.astype(F32), (16, per_owner))
                    parts.append((at_hi * value).astype(BF16))
            sums = sums + lax.dot_general(
                jnp.concatenate(parts, axis=0),
                lane,
                (((1,), (1,)), ((), ())),
                preferred_element_type=F32,
            )
        for k in range(fanout + 2):
            hi = sums[32 * k : 32 * k + 16, :]
            lo = sums[32 * k + 16 : 32 * k + 32, :]
            value = (hi * 256.0 + lo).astype(I32)
            lists[h, k, :, :] = value if k <= fanout else half * CAP - value
        lane = iota((8, LANES), 1)
        begins = jnp.zeros((8, LANES), F32)
        for v in range(16):
            begins = begins + jnp.where(lane == v, bases[v], 0.0)
        lists[h, fanout + 2, 0:8, :] = begins.astype(I32)
        lists[h, fanout + 2, 8:16, :] = jnp.zeros((8, LANES), I32)


def list_copies(fanout, h, lists, ids, places, begins, sems):
    block = 16 * LANES

    def piece(k, length):
        at = pl.multiple_of((h * (fanout + 3) + k) * block, block)
        return lists.at[pl.ds(at, length)]

    last = fanout + 2
    copies = [
        pltpu.make_async_copy(piece(k, POSITIONS), ref, sems.at[k])
        for k, ref in enumerate(list(ids) + [places])
    ]
    copies.append(pltpu.make_async_copy(piece(last, LANES), begins, sems.at[last]))
    start_all(copies[fanout + 1 :] + copies[: fanout + 1])
    return copies


def look_up(fanout, copies, table, ids, places, begins, self_rows, mean_rows):
    for copy in [copies[0]] + copies[fanout + 1 :]:
        copy.wait()
    for v in range(1, fanout + 1):
        copies[v].wait()
        begin = begins[v - 1]
        end = begins[v]

        def body(i, carry, v=v, begin=begin):
            for u in range(UNROLL):
                at = begin + i * UNROLL + u
                to = places[at]
                self_rows[pl.ds(to, 1), :] = table[pl.ds(ids[0][at], 1), :]
                total = tree_sum([table[pl.ds(ids[k][at], 1), :] for k in range(1, v + 1)])
                mean_rows[pl.ds(to, 1), :] = total * (1.0 / v)
            return carry

        lax.fori_loop(0, jnp.right_shift(end - begin, UNROLL.bit_length() - 1), body, 0)


def block_of(z, side, width, self_rows, mean_rows):
    valid = iota((CAP, LANES), 1) < width
    at = pl.multiple_of((z * 2 + side) * CAP, CAP)
    parts = [jnp.where(valid, rows[pl.ds(at, CAP), :], 0.0) for rows in (self_rows, mean_rows)]
    return jnp.concatenate(parts, axis=1).astype(BF16)


def stage(source, staged, sems):
    blocks, _, part = staged.shape
    copies = [
        pltpu.make_async_copy(source.at[:, pl.ds(b * part, part)], staged.at[b], sems.at[b])
        for b in range(blocks)
    ]
    start_all(copies)
    return copies


def turn_staged(copies, staged, table, base):
    part = staged.shape[2]
    for b, copy in enumerate(copies):
        copy.wait()
        turn(staged.at[b], table, pl.multiple_of(base + b * part, part))


def own_kernel(which, halves, me, features, *refs):
    table, staged, sems = refs[-3:]
    length = features.shape[1]
    half = length // halves
    copies = stage(features.at[:, pl.ds(which * half, half)], staged, sems)
    turn_staged(copies, staged, table, me[2] * length + which * half)


def join_kernel(*refs):
    *parts, out = refs
    at = 0
    for part in parts:
        out[at : at + part.shape[0], :] = part[...]
        at += part.shape[0]


def hand_out(blocks, sems):
    copies = []
    for i, (make, scratch, out) in enumerate(blocks):
        scratch[...] = make()
        copies.append(pltpu.make_async_copy(scratch, out, sems.at[i]))
        copies[-1].start()
    for copy in copies:
        copy.wait()


def first_kernel(
    fanout, me, lists, table_in, other, table, keep_hbm, send_hbm, *scratch
):
    del table_in
    ids = scratch[: fanout + 1]
    places, begins, self_rows, mean_rows, sems = scratch[fanout + 1 : fanout + 6]
    staged, staged_sems, keep, send, out_sems = scratch[fanout + 6 :]
    width, length = other.shape
    x, h, rep = me[0], me[1], me[2]
    staging = stage(other, staged, staged_sems)
    copies = list_copies(fanout, h, lists, ids, places, begins, sems)
    self_rows[...] = jnp.zeros_like(self_rows)
    mean_rows[...] = jnp.zeros_like(mean_rows)
    turn_staged(staging, staged, table, (1 - rep) * length)
    look_up(fanout, copies, table, ids, places, begins, self_rows, mean_rows)
    hand_out(
        [
            (
                functools.partial(block_of, z, side, width, self_rows, mean_rows),
                held.at[z],
                out.at[z],
            )
            for held, out, side in ((send, send_hbm, 1 - x), (keep, keep_hbm, x))
            for z in range(2)
        ],
        out_sems,
    )


def second_kernel(fanout, width, me, lists, table, *refs):
    outs, scratch = refs[:4], refs[4:]
    ids = scratch[: fanout + 1]
    places, begins, self_rows, mean_rows, sems = scratch[fanout + 1 : fanout + 6]
    *held, out_sems = scratch[fanout + 6 :]
    x, h, zl = me[0], 1 - me[1], me[3]
    copies = list_copies(fanout, h, lists, ids, places, begins, sems)
    self_rows[...] = jnp.zeros_like(self_rows)
    mean_rows[...] = jnp.zeros_like(mean_rows)
    look_up(fanout, copies, table, ids, places, begins, self_rows, mean_rows)
    sides = ((1 - zl, 1 - x), (zl, 1 - x), (1 - zl, x), (zl, x))
    hand_out(
        [
            (functools.partial(block_of, z, side, width, self_rows, mean_rows), one, out)
            for (z, side), one, out in zip(sides, held, outs)
        ],
        out_sems,
    )


def partial(rows, weights):
    width = weights.shape[0] // 2
    return jnp.dot(rows[:, 0:width], weights[0:width, :], preferred_element_type=F32) + jnp.dot(
        rows[:, LANES : LANES + width], weights[width:, :], preferred_element_type=F32
    )


def far_kernel(me, keep, got, weights, weights_got, out_0, out_1):
    zl = me[3]
    for which, out in ((zl, out_0), (1 - zl, out_1)):
        total = partial(keep[which], weights) + partial(got[which], weights_got)
        out[...] = total.astype(BF16)


def near_kernel(keep_hbm, got, weights, weights_got, out, keep, sem):
    copy = pltpu.make_async_copy(keep_hbm, keep, sem)
    copy.start()
    theirs = partial(got, weights_got)
    copy.wait()
    out[...] = (partial(keep, weights) + theirs).astype(out.dtype)


def last_kernel(
    mine, a, b, c, counts, bias_one, self_two, neigh_two, bias_two, out_weight, out_bias, out
):
    pre = mine[...] + a[...].astype(F32) + b[...].astype(F32) + c[...].astype(F32)
    hidden = jnp.maximum(pre + bias_one[...], 0.0).astype(BF16)
    seeds = counts.shape[1]
    same = iota((seeds, seeds), 0) == iota((seeds, seeds), 1)
    count = jnp.sum(jnp.where(same, counts[...].astype(F32), 0.0), axis=1, keepdims=True)
    count = count.astype(I32)
    earlier = (iota((seeds, seeds), 0) > iota((seeds, seeds), 1)).astype(BF16)
    needs = jnp.broadcast_to((count + 1).astype(F32), (seeds, LANES)).astype(BF16)
    offset = jnp.dot(earlier, needs, preferred_element_type=F32)[:, 0:1].astype(I32)
    place = iota((seeds, CAP), 1) - offset
    is_self = (place == 0).astype(F32).astype(BF16)
    is_near = ((place >= 1) & (place <= count)).astype(F32).astype(BF16)
    own = jnp.dot(is_self, hidden, preferred_element_type=F32).astype(BF16)
    total = jnp.dot(is_near, hidden, preferred_element_type=F32)
    mean = (total / count.astype(F32)).astype(BF16)
    pre_two = (
        jnp.dot(own, self_two[...], preferred_element_type=F32)
        + jnp.dot(mean, neigh_two[...], preferred_element_type=F32)
        + bias_two[...]
    )
    hidden_two = jnp.maximum(pre_two, 0.0).astype(BF16)
    logits = lax.dot_general(
        hidden_two, out_weight[...], (((1,), (1,)), ((), ())), preferred_element_type=F32
    )
    out[...] = logits + out_bias[...]


def params(limit):
    return pltpu.CompilerParams(vmem_limit_bytes=limit * MIB)


def shape(dims, dtype):
    return jax.ShapeDtypeStruct(dims, dtype)


def order_call(per_seed, me, own, got, self_ids, neighbour_ids, count_one):
    owners = sum(x.shape[0] for x in (own, *got))
    lists, most = pl.pallas_call(
        functools.partial(order_kernel, per_seed),
        out_shape=(shape((2, neighbour_ids.shape[0] + 3, 16, LANES), I32), shape((1,), I32)),
        in_specs=[SMEM] + [VMEM] * 8,
        out_specs=(VMEM, SMEM),
        scratch_shapes=[pltpu.VMEM((owners, own.shape[1]), I32)],
        compiler_params=params(10),
        name="order",
    )(me, own, *got, self_ids, neighbour_ids, count_one)
    return lists.reshape(-1), most[0]


def list_scratch(fanout):
    return (
        [pltpu.SMEM((POSITIONS,), I32) for _ in range(fanout + 2)]
        + [pltpu.SMEM((LANES,), I32)]
        + [pltpu.VMEM((4 * CAP + 8, LANES), F32) for _ in range(2)]
        + [pltpu.SemaphoreType.DMA((fanout + 3,))]
    )


def own_call(which, halves, me, features, *table):
    width, length = features.shape
    parts = 8 // halves
    return pl.pallas_call(
        functools.partial(own_kernel, which, halves),
        out_shape=shape((2 * length, LANES), F32),
        in_specs=[SMEM, HBM] + [VMEM] * len(table),
        out_specs=VMEM,
        scratch_shapes=[
            pltpu.VMEM((parts, width, length // 8), BF16),
            pltpu.SemaphoreType.DMA((parts,)),
        ],
        input_output_aliases={2: 0} if table else {},
        compiler_params=params(FIRST_MIB if table else OWN_MIB),
        name="own_rows",
    )(me, features, *table)


def join_call(*parts):
    rows = sum(part.shape[0] for part in parts)
    return pl.pallas_call(
        join_kernel,
        out_shape=shape((rows, parts[0].shape[1]), parts[0].dtype),
        in_specs=[VMEM] * len(parts),
        out_specs=VMEM,
        compiler_params=params(1),
        name="join",
    )(*parts)


def first_call(fanout, me, lists, table, other):
    width, length = other.shape
    dims = (2, CAP, 2 * LANES)
    return pl.pallas_call(
        functools.partial(first_kernel, fanout),
        out_shape=(shape((2 * length, LANES), F32), pltpu.HBM(dims, BF16), pltpu.HBM(dims, BF16)),
        in_specs=[SMEM, ANY, VMEM, HBM],
        out_specs=(VMEM, HBM, HBM),
        scratch_shapes=list_scratch(fanout)
        + [
            pltpu.VMEM((8, width, length // 8), BF16),
            pltpu.SemaphoreType.DMA((8,)),
            pltpu.VMEM(dims, BF16),
            pltpu.VMEM(dims, BF16),
            pltpu.SemaphoreType.DMA((4,)),
        ],
        input_output_aliases={2: 0},
        compiler_params=params(FIRST_MIB),
        name="first_half",
    )(me, lists, table, other)


def second_call(fanout, width, me, lists, table):
    dims = (CAP, 2 * LANES)
    return pl.pallas_call(
        functools.partial(second_kernel, fanout, width),
        out_shape=(pltpu.HBM(dims, BF16),) * 4,
        in_specs=[SMEM, ANY, VMEM],
        out_specs=(HBM,) * 4,
        scratch_shapes=list_scratch(fanout)
        + [pltpu.VMEM(dims, BF16) for _ in range(4)]
        + [pltpu.SemaphoreType.DMA((4,))],
        compiler_params=params(10),
        name="second_half",
    )(me, lists, table)


def far_call(me, keep, got, weights, weights_got):
    part = shape((CAP, weights.shape[1]), BF16)
    return pl.pallas_call(
        far_kernel,
        out_shape=(part, part),
        in_specs=[SMEM] + [VMEM] * 4,
        out_specs=(VMEM, VMEM),
        compiler_params=params(10),
        name="project_far",
    )(me, keep, got, weights, weights_got)


def near_call(keep, got, weights, weights_got, kind):
    return pl.pallas_call(
        near_kernel,
        out_shape=shape((CAP, weights.shape[1]), kind),
        in_specs=[HBM] + [VMEM] * 3,
        out_specs=VMEM,
        scratch_shapes=[pltpu.VMEM(keep.shape, BF16), pltpu.SemaphoreType.DMA],
        compiler_params=params(10),
        name="project_near",
    )(pltpu.with_memory_space_constraint(keep, pltpu.HBM), got, weights, weights_got)


def last_call(*args):
    seeds = args[4].shape[1]
    classes = args[-1].shape[1]
    return pl.pallas_call(
        last_kernel,
        out_shape=shape((seeds, classes), F32),
        in_specs=[VMEM] * len(args),
        out_specs=VMEM,
        compiler_params=params(10),
        name="layer_two",
    )(*args)


def main(
    features,
    self_ids,
    neighbour_ids,
    count_one,
    count_two,
    self_one,
    neigh_one,
    bias_one,
    self_two,
    neigh_two,
    bias_two,
    out_weight,
    out_bias,
):
    owners = lax.axis_size("col")
    seeds = count_two.shape[0]
    per_owner = self_ids.shape[0] // owners
    per_seed = per_owner // seeds
    fanout = neighbour_ids.shape[0]
    width = features.shape[0]
    col = lax.axis_index("col")
    rep = lax.axis_index("rep")
    z = col // 2
    me = jnp.stack([col % 2, 1 - z // 2, rep, z % 2, col]).astype(I32)

    def across(value, bit):
        return lax.ppermute(value, "col", [(i, i ^ bit) for i in range(owners)])

    other = lax.ppermute(features, "rep", [(0, 1), (1, 0)])
    held = pltpu.with_memory_space_constraint(features, pltpu.HBM)
    own = count_two[None, :]
    got_1 = across(own, 1)
    weights = join_call(self_one, neigh_one)
    table, got_1, weights = lax.optimization_barrier(
        (own_call(0, 2, me, held), got_1, weights)
    )
    pair = join_call(own, got_1)
    got = tuple(across(pair, bit) for bit in (4, 6, 2))
    weights_got = across(weights, 1)
    table, got, weights_got = lax.optimization_barrier(
        (own_call(1, 2, me, held, table), got, weights_got)
    )
    got = (got_1, got[2], got[0], got[1])
    lists, most = order_call(per_seed, me, own, got, self_ids, neighbour_ids, count_one)
    table, keep_far, send_far = first_call(fanout, me, lists, table, other)
    got_far = across(send_far, 1)
    send_on, send_own, keep_on, keep_own = second_call(fanout, width, me, lists, table)
    far = far_call(me, keep_far, got_far, weights, weights_got)
    far, send_on, send_own = lax.optimization_barrier((far, send_on, send_own))
    far_got = [across(far[0], 4), across(far[1], 6)]
    got_on = across(send_on, 1)
    got_own = across(send_own, 1)
    near = near_call(keep_on, got_on, weights, weights_got, BF16)
    far_got.append(across(near, 2))
    mine = near_call(keep_own, got_own, weights, weights_got, F32)
    fast = last_call(
        mine,
        *far_got,
        own,
        bias_one[None, :],
        self_two,
        neigh_two,
        bias_two[None, :],
        out_weight.T,
        out_bias[None, :],
    )
    return lax.cond(
        most > CAP,
        lambda: general(
            other,
            features,
            self_ids,
            neighbour_ids,
            count_one,
            count_two,
            self_one,
            neigh_one,
            bias_one,
            self_two,
            neigh_two,
            bias_two,
            out_weight,
            out_bias,
        ),
        lambda: fast,
    )


def local(*args):
    features, self_ids, neighbour_ids = args[0], args[1], args[2]
    sizes = (lax.axis_size("groups"), lax.axis_size("col"), lax.axis_size("rep"))
    small = (
        sizes == (2, 8, 2)
        and features.shape[0] <= LANES
        and features.shape[1] <= 32768
        and self_ids.shape[0] * (neighbour_ids.shape[0] + 1) <= 2**17
        and neighbour_ids.shape[0] <= 15
    )
    if small:
        return main(*args)
    return general(lax.ppermute(features, "rep", [(0, 1), (1, 0)]), *args)


def solution(mesh):
    placed = (
        P("col", ("groups", "rep")),
        P(("groups", "rep")),
        P(None, ("groups", "rep")),
        P(("groups", "rep")),
        P(("groups", "col", "rep")),
        P("col", None),
        P("col", None),
        P(),
        P(),
        P(),
        P(),
        P(),
        P(),
    )
    return jax.shard_map(
        local,
        mesh=mesh,
        in_specs=placed,
        out_specs=P(("groups", "col", "rep"), None),
        check_vma=False,
    )
```

```python
import functools

import jax
import jax.numpy as jnp
import numpy as np
from jax import lax
from jax.experimental import pallas as pl
from jax.experimental.pallas import tpu as pltpu
from jax.sharding import PartitionSpec as P

CAP = 272
UNROLL = 8
POSITIONS = 10 * 128
FIRST_MIB = 12
OWN_MIB = 18
LANES = 128
MIB = 2**20
BF16 = jnp.bfloat16
F32 = jnp.float32
I32 = jnp.int32


def gathered(value, axis):
    copies = jnp.broadcast_to(value[None], (lax.axis_size(axis),) + value.shape)
    pieces = lax.all_to_all(copies, axis, split_axis=0, concat_axis=0, tiled=True)
    return pieces.reshape((-1,) + value.shape[1:])


def general(
    other,
    features,
    self_ids,
    neighbour_ids,
    count_one,
    count_two,
    self_one,
    neigh_one,
    bias_one,
    self_two,
    neigh_two,
    bias_two,
    out_weight,
    out_bias,
):
    mine = jnp.where(lax.axis_index("rep") == 0, 0, 1)
    table_cols = jnp.where(
        mine == 0,
        jnp.concatenate([features, other], axis=1),
        jnp.concatenate([other, features], axis=1),
    )
    table_rows = table_cols.T
    blocks = lax.axis_size("col")
    total_rows = self_ids.shape[0]
    per_owner = total_rows // blocks
    fanout = neighbour_ids.shape[0]
    width = table_rows.shape[1]
    all_ids = jnp.concatenate([self_ids[None, :], neighbour_ids], axis=0)
    fetched = jnp.take(table_rows, all_ids, axis=0)
    self_x = fetched[0]
    mask = (jnp.arange(fanout)[:, None] < count_one[None, :]).astype(BF16)
    summed = jnp.einsum("kmc,km->mc", fetched[1:], mask, preferred_element_type=F32)
    mean_one = (summed / count_one[:, None].astype(F32)).astype(BF16)
    full_self, full_neigh = gathered(self_one, "col"), gathered(neigh_one, "col")
    stacked = jnp.stack([self_x, mean_one], axis=0).reshape(2, blocks, per_owner, width)
    pieces = lax.all_to_all(stacked, "col", split_axis=1, concat_axis=3, tiled=True)
    pre_one = jnp.dot(pieces[0, 0], full_self, preferred_element_type=F32) + jnp.dot(
        pieces[1, 0], full_neigh, preferred_element_type=F32
    )
    hidden_one = jax.nn.relu(pre_one + bias_one).astype(BF16)
    seeds = count_two.shape[0]
    hidden = hidden_one.shape[1]
    grouped = hidden_one.reshape(seeds, per_owner // seeds, hidden)
    mask_two = (jnp.arange(grouped.shape[1] - 1)[None, :] < count_two[:, None]).astype(BF16)
    summed_two = jnp.einsum("skh,sk->sh", grouped[:, 1:, :], mask_two, preferred_element_type=F32)
    mean_two = (summed_two / count_two[:, None].astype(F32)).astype(BF16)
    pre_two = jnp.dot(grouped[:, 0, :], self_two, preferred_element_type=F32) + jnp.dot(
        mean_two, neigh_two, preferred_element_type=F32
    )
    hidden_two = jax.nn.relu(pre_two + bias_two).astype(BF16)
    return jnp.dot(hidden_two, out_weight, preferred_element_type=F32) + out_bias


def iota(shape, dim):
    return lax.broadcasted_iota(I32, shape, dim)


def tree_sum(terms):
    while len(terms) > 1:
        odd = [terms[-1]] if len(terms) % 2 else []
        terms = [a + b for a, b in zip(terms[::2], terms[1::2])] + odd
    return terms[0]


VMEM = pl.BlockSpec(memory_space=pltpu.VMEM)
SMEM = pl.BlockSpec(memory_space=pltpu.SMEM)
HBM = pl.BlockSpec(memory_space=pltpu.HBM)
ANY = pl.BlockSpec(memory_space=pl.ANY)


def start_all(copies):
    for copy in copies:
        copy.start()


def turn(source, table, base):
    width, length = source.shape
    step = 512
    unroll = 8

    def body(i, carry):
        for u in range(unroll):
            off = pl.multiple_of((i * unroll + u) * step, step)
            rows = source[:, pl.ds(off, step)].T.astype(F32)
            table[pl.ds(pl.multiple_of(base + off, step), step), 0:width] = rows
        return carry

    lax.fori_loop(0, length // step // unroll, body, 0)


def order_kernel(
    per_seed, me, own, got_1, got_2, got_4, got_6, self_ids, neighbour_ids, count_one, lists, most, counts_rel
):
    owners, seeds = counts_rel.shape
    fanout = neighbour_ids.shape[0]
    per_owner = count_one.shape[0] // owners
    half = owners // 2
    mine = me[4]
    counts_rel[0:1, :] = own[...]
    counts_rel[1:2, :] = got_1[...]
    counts_rel[2:4, :] = got_2[...]
    counts_rel[4:6, :] = got_4[...]
    counts_rel[6:8, :] = got_6[...]
    own_ids = self_ids[...].reshape(1, owners * per_owner)
    ones = count_one[...].reshape(1, owners * per_owner)
    counts = jnp.concatenate(
        [counts_rel[pl.ds(jnp.bitwise_xor(mine, c), 1), :] for c in range(owners)], axis=0
    ).astype(F32)
    needs = (counts + 1.0).astype(BF16)
    most[0] = jnp.max(jnp.sum(counts + 1.0, axis=1, keepdims=True)).astype(I32)
    column = iota((seeds, per_owner), 1).astype(F32)
    seed_of = jnp.floor((column + 0.5) * (1.0 / per_seed))
    seed = iota((seeds, per_owner), 0).astype(F32)
    t = column[0:1, :] - seed_of[0:1, :] * per_seed
    of_row = jnp.dot(
        counts.astype(BF16), (seed == seed_of).astype(BF16), preferred_element_type=F32
    )
    slot = t + jnp.dot(needs, (seed < seed_of).astype(BF16), preferred_element_type=F32)
    used = (t <= of_row) & (slot < CAP)
    slot = slot.astype(I32)
    keys = [
        jnp.where(used[c : c + 1, :], ones[:, c * per_owner : (c + 1) * per_owner], 0)
        for c in range(owners)
    ]
    kinds = [
        iota((16, per_owner), 0) == jnp.broadcast_to(key, (16, per_owner)) for key in keys
    ]
    stacked = jnp.concatenate([k.astype(F32).astype(BF16) for k in kinds], axis=0)
    left = (iota((per_owner, per_owner), 0) < iota((per_owner, per_owner), 1)).astype(BF16)
    prefix = jnp.dot(stacked, left, preferred_element_type=F32)
    total = jnp.dot(stacked, jnp.ones((per_owner, LANES), BF16), preferred_element_type=F32)
    for h in range(2):
        carry = jnp.zeros((16, LANES), F32)
        carries = []
        for c in range(h * half, (h + 1) * half):
            carries.append(carry)
            carry = carry + total[c * 16 : (c + 1) * 16, :]
        sizes = jnp.floor((carry + (UNROLL - 1)) * (1.0 / UNROLL)) * UNROLL
        bases = [jnp.zeros((1, LANES), F32)]
        for v in range(1, 16):
            bases.append(bases[-1] + sizes[v : v + 1, :])
        first = jnp.concatenate([bases[0]] + bases[:15], axis=0)
        sums = jnp.zeros((2 * (fanout + 2) * 16, LANES), F32)
        for i, c in enumerate(range(h * half, (h + 1) * half)):
            begin = (first + carries[i])[:, 0:1]
            spot = jnp.where(kinds[c], prefix[c * 16 : (c + 1) * 16, :] + begin, 0.0)
            spot = jnp.sum(spot, axis=0, keepdims=True).astype(I32)
            spot = jnp.where(keys[c] > 0, spot, -1)
            spot_lo = jnp.bitwise_and(spot, LANES - 1)
            spot_hi = jnp.right_shift(spot, 7)
            lane = (iota((LANES, per_owner), 0) == spot_lo).astype(F32).astype(BF16)
            at_hi = (iota((16, per_owner), 0) == spot_hi).astype(F32)
            columns = slice(c * per_owner, (c + 1) * per_owner)
            rows = [own_ids[:, columns]]
            rows += [neighbour_ids[k : k + 1, columns] for k in range(fanout)]
            rows += [half * CAP - (slot[c : c + 1, :] + i * CAP)]
            parts = []
            for row in rows:
                for byte in (jnp.right_shift(row, 8), jnp.bitwise_and(row, 255)):
                    value = jnp.broadcast_to(byte.astype(F32), (16, per_owner))
                    parts.append((at_hi * value).astype(BF16))
            sums = sums + lax.dot_general(
                jnp.concatenate(parts, axis=0),
                lane,
                (((1,), (1,)), ((), ())),
                preferred_element_type=F32,
            )
        for k in range(fanout + 2):
            hi = sums[32 * k : 32 * k + 16, :]
            lo = sums[32 * k + 16 : 32 * k + 32, :]
            value = (hi * 256.0 + lo).astype(I32)
            lists[h, k, :, :] = value if k <= fanout else half * CAP - value
        lane = iota((8, LANES), 1)
        begins = jnp.zeros((8, LANES), F32)
        for v in range(16):
            begins = begins + jnp.where(lane == v, bases[v], 0.0)
        lists[h, fanout + 2, 0:8, :] = begins.astype(I32)
        lists[h, fanout + 2, 8:16, :] = jnp.zeros((8, LANES), I32)


def list_copies(fanout, h, lists, ids, places, begins, sems):
    block = 16 * LANES

    def piece(k, length):
        at = pl.multiple_of((h * (fanout + 3) + k) * block, block)
        return lists.at[pl.ds(at, length)]

    last = fanout + 2
    copies = [
        pltpu.make_async_copy(piece(k, POSITIONS), ref, sems.at[k])
        for k, ref in enumerate(list(ids) + [places])
    ]
    copies.append(pltpu.make_async_copy(piece(last, LANES), begins, sems.at[last]))
    start_all(copies[fanout + 1 :] + copies[: fanout + 1])
    return copies


def look_up(fanout, copies, table, ids, places, begins, self_rows, mean_rows):
    for copy in [copies[0]] + copies[fanout + 1 :]:
        copy.wait()
    for v in range(1, fanout + 1):
        copies[v].wait()
        begin = begins[v - 1]
        end = begins[v]

        def body(i, carry, v=v, begin=begin):
            for u in range(UNROLL):
                at = begin + i * UNROLL + u
                to = places[at]
                self_rows[pl.ds(to, 1), :] = table[pl.ds(ids[0][at], 1), :]
                total = tree_sum([table[pl.ds(ids[k][at], 1), :] for k in range(1, v + 1)])
                mean_rows[pl.ds(to, 1), :] = total * (1.0 / v)
            return carry

        lax.fori_loop(0, jnp.right_shift(end - begin, UNROLL.bit_length() - 1), body, 0)


def write_out(x, width, self_rows, mean_rows, keep, send):
    lane = iota((CAP, LANES), 1)
    rest = 2 * width - LANES
    for ref, side in ((keep, x), (send, 1 - x)):
        turned = []
        for z in range(2):
            at = pl.multiple_of((z * 2 + side) * CAP, CAP)
            mean = jnp.where(lane < width, mean_rows[pl.ds(at, CAP), :], 0.0)
            turned.append(pltpu.roll(mean, width, 1))
            own = self_rows[pl.ds(at, CAP), :]
            ref[z, :, :] = jnp.where(lane < width, own, turned[z]).astype(BF16)
        right = pltpu.roll(turned[1], LANES // 2, 1)
        block = jnp.where(lane < LANES // 2, turned[0], right)
        used = (lane < rest) | ((lane >= LANES // 2) & (lane < LANES // 2 + rest))
        ref[2, :, :] = jnp.where(used, block, 0.0).astype(BF16)


def stage(source, staged, sems):
    blocks, _, part = staged.shape
    copies = [
        pltpu.make_async_copy(source.at[:, pl.ds(b * part, part)], staged.at[b], sems.at[b])
        for b in range(blocks)
    ]
    start_all(copies)
    return copies


def turn_staged(copies, staged, table, base):
    part = staged.shape[2]
    for b, copy in enumerate(copies):
        copy.wait()
        turn(staged.at[b], table, pl.multiple_of(base + b * part, part))


def own_kernel(which, halves, me, features, *refs):
    table, staged, sems = refs[-3:]
    length = features.shape[1]
    half = length // halves
    copies = stage(features.at[:, pl.ds(which * half, half)], staged, sems)
    turn_staged(copies, staged, table, me[2] * length + which * half)


def join_kernel(*refs):
    *parts, out = refs
    at = 0
    for part in parts:
        out[at : at + part.shape[0], :] = part[...]
        at += part.shape[0]


def hand_out(keep, send, keep_hbm, send_hbm, sems):
    copies = [
        pltpu.make_async_copy(send, send_hbm, sems.at[0]),
        pltpu.make_async_copy(keep, keep_hbm, sems.at[1]),
    ]
    start_all(copies)
    for copy in copies:
        copy.wait()


def first_kernel(
    fanout, me, lists, table_in, other, table, keep_hbm, send_hbm, *scratch
):
    del table_in
    ids = scratch[: fanout + 1]
    places, begins, self_rows, mean_rows, sems = scratch[fanout + 1 : fanout + 6]
    staged, staged_sems, keep, send, out_sems = scratch[fanout + 6 :]
    width, length = other.shape
    x, h, rep = me[0], me[1], me[2]
    staging = stage(other, staged, staged_sems)
    copies = list_copies(fanout, h, lists, ids, places, begins, sems)
    self_rows[...] = jnp.zeros_like(self_rows)
    mean_rows[...] = jnp.zeros_like(mean_rows)
    turn_staged(staging, staged, table, (1 - rep) * length)
    look_up(fanout, copies, table, ids, places, begins, self_rows, mean_rows)
    write_out(x, width, self_rows, mean_rows, keep, send)
    hand_out(keep, send, keep_hbm, send_hbm, out_sems)


def second_kernel(fanout, width, me, lists, table, keep_hbm, send_hbm, *scratch):
    ids = scratch[: fanout + 1]
    places, begins, self_rows, mean_rows, sems, keep, send, out_sems = scratch[fanout + 1 :]
    x, h = me[0], 1 - me[1]
    copies = list_copies(fanout, h, lists, ids, places, begins, sems)
    self_rows[...] = jnp.zeros_like(self_rows)
    mean_rows[...] = jnp.zeros_like(mean_rows)
    look_up(fanout, copies, table, ids, places, begins, self_rows, mean_rows)
    write_out(x, width, self_rows, mean_rows, keep, send)
    hand_out(keep, send, keep_hbm, send_hbm, out_sems)


def partials(blocks, weights):
    rest = weights.shape[0] - LANES
    return [
        jnp.dot(blocks[z], weights[0:LANES, :], preferred_element_type=F32)
        + jnp.dot(
            blocks[2, :, z * LANES // 2 : z * LANES // 2 + rest],
            weights[LANES:, :],
            preferred_element_type=F32,
        )
        for z in range(2)
    ]


def far_kernel(me, keep, got, weights, weights_got, out_0, out_1):
    zl = me[3]
    pre = [a + b for a, b in zip(partials(keep, weights), partials(got, weights_got))]
    out_0[...] = jnp.where(zl == 0, pre[0], pre[1]).astype(BF16)
    out_1[...] = jnp.where(zl == 0, pre[1], pre[0]).astype(BF16)


def near_kernel(me, keep_hbm, got, weights, weights_got, out_0, out_1, keep, sem):
    copy = pltpu.make_async_copy(keep_hbm, keep, sem)
    copy.start()
    zl = me[3]
    theirs = partials(got, weights_got)
    copy.wait()
    pre = [a + b for a, b in zip(partials(keep, weights), theirs)]
    out_0[...] = jnp.where(zl == 0, pre[0], pre[1])
    out_1[...] = jnp.where(zl == 0, pre[1], pre[0]).astype(BF16)


def last_kernel(
    mine, a, b, c, counts, bias_one, self_two, neigh_two, bias_two, out_weight, out_bias, out
):
    pre = mine[...] + a[...].astype(F32) + b[...].astype(F32) + c[...].astype(F32)
    hidden = jnp.maximum(pre + bias_one[...], 0.0).astype(BF16)
    seeds = counts.shape[1]
    same = iota((seeds, seeds), 0) == iota((seeds, seeds), 1)
    count = jnp.sum(jnp.where(same, counts[...].astype(F32), 0.0), axis=1, keepdims=True)
    count = count.astype(I32)
    earlier = (iota((seeds, seeds), 0) > iota((seeds, seeds), 1)).astype(BF16)
    needs = jnp.broadcast_to((count + 1).astype(F32), (seeds, LANES)).astype(BF16)
    offset = jnp.dot(earlier, needs, preferred_element_type=F32)[:, 0:1].astype(I32)
    place = iota((seeds, CAP), 1) - offset
    is_self = (place == 0).astype(F32).astype(BF16)
    is_near = ((place >= 1) & (place <= count)).astype(F32).astype(BF16)
    own = jnp.dot(is_self, hidden, preferred_element_type=F32).astype(BF16)
    total = jnp.dot(is_near, hidden, preferred_element_type=F32)
    mean = (total / count.astype(F32)).astype(BF16)
    pre_two = (
        jnp.dot(own, self_two[...], preferred_element_type=F32)
        + jnp.dot(mean, neigh_two[...], preferred_element_type=F32)
        + bias_two[...]
    )
    hidden_two = jnp.maximum(pre_two, 0.0).astype(BF16)
    logits = lax.dot_general(
        hidden_two, out_weight[...], (((1,), (1,)), ((), ())), preferred_element_type=F32
    )
    out[...] = logits + out_bias[...]


def params(limit):
    return pltpu.CompilerParams(vmem_limit_bytes=limit * MIB)


def shape(dims, dtype):
    return jax.ShapeDtypeStruct(dims, dtype)


def order_call(per_seed, me, own, got, self_ids, neighbour_ids, count_one):
    owners = sum(x.shape[0] for x in (own, *got))
    lists, most = pl.pallas_call(
        functools.partial(order_kernel, per_seed),
        out_shape=(shape((2, neighbour_ids.shape[0] + 3, 16, LANES), I32), shape((1,), I32)),
        in_specs=[SMEM] + [VMEM] * 8,
        out_specs=(VMEM, SMEM),
        scratch_shapes=[pltpu.VMEM((owners, own.shape[1]), I32)],
        compiler_params=params(10),
        name="order",
    )(me, own, *got, self_ids, neighbour_ids, count_one)
    return lists.reshape(-1), most[0]


def list_scratch(fanout):
    return (
        [pltpu.SMEM((POSITIONS,), I32) for _ in range(fanout + 2)]
        + [pltpu.SMEM((LANES,), I32)]
        + [pltpu.VMEM((4 * CAP + 8, LANES), F32) for _ in range(2)]
        + [pltpu.SemaphoreType.DMA((fanout + 3,))]
    )


def own_call(which, halves, me, features, *table):
    width, length = features.shape
    parts = 8 // halves
    return pl.pallas_call(
        functools.partial(own_kernel, which, halves),
        out_shape=shape((2 * length, LANES), F32),
        in_specs=[SMEM, HBM] + [VMEM] * len(table),
        out_specs=VMEM,
        scratch_shapes=[
            pltpu.VMEM((parts, width, length // 8), BF16),
            pltpu.SemaphoreType.DMA((parts,)),
        ],
        input_output_aliases={2: 0} if table else {},
        compiler_params=params(FIRST_MIB if table else OWN_MIB),
        name="own_rows",
    )(me, features, *table)


def join_call(*parts):
    rows = sum(part.shape[0] for part in parts)
    return pl.pallas_call(
        join_kernel,
        out_shape=shape((rows, parts[0].shape[1]), parts[0].dtype),
        in_specs=[VMEM] * len(parts),
        out_specs=VMEM,
        compiler_params=params(1),
        name="join",
    )(*parts)


def first_call(fanout, me, lists, table, other):
    width, length = other.shape
    dims = (3, CAP, LANES)
    return pl.pallas_call(
        functools.partial(first_kernel, fanout),
        out_shape=(shape((2 * length, LANES), F32), pltpu.HBM(dims, BF16), pltpu.HBM(dims, BF16)),
        in_specs=[SMEM, ANY, VMEM, HBM],
        out_specs=(VMEM, HBM, HBM),
        scratch_shapes=list_scratch(fanout)
        + [
            pltpu.VMEM((8, width, length // 8), BF16),
            pltpu.SemaphoreType.DMA((8,)),
            pltpu.VMEM(dims, BF16),
            pltpu.VMEM(dims, BF16),
            pltpu.SemaphoreType.DMA((2,)),
        ],
        input_output_aliases={2: 0},
        compiler_params=params(FIRST_MIB),
        name="first_half",
    )(me, lists, table, other)


def second_call(fanout, width, me, lists, table):
    dims = (3, CAP, LANES)
    halves = pltpu.HBM(dims, BF16)
    return pl.pallas_call(
        functools.partial(second_kernel, fanout, width),
        out_shape=(halves, halves),
        in_specs=[SMEM, ANY, VMEM],
        out_specs=(HBM, HBM),
        scratch_shapes=list_scratch(fanout)
        + [pltpu.VMEM(dims, BF16) for _ in range(2)]
        + [pltpu.SemaphoreType.DMA((2,))],
        compiler_params=params(10),
        name="second_half",
    )(me, lists, table)


def far_call(me, keep, got, weights, weights_got):
    part = shape((CAP, weights.shape[1]), BF16)
    return pl.pallas_call(
        far_kernel,
        out_shape=(part, part),
        in_specs=[SMEM] + [VMEM] * 4,
        out_specs=(VMEM, VMEM),
        compiler_params=params(10),
        name="project_far",
    )(me, keep, got, weights, weights_got)


def near_call(me, keep, got, weights, weights_got):
    dims = (CAP, weights.shape[1])
    return pl.pallas_call(
        near_kernel,
        out_shape=(shape(dims, F32), shape(dims, BF16)),
        in_specs=[SMEM, HBM] + [VMEM] * 3,
        out_specs=(VMEM, VMEM),
        scratch_shapes=[pltpu.VMEM(keep.shape, BF16), pltpu.SemaphoreType.DMA],
        compiler_params=params(10),
        name="project_near",
    )(me, pltpu.with_memory_space_constraint(keep, pltpu.HBM), got, weights, weights_got)


def last_call(*args):
    seeds = args[4].shape[1]
    classes = args[-1].shape[1]
    return pl.pallas_call(
        last_kernel,
        out_shape=shape((seeds, classes), F32),
        in_specs=[VMEM] * len(args),
        out_specs=VMEM,
        compiler_params=params(10),
        name="layer_two",
    )(*args)


def main(
    features,
    self_ids,
    neighbour_ids,
    count_one,
    count_two,
    self_one,
    neigh_one,
    bias_one,
    self_two,
    neigh_two,
    bias_two,
    out_weight,
    out_bias,
):
    owners = lax.axis_size("col")
    seeds = count_two.shape[0]
    per_owner = self_ids.shape[0] // owners
    per_seed = per_owner // seeds
    fanout = neighbour_ids.shape[0]
    width = features.shape[0]
    col = lax.axis_index("col")
    rep = lax.axis_index("rep")
    z = col // 2
    me = jnp.stack([col % 2, 1 - z // 2, rep, z % 2, col]).astype(I32)

    def across(value, bit):
        return lax.ppermute(value, "col", [(i, i ^ bit) for i in range(owners)])

    other = lax.ppermute(features, "rep", [(0, 1), (1, 0)])
    held = pltpu.with_memory_space_constraint(features, pltpu.HBM)
    own = count_two[None, :]
    got_1 = across(own, 1)
    weights = join_call(self_one, neigh_one)
    table, got_1, weights = lax.optimization_barrier(
        (own_call(0, 2, me, held), got_1, weights)
    )
    pair = join_call(own, got_1)
    got = tuple(across(pair, bit) for bit in (4, 6, 2))
    weights_got = across(weights, 1)
    table, got, weights_got = lax.optimization_barrier(
        (own_call(1, 2, me, held, table), got, weights_got)
    )
    got = (got_1, got[2], got[0], got[1])
    lists, most = order_call(per_seed, me, own, got, self_ids, neighbour_ids, count_one)
    table, keep_far, send_far = first_call(fanout, me, lists, table, other)
    got_far = across(send_far, 1)
    keep_near, send_near = second_call(fanout, width, me, lists, table)
    far = far_call(me, keep_far, got_far, weights, weights_got)
    far, send_near = lax.optimization_barrier((far, send_near))
    far_got = [across(far[0], 4), across(far[1], 6)]
    got_near = across(send_near, 1)
    near = near_call(me, keep_near, got_near, weights, weights_got)
    far_got.append(across(near[1], 2))
    fast = last_call(
        near[0],
        *far_got,
        own,
        bias_one[None, :],
        self_two,
        neigh_two,
        bias_two[None, :],
        out_weight.T,
        out_bias[None, :],
    )
    return lax.cond(
        most > CAP,
        lambda: general(
            other,
            features,
            self_ids,
            neighbour_ids,
            count_one,
            count_two,
            self_one,
            neigh_one,
            bias_one,
            self_two,
            neigh_two,
            bias_two,
            out_weight,
            out_bias,
        ),
        lambda: fast,
    )


def local(*args):
    features, self_ids, neighbour_ids = args[0], args[1], args[2]
    sizes = (lax.axis_size("groups"), lax.axis_size("col"), lax.axis_size("rep"))
    small = (
        sizes == (2, 8, 2)
        and LANES // 2 < features.shape[0] <= 3 * LANES // 4
        and features.shape[1] <= 32768
        and self_ids.shape[0] * (neighbour_ids.shape[0] + 1) <= 2**17
        and neighbour_ids.shape[0] <= 15
    )
    if small:
        return main(*args)
    return general(lax.ppermute(features, "rep", [(0, 1), (1, 0)]), *args)


def solution(mesh):
    placed = (
        P("col", ("groups", "rep")),
        P(("groups", "rep")),
        P(None, ("groups", "rep")),
        P(("groups", "rep")),
        P(("groups", "col", "rep")),
        P("col", None),
        P("col", None),
        P(),
        P(),
        P(),
        P(),
        P(),
        P(),
    )
    return jax.shard_map(
        local,
        mesh=mesh,
        in_specs=placed,
        out_specs=P(("groups", "col", "rep"), None),
        check_vma=False,
    )
```

```python
import functools

import jax
import jax.numpy as jnp
import numpy as np
from jax import lax
from jax.experimental import pallas as pl
from jax.experimental.pallas import tpu as pltpu
from jax.sharding import PartitionSpec as P

CAP = 272
UNROLL = 8
POSITIONS = 10 * 128
FIRST_MIB = 12
OWN_MIB = 18
LANES = 128
MIB = 2**20
BF16 = jnp.bfloat16
F32 = jnp.float32
I32 = jnp.int32


def gathered(value, axis):
    copies = jnp.broadcast_to(value[None], (lax.axis_size(axis),) + value.shape)
    pieces = lax.all_to_all(copies, axis, split_axis=0, concat_axis=0, tiled=True)
    return pieces.reshape((-1,) + value.shape[1:])


def general(
    other,
    features,
    self_ids,
    neighbour_ids,
    count_one,
    count_two,
    self_one,
    neigh_one,
    bias_one,
    self_two,
    neigh_two,
    bias_two,
    out_weight,
    out_bias,
):
    mine = jnp.where(lax.axis_index("rep") == 0, 0, 1)
    table_cols = jnp.where(
        mine == 0,
        jnp.concatenate([features, other], axis=1),
        jnp.concatenate([other, features], axis=1),
    )
    table_rows = table_cols.T
    blocks = lax.axis_size("col")
    total_rows = self_ids.shape[0]
    per_owner = total_rows // blocks
    fanout = neighbour_ids.shape[0]
    width = table_rows.shape[1]
    all_ids = jnp.concatenate([self_ids[None, :], neighbour_ids], axis=0)
    fetched = jnp.take(table_rows, all_ids, axis=0)
    self_x = fetched[0]
    mask = (jnp.arange(fanout)[:, None] < count_one[None, :]).astype(BF16)
    summed = jnp.einsum("kmc,km->mc", fetched[1:], mask, preferred_element_type=F32)
    mean_one = (summed / count_one[:, None].astype(F32)).astype(BF16)
    full_self, full_neigh = gathered(self_one, "col"), gathered(neigh_one, "col")
    stacked = jnp.stack([self_x, mean_one], axis=0).reshape(2, blocks, per_owner, width)
    pieces = lax.all_to_all(stacked, "col", split_axis=1, concat_axis=3, tiled=True)
    pre_one = jnp.dot(pieces[0, 0], full_self, preferred_element_type=F32) + jnp.dot(
        pieces[1, 0], full_neigh, preferred_element_type=F32
    )
    hidden_one = jax.nn.relu(pre_one + bias_one).astype(BF16)
    seeds = count_two.shape[0]
    hidden = hidden_one.shape[1]
    grouped = hidden_one.reshape(seeds, per_owner // seeds, hidden)
    mask_two = (jnp.arange(grouped.shape[1] - 1)[None, :] < count_two[:, None]).astype(BF16)
    summed_two = jnp.einsum("skh,sk->sh", grouped[:, 1:, :], mask_two, preferred_element_type=F32)
    mean_two = (summed_two / count_two[:, None].astype(F32)).astype(BF16)
    pre_two = jnp.dot(grouped[:, 0, :], self_two, preferred_element_type=F32) + jnp.dot(
        mean_two, neigh_two, preferred_element_type=F32
    )
    hidden_two = jax.nn.relu(pre_two + bias_two).astype(BF16)
    return jnp.dot(hidden_two, out_weight, preferred_element_type=F32) + out_bias


def iota(shape, dim):
    return lax.broadcasted_iota(I32, shape, dim)


def tree_sum(terms):
    while len(terms) > 1:
        odd = [terms[-1]] if len(terms) % 2 else []
        terms = [a + b for a, b in zip(terms[::2], terms[1::2])] + odd
    return terms[0]


VMEM = pl.BlockSpec(memory_space=pltpu.VMEM)
SMEM = pl.BlockSpec(memory_space=pltpu.SMEM)
HBM = pl.BlockSpec(memory_space=pltpu.HBM)
ANY = pl.BlockSpec(memory_space=pl.ANY)


def start_all(copies):
    for copy in copies:
        copy.start()


def turn(source, table, base):
    width, length = source.shape
    step = 512
    unroll = 8

    def body(i, carry):
        for u in range(unroll):
            off = pl.multiple_of((i * unroll + u) * step, step)
            rows = source[:, pl.ds(off, step)].T.astype(F32)
            table[pl.ds(pl.multiple_of(base + off, step), step), 0:width] = rows
        return carry

    lax.fori_loop(0, length // step // unroll, body, 0)


def order_kernel(
    per_seed, me, own, got_1, got_2, got_4, got_6, self_ids, neighbour_ids, count_one, lists, most, counts_rel
):
    owners, seeds = counts_rel.shape
    fanout = neighbour_ids.shape[0]
    per_owner = count_one.shape[0] // owners
    half = owners // 2
    mine = me[4]
    counts_rel[0:1, :] = own[...]
    counts_rel[1:2, :] = got_1[...]
    counts_rel[2:4, :] = got_2[...]
    counts_rel[4:6, :] = got_4[...]
    counts_rel[6:8, :] = got_6[...]
    own_ids = self_ids[...].reshape(1, owners * per_owner)
    ones = count_one[...].reshape(1, owners * per_owner)
    counts = jnp.concatenate(
        [counts_rel[pl.ds(jnp.bitwise_xor(mine, c), 1), :] for c in range(owners)], axis=0
    ).astype(F32)
    needs = (counts + 1.0).astype(BF16)
    most[0] = jnp.max(jnp.sum(counts + 1.0, axis=1, keepdims=True)).astype(I32)
    column = iota((seeds, per_owner), 1).astype(F32)
    seed_of = jnp.floor((column + 0.5) * (1.0 / per_seed))
    seed = iota((seeds, per_owner), 0).astype(F32)
    t = column[0:1, :] - seed_of[0:1, :] * per_seed
    of_row = jnp.dot(
        counts.astype(BF16), (seed == seed_of).astype(BF16), preferred_element_type=F32
    )
    slot = t + jnp.dot(needs, (seed < seed_of).astype(BF16), preferred_element_type=F32)
    used = (t <= of_row) & (slot < CAP)
    slot = slot.astype(I32)
    keys = [
        jnp.where(used[c : c + 1, :], ones[:, c * per_owner : (c + 1) * per_owner], 0)
        for c in range(owners)
    ]
    kinds = [
        iota((16, per_owner), 0) == jnp.broadcast_to(key, (16, per_owner)) for key in keys
    ]
    stacked = jnp.concatenate([k.astype(F32).astype(BF16) for k in kinds], axis=0)
    left = (iota((per_owner, per_owner), 0) < iota((per_owner, per_owner), 1)).astype(BF16)
    prefix = jnp.dot(stacked, left, preferred_element_type=F32)
    total = jnp.dot(stacked, jnp.ones((per_owner, LANES), BF16), preferred_element_type=F32)
    for h in range(2):
        carry = jnp.zeros((16, LANES), F32)
        carries = []
        for c in range(h * half, (h + 1) * half):
            carries.append(carry)
            carry = carry + total[c * 16 : (c + 1) * 16, :]
        sizes = jnp.floor((carry + (UNROLL - 1)) * (1.0 / UNROLL)) * UNROLL
        bases = [jnp.zeros((1, LANES), F32)]
        for v in range(1, 16):
            bases.append(bases[-1] + sizes[v : v + 1, :])
        first = jnp.concatenate([bases[0]] + bases[:15], axis=0)
        sums = jnp.zeros((2 * (fanout + 2) * 16, LANES), F32)
        for i, c in enumerate(range(h * half, (h + 1) * half)):
            begin = (first + carries[i])[:, 0:1]
            spot = jnp.where(kinds[c], prefix[c * 16 : (c + 1) * 16, :] + begin, 0.0)
            spot = jnp.sum(spot, axis=0, keepdims=True).astype(I32)
            spot = jnp.where(keys[c] > 0, spot, -1)
            spot_lo = jnp.bitwise_and(spot, LANES - 1)
            spot_hi = jnp.right_shift(spot, 7)
            lane = (iota((LANES, per_owner), 0) == spot_lo).astype(F32).astype(BF16)
            at_hi = (iota((16, per_owner), 0) == spot_hi).astype(F32)
            columns = slice(c * per_owner, (c + 1) * per_owner)
            rows = [own_ids[:, columns]]
            rows += [neighbour_ids[k : k + 1, columns] for k in range(fanout)]
            rows += [half * CAP - (slot[c : c + 1, :] + i * CAP)]
            parts = []
            for row in rows:
                for byte in (jnp.right_shift(row, 8), jnp.bitwise_and(row, 255)):
                    value = jnp.broadcast_to(byte.astype(F32), (16, per_owner))
                    parts.append((at_hi * value).astype(BF16))
            sums = sums + lax.dot_general(
                jnp.concatenate(parts, axis=0),
                lane,
                (((1,), (1,)), ((), ())),
                preferred_element_type=F32,
            )
        for k in range(fanout + 2):
            hi = sums[32 * k : 32 * k + 16, :]
            lo = sums[32 * k + 16 : 32 * k + 32, :]
            value = (hi * 256.0 + lo).astype(I32)
            lists[h, k, :, :] = value if k <= fanout else half * CAP - value
        lane = iota((8, LANES), 1)
        begins = jnp.zeros((8, LANES), F32)
        for v in range(16):
            begins = begins + jnp.where(lane == v, bases[v], 0.0)
        lists[h, fanout + 2, 0:8, :] = begins.astype(I32)
        lists[h, fanout + 2, 8:16, :] = jnp.zeros((8, LANES), I32)


def list_copies(fanout, h, lists, ids, places, begins, sems):
    block = 16 * LANES

    def piece(k, length):
        at = pl.multiple_of((h * (fanout + 3) + k) * block, block)
        return lists.at[pl.ds(at, length)]

    last = fanout + 2
    copies = [
        pltpu.make_async_copy(piece(k, POSITIONS), ref, sems.at[k])
        for k, ref in enumerate(list(ids) + [places])
    ]
    copies.append(pltpu.make_async_copy(piece(last, LANES), begins, sems.at[last]))
    start_all(copies[fanout + 1 :] + copies[: fanout + 1])
    return copies


def look_up(fanout, copies, table, ids, places, begins, self_rows, mean_rows):
    for copy in [copies[0]] + copies[fanout + 1 :]:
        copy.wait()
    for v in range(1, fanout + 1):
        copies[v].wait()
        begin = begins[v - 1]
        end = begins[v]

        def body(i, carry, v=v, begin=begin):
            for u in range(UNROLL):
                at = begin + i * UNROLL + u
                to = places[at]
                self_rows[pl.ds(to, 1), :] = table[pl.ds(ids[0][at], 1), :]
                total = tree_sum([table[pl.ds(ids[k][at], 1), :] for k in range(1, v + 1)])
                mean_rows[pl.ds(to, 1), :] = total * (1.0 / v)
            return carry

        lax.fori_loop(0, jnp.right_shift(end - begin, UNROLL.bit_length() - 1), body, 0)


def lay_out(ref, side, width, self_rows, mean_rows):
    lane = iota((CAP, LANES), 1)
    rest = 2 * width - LANES
    turned = []
    for z in range(2):
        at = pl.multiple_of((z * 2 + side) * CAP, CAP)
        mean = jnp.where(lane < width, mean_rows[pl.ds(at, CAP), :], 0.0)
        turned.append(pltpu.roll(mean, width, 1))
        own = self_rows[pl.ds(at, CAP), :]
        ref[z, :, :] = jnp.where(lane < width, own, turned[z]).astype(BF16)
    right = pltpu.roll(turned[1], LANES // 2, 1)
    block = jnp.where(lane < LANES // 2, turned[0], right)
    used = (lane < rest) | ((lane >= LANES // 2) & (lane < LANES // 2 + rest))
    ref[2, :, :] = jnp.where(used, block, 0.0).astype(BF16)


def stage(source, staged, sems):
    blocks, _, part = staged.shape
    copies = [
        pltpu.make_async_copy(source.at[:, pl.ds(b * part, part)], staged.at[b], sems.at[b])
        for b in range(blocks)
    ]
    start_all(copies)
    return copies


def turn_staged(copies, staged, table, base):
    part = staged.shape[2]
    for b, copy in enumerate(copies):
        copy.wait()
        turn(staged.at[b], table, pl.multiple_of(base + b * part, part))


def own_kernel(which, halves, me, features, *refs):
    table, staged, sems = refs[-3:]
    length = features.shape[1]
    half = length // halves
    copies = stage(features.at[:, pl.ds(which * half, half)], staged, sems)
    turn_staged(copies, staged, table, me[2] * length + which * half)


def join_kernel(*refs):
    *parts, out = refs
    at = 0
    for part in parts:
        out[at : at + part.shape[0], :] = part[...]
        at += part.shape[0]


def hand_out(x, width, self_rows, mean_rows, keep, send, keep_hbm, send_hbm, sems):
    copies = []
    for i, (ref, out, side) in enumerate(((send, send_hbm, 1 - x), (keep, keep_hbm, x))):
        lay_out(ref, side, width, self_rows, mean_rows)
        copies.append(pltpu.make_async_copy(ref, out, sems.at[i]))
        copies[-1].start()
    for copy in copies:
        copy.wait()


def first_kernel(
    fanout, me, lists, table_in, other, table, keep_hbm, send_hbm, *scratch
):
    del table_in
    ids = scratch[: fanout + 1]
    places, begins, self_rows, mean_rows, sems = scratch[fanout + 1 : fanout + 6]
    staged, staged_sems, keep, send, out_sems = scratch[fanout + 6 :]
    width, length = other.shape
    x, h, rep = me[0], me[1], me[2]
    staging = stage(other, staged, staged_sems)
    copies = list_copies(fanout, h, lists, ids, places, begins, sems)
    self_rows[...] = jnp.zeros_like(self_rows)
    mean_rows[...] = jnp.zeros_like(mean_rows)
    turn_staged(staging, staged, table, (1 - rep) * length)
    look_up(fanout, copies, table, ids, places, begins, self_rows, mean_rows)
    hand_out(x, width, self_rows, mean_rows, keep, send, keep_hbm, send_hbm, out_sems)


def second_kernel(fanout, width, me, lists, table, keep_hbm, send_hbm, *scratch):
    ids = scratch[: fanout + 1]
    places, begins, self_rows, mean_rows, sems, keep, send, out_sems = scratch[fanout + 1 :]
    x, h = me[0], 1 - me[1]
    copies = list_copies(fanout, h, lists, ids, places, begins, sems)
    self_rows[...] = jnp.zeros_like(self_rows)
    mean_rows[...] = jnp.zeros_like(mean_rows)
    look_up(fanout, copies, table, ids, places, begins, self_rows, mean_rows)
    hand_out(x, width, self_rows, mean_rows, keep, send, keep_hbm, send_hbm, out_sems)


def partials(blocks, weights):
    rest = weights.shape[0] - LANES
    return [
        jnp.dot(blocks[z], weights[0:LANES, :], preferred_element_type=F32)
        + jnp.dot(
            blocks[2, :, z * LANES // 2 : z * LANES // 2 + rest],
            weights[LANES:, :],
            preferred_element_type=F32,
        )
        for z in range(2)
    ]


def far_kernel(me, keep, got, weights, weights_got, later, out_0, out_1, loaded, sem):
    copy = pltpu.make_async_copy(later, loaded, sem)
    copy.start()
    zl = me[3]
    pre = [a + b for a, b in zip(partials(keep, weights), partials(got, weights_got))]
    out_0[...] = jnp.where(zl == 0, pre[0], pre[1]).astype(BF16)
    out_1[...] = jnp.where(zl == 0, pre[1], pre[0]).astype(BF16)
    copy.wait()


def near_kernel(me, keep, got, weights, weights_got, out_0, out_1):
    zl = me[3]
    theirs = partials(got, weights_got)
    pre = [a + b for a, b in zip(partials(keep, weights), theirs)]
    out_0[...] = jnp.where(zl == 0, pre[0], pre[1])
    out_1[...] = jnp.where(zl == 0, pre[1], pre[0]).astype(BF16)


def last_kernel(
    mine, a, b, c, counts, bias_one, self_two, neigh_two, bias_two, out_weight, out_bias, out
):
    pre = mine[...] + a[...].astype(F32) + b[...].astype(F32) + c[...].astype(F32)
    hidden = jnp.maximum(pre + bias_one[...], 0.0).astype(BF16)
    seeds = counts.shape[1]
    same = iota((seeds, seeds), 0) == iota((seeds, seeds), 1)
    count = jnp.sum(jnp.where(same, counts[...].astype(F32), 0.0), axis=1, keepdims=True)
    count = count.astype(I32)
    earlier = (iota((seeds, seeds), 0) > iota((seeds, seeds), 1)).astype(BF16)
    needs = jnp.broadcast_to((count + 1).astype(F32), (seeds, LANES)).astype(BF16)
    offset = jnp.dot(earlier, needs, preferred_element_type=F32)[:, 0:1].astype(I32)
    place = iota((seeds, CAP), 1) - offset
    is_self = (place == 0).astype(F32).astype(BF16)
    is_near = ((place >= 1) & (place <= count)).astype(F32).astype(BF16)
    own = jnp.dot(is_self, hidden, preferred_element_type=F32).astype(BF16)
    total = jnp.dot(is_near, hidden, preferred_element_type=F32)
    mean = (total / count.astype(F32)).astype(BF16)
    pre_two = (
        jnp.dot(own, self_two[...], preferred_element_type=F32)
        + jnp.dot(mean, neigh_two[...], preferred_element_type=F32)
        + bias_two[...]
    )
    hidden_two = jnp.maximum(pre_two, 0.0).astype(BF16)
    logits = lax.dot_general(
        hidden_two, out_weight[...], (((1,), (1,)), ((), ())), preferred_element_type=F32
    )
    out[...] = logits + out_bias[...]


def params(limit):
    return pltpu.CompilerParams(vmem_limit_bytes=limit * MIB)


def shape(dims, dtype):
    return jax.ShapeDtypeStruct(dims, dtype)


def order_call(per_seed, me, own, got, self_ids, neighbour_ids, count_one):
    owners = sum(x.shape[0] for x in (own, *got))
    lists, most = pl.pallas_call(
        functools.partial(order_kernel, per_seed),
        out_shape=(shape((2, neighbour_ids.shape[0] + 3, 16, LANES), I32), shape((1,), I32)),
        in_specs=[SMEM] + [VMEM] * 8,
        out_specs=(VMEM, SMEM),
        scratch_shapes=[pltpu.VMEM((owners, own.shape[1]), I32)],
        compiler_params=params(10),
        name="order",
    )(me, own, *got, self_ids, neighbour_ids, count_one)
    return lists.reshape(-1), most[0]


def list_scratch(fanout):
    return (
        [pltpu.SMEM((POSITIONS,), I32) for _ in range(fanout + 2)]
        + [pltpu.SMEM((LANES,), I32)]
        + [pltpu.VMEM((4 * CAP + 8, LANES), F32) for _ in range(2)]
        + [pltpu.SemaphoreType.DMA((fanout + 3,))]
    )


def own_call(which, halves, me, features, *table):
    width, length = features.shape
    parts = 8 // halves
    return pl.pallas_call(
        functools.partial(own_kernel, which, halves),
        out_shape=shape((2 * length, LANES), F32),
        in_specs=[SMEM, HBM] + [VMEM] * len(table),
        out_specs=VMEM,
        scratch_shapes=[
            pltpu.VMEM((parts, width, length // 8), BF16),
            pltpu.SemaphoreType.DMA((parts,)),
        ],
        input_output_aliases={2: 0} if table else {},
        compiler_params=params(FIRST_MIB if table else OWN_MIB),
        name="own_rows",
    )(me, features, *table)


def join_call(*parts):
    rows = sum(part.shape[0] for part in parts)
    return pl.pallas_call(
        join_kernel,
        out_shape=shape((rows, parts[0].shape[1]), parts[0].dtype),
        in_specs=[VMEM] * len(parts),
        out_specs=VMEM,
        compiler_params=params(1),
        name="join",
    )(*parts)


def first_call(fanout, me, lists, table, other):
    width, length = other.shape
    dims = (3, CAP, LANES)
    return pl.pallas_call(
        functools.partial(first_kernel, fanout),
        out_shape=(shape((2 * length, LANES), F32), pltpu.HBM(dims, BF16), pltpu.HBM(dims, BF16)),
        in_specs=[SMEM, ANY, VMEM, HBM],
        out_specs=(VMEM, HBM, HBM),
        scratch_shapes=list_scratch(fanout)
        + [
            pltpu.VMEM((8, width, length // 8), BF16),
            pltpu.SemaphoreType.DMA((8,)),
            pltpu.VMEM(dims, BF16),
            pltpu.VMEM(dims, BF16),
            pltpu.SemaphoreType.DMA((2,)),
        ],
        input_output_aliases={2: 0},
        compiler_params=params(FIRST_MIB),
        name="first_half",
    )(me, lists, table, other)


def second_call(fanout, width, me, lists, table):
    dims = (3, CAP, LANES)
    halves = pltpu.HBM(dims, BF16)
    return pl.pallas_call(
        functools.partial(second_kernel, fanout, width),
        out_shape=(halves, halves),
        in_specs=[SMEM, ANY, VMEM],
        out_specs=(HBM, HBM),
        scratch_shapes=list_scratch(fanout)
        + [pltpu.VMEM(dims, BF16) for _ in range(2)]
        + [pltpu.SemaphoreType.DMA((2,))],
        compiler_params=params(10),
        name="second_half",
    )(me, lists, table)


def far_call(me, keep, got, weights, weights_got, later):
    part = shape((CAP, weights.shape[1]), BF16)
    return pl.pallas_call(
        far_kernel,
        out_shape=(part, part, shape(later.shape, BF16)),
        in_specs=[SMEM] + [VMEM] * 4 + [HBM],
        out_specs=(VMEM, VMEM, VMEM),
        scratch_shapes=[pltpu.SemaphoreType.DMA],
        compiler_params=params(10),
        name="project_far",
    )(me, keep, got, weights, weights_got, pltpu.with_memory_space_constraint(later, pltpu.HBM))


def near_call(me, keep, got, weights, weights_got):
    dims = (CAP, weights.shape[1])
    return pl.pallas_call(
        near_kernel,
        out_shape=(shape(dims, F32), shape(dims, BF16)),
        in_specs=[SMEM] + [VMEM] * 4,
        out_specs=(VMEM, VMEM),
        compiler_params=params(10),
        name="project_near",
    )(me, keep, got, weights, weights_got)


def last_call(*args):
    seeds = args[4].shape[1]
    classes = args[-1].shape[1]
    return pl.pallas_call(
        last_kernel,
        out_shape=shape((seeds, classes), F32),
        in_specs=[VMEM] * len(args),
        out_specs=VMEM,
        compiler_params=params(10),
        name="layer_two",
    )(*args)


def main(
    features,
    self_ids,
    neighbour_ids,
    count_one,
    count_two,
    self_one,
    neigh_one,
    bias_one,
    self_two,
    neigh_two,
    bias_two,
    out_weight,
    out_bias,
):
    owners = lax.axis_size("col")
    seeds = count_two.shape[0]
    per_owner = self_ids.shape[0] // owners
    per_seed = per_owner // seeds
    fanout = neighbour_ids.shape[0]
    width = features.shape[0]
    col = lax.axis_index("col")
    rep = lax.axis_index("rep")
    z = col // 2
    me = jnp.stack([col % 2, 1 - z // 2, rep, z % 2, col]).astype(I32)

    def across(value, bit):
        return lax.ppermute(value, "col", [(i, i ^ bit) for i in range(owners)])

    other = lax.ppermute(features, "rep", [(0, 1), (1, 0)])
    held = pltpu.with_memory_space_constraint(features, pltpu.HBM)
    own = count_two[None, :]
    got_1 = across(own, 1)
    weights = join_call(self_one, neigh_one)
    table, got_1, weights = lax.optimization_barrier(
        (own_call(0, 2, me, held), got_1, weights)
    )
    pair = join_call(own, got_1)
    got = tuple(across(pair, bit) for bit in (4, 6, 2))
    weights_got = across(weights, 1)
    table, got, weights_got = lax.optimization_barrier(
        (own_call(1, 2, me, held, table), got, weights_got)
    )
    got = (got_1, got[2], got[0], got[1])
    lists, most = order_call(per_seed, me, own, got, self_ids, neighbour_ids, count_one)
    table, keep_far, send_far = first_call(fanout, me, lists, table, other)
    got_far = across(send_far, 1)
    keep_near, send_near = second_call(fanout, width, me, lists, table)
    *far, keep_near = far_call(me, keep_far, got_far, weights, weights_got, keep_near)
    far, send_near = lax.optimization_barrier((far, send_near))
    far_got = [across(far[0], 4), across(far[1], 6)]
    got_near = across(send_near, 1)
    near = near_call(me, keep_near, got_near, weights, weights_got)
    far_got.append(across(near[1], 2))
    fast = last_call(
        near[0],
        *far_got,
        own,
        bias_one[None, :],
        self_two,
        neigh_two,
        bias_two[None, :],
        out_weight.T,
        out_bias[None, :],
    )
    return lax.cond(
        most > CAP,
        lambda: general(
            other,
            features,
            self_ids,
            neighbour_ids,
            count_one,
            count_two,
            self_one,
            neigh_one,
            bias_one,
            self_two,
            neigh_two,
            bias_two,
            out_weight,
            out_bias,
        ),
        lambda: fast,
    )


def local(*args):
    features, self_ids, neighbour_ids = args[0], args[1], args[2]
    sizes = (lax.axis_size("groups"), lax.axis_size("col"), lax.axis_size("rep"))
    small = (
        sizes == (2, 8, 2)
        and LANES // 2 < features.shape[0] <= 3 * LANES // 4
        and features.shape[1] <= 32768
        and self_ids.shape[0] * (neighbour_ids.shape[0] + 1) <= 2**17
        and neighbour_ids.shape[0] <= 15
    )
    if small:
        return main(*args)
    return general(lax.ppermute(features, "rep", [(0, 1), (1, 0)]), *args)


def solution(mesh):
    placed = (
        P("col", ("groups", "rep")),
        P(("groups", "rep")),
        P(None, ("groups", "rep")),
        P(("groups", "rep")),
        P(("groups", "col", "rep")),
        P("col", None),
        P("col", None),
        P(),
        P(),
        P(),
        P(),
        P(),
        P(),
    )
    return jax.shard_map(
        local,
        mesh=mesh,
        in_specs=placed,
        out_specs=P(("groups", "col", "rep"), None),
        check_vma=False,
    )
```

```python
import functools

import jax
import jax.numpy as jnp
import numpy as np
from jax import lax
from jax.experimental import pallas as pl
from jax.experimental.pallas import tpu as pltpu
from jax.sharding import PartitionSpec as P

CAP = 272
UNROLL = 8
POSITIONS = 10 * 128
FIRST_MIB = 12
OWN_MIB = 18
LANES = 128
MIB = 2**20
BF16 = jnp.bfloat16
F32 = jnp.float32
I32 = jnp.int32


def gathered(value, axis):
    copies = jnp.broadcast_to(value[None], (lax.axis_size(axis),) + value.shape)
    pieces = lax.all_to_all(copies, axis, split_axis=0, concat_axis=0, tiled=True)
    return pieces.reshape((-1,) + value.shape[1:])


def general(
    other,
    features,
    self_ids,
    neighbour_ids,
    count_one,
    count_two,
    self_one,
    neigh_one,
    bias_one,
    self_two,
    neigh_two,
    bias_two,
    out_weight,
    out_bias,
):
    mine = jnp.where(lax.axis_index("rep") == 0, 0, 1)
    table_cols = jnp.where(
        mine == 0,
        jnp.concatenate([features, other], axis=1),
        jnp.concatenate([other, features], axis=1),
    )
    table_rows = table_cols.T
    blocks = lax.axis_size("col")
    total_rows = self_ids.shape[0]
    per_owner = total_rows // blocks
    fanout = neighbour_ids.shape[0]
    width = table_rows.shape[1]
    all_ids = jnp.concatenate([self_ids[None, :], neighbour_ids], axis=0)
    fetched = jnp.take(table_rows, all_ids, axis=0)
    self_x = fetched[0]
    mask = (jnp.arange(fanout)[:, None] < count_one[None, :]).astype(BF16)
    summed = jnp.einsum("kmc,km->mc", fetched[1:], mask, preferred_element_type=F32)
    mean_one = (summed / count_one[:, None].astype(F32)).astype(BF16)
    full_self, full_neigh = gathered(self_one, "col"), gathered(neigh_one, "col")
    stacked = jnp.stack([self_x, mean_one], axis=0).reshape(2, blocks, per_owner, width)
    pieces = lax.all_to_all(stacked, "col", split_axis=1, concat_axis=3, tiled=True)
    pre_one = jnp.dot(pieces[0, 0], full_self, preferred_element_type=F32) + jnp.dot(
        pieces[1, 0], full_neigh, preferred_element_type=F32
    )
    hidden_one = jax.nn.relu(pre_one + bias_one).astype(BF16)
    seeds = count_two.shape[0]
    hidden = hidden_one.shape[1]
    grouped = hidden_one.reshape(seeds, per_owner // seeds, hidden)
    mask_two = (jnp.arange(grouped.shape[1] - 1)[None, :] < count_two[:, None]).astype(BF16)
    summed_two = jnp.einsum("skh,sk->sh", grouped[:, 1:, :], mask_two, preferred_element_type=F32)
    mean_two = (summed_two / count_two[:, None].astype(F32)).astype(BF16)
    pre_two = jnp.dot(grouped[:, 0, :], self_two, preferred_element_type=F32) + jnp.dot(
        mean_two, neigh_two, preferred_element_type=F32
    )
    hidden_two = jax.nn.relu(pre_two + bias_two).astype(BF16)
    return jnp.dot(hidden_two, out_weight, preferred_element_type=F32) + out_bias


def iota(shape, dim):
    return lax.broadcasted_iota(I32, shape, dim)


def tree_sum(terms):
    while len(terms) > 1:
        odd = [terms[-1]] if len(terms) % 2 else []
        terms = [a + b for a, b in zip(terms[::2], terms[1::2])] + odd
    return terms[0]


VMEM = pl.BlockSpec(memory_space=pltpu.VMEM)
SMEM = pl.BlockSpec(memory_space=pltpu.SMEM)
HBM = pl.BlockSpec(memory_space=pltpu.HBM)
ANY = pl.BlockSpec(memory_space=pl.ANY)


def start_all(copies):
    for copy in copies:
        copy.start()


def turn(source, table, base):
    width, length = source.shape
    step = 512
    unroll = 8

    def body(i, carry):
        for u in range(unroll):
            off = pl.multiple_of((i * unroll + u) * step, step)
            rows = source[:, pl.ds(off, step)].T.astype(F32)
            table[pl.ds(pl.multiple_of(base + off, step), step), 0:width] = rows
        return carry

    lax.fori_loop(0, length // step // unroll, body, 0)


def order_kernel(
    per_seed, me, own, got_1, got_2, got_4, got_6, self_ids, neighbour_ids, count_one, lists, most, counts_rel
):
    owners, seeds = counts_rel.shape
    fanout = neighbour_ids.shape[0]
    per_owner = count_one.shape[0] // owners
    half = owners // 2
    mine = me[4]
    counts_rel[0:1, :] = own[...]
    counts_rel[1:2, :] = got_1[...]
    counts_rel[2:4, :] = got_2[...]
    counts_rel[4:6, :] = got_4[...]
    counts_rel[6:8, :] = got_6[...]
    own_ids = self_ids[...].reshape(1, owners * per_owner)
    ones = count_one[...].reshape(1, owners * per_owner)
    counts = jnp.concatenate(
        [counts_rel[pl.ds(jnp.bitwise_xor(mine, c), 1), :] for c in range(owners)], axis=0
    ).astype(F32)
    needs = (counts + 1.0).astype(BF16)
    most[0] = jnp.max(jnp.sum(counts + 1.0, axis=1, keepdims=True)).astype(I32)
    column = iota((seeds, per_owner), 1).astype(F32)
    seed_of = jnp.floor((column + 0.5) * (1.0 / per_seed))
    seed = iota((seeds, per_owner), 0).astype(F32)
    t = column[0:1, :] - seed_of[0:1, :] * per_seed
    of_row = jnp.dot(
        counts.astype(BF16), (seed == seed_of).astype(BF16), preferred_element_type=F32
    )
    slot = t + jnp.dot(needs, (seed < seed_of).astype(BF16), preferred_element_type=F32)
    used = (t <= of_row) & (slot < CAP)
    slot = slot.astype(I32)
    keys = [
        jnp.where(used[c : c + 1, :], ones[:, c * per_owner : (c + 1) * per_owner], 0)
        for c in range(owners)
    ]
    kinds = [
        iota((16, per_owner), 0) == jnp.broadcast_to(key, (16, per_owner)) for key in keys
    ]
    stacked = jnp.concatenate([k.astype(F32).astype(BF16) for k in kinds], axis=0)
    left = (iota((per_owner, per_owner), 0) < iota((per_owner, per_owner), 1)).astype(BF16)
    prefix = jnp.dot(stacked, left, preferred_element_type=F32)
    total = jnp.dot(stacked, jnp.ones((per_owner, LANES), BF16), preferred_element_type=F32)
    for h in range(2):
        carry = jnp.zeros((16, LANES), F32)
        carries = []
        for c in range(h * half, (h + 1) * half):
            carries.append(carry)
            carry = carry + total[c * 16 : (c + 1) * 16, :]
        sizes = jnp.floor((carry + (UNROLL - 1)) * (1.0 / UNROLL)) * UNROLL
        bases = [jnp.zeros((1, LANES), F32)]
        for v in range(1, 16):
            bases.append(bases[-1] + sizes[v : v + 1, :])
        first = jnp.concatenate([bases[0]] + bases[:15], axis=0)
        sums = jnp.zeros((2 * (fanout + 2) * 16, LANES), F32)
        for i, c in enumerate(range(h * half, (h + 1) * half)):
            begin = (first + carries[i])[:, 0:1]
            spot = jnp.where(kinds[c], prefix[c * 16 : (c + 1) * 16, :] + begin, 0.0)
            spot = jnp.sum(spot, axis=0, keepdims=True).astype(I32)
            spot = jnp.where(keys[c] > 0, spot, -1)
            spot_lo = jnp.bitwise_and(spot, LANES - 1)
            spot_hi = jnp.right_shift(spot, 7)
            lane = (iota((LANES, per_owner), 0) == spot_lo).astype(F32).astype(BF16)
            at_hi = (iota((16, per_owner), 0) == spot_hi).astype(F32)
            columns = slice(c * per_owner, (c + 1) * per_owner)
            rows = [own_ids[:, columns]]
            rows += [neighbour_ids[k : k + 1, columns] for k in range(fanout)]
            rows += [half * CAP - (slot[c : c + 1, :] + i * CAP)]
            parts = []
            for row in rows:
                for byte in (jnp.right_shift(row, 8), jnp.bitwise_and(row, 255)):
                    value = jnp.broadcast_to(byte.astype(F32), (16, per_owner))
                    parts.append((at_hi * value).astype(BF16))
            sums = sums + lax.dot_general(
                jnp.concatenate(parts, axis=0),
                lane,
                (((1,), (1,)), ((), ())),
                preferred_element_type=F32,
            )
        for k in range(fanout + 2):
            hi = sums[32 * k : 32 * k + 16, :]
            lo = sums[32 * k + 16 : 32 * k + 32, :]
            value = (hi * 256.0 + lo).astype(I32)
            lists[h, k, :, :] = value if k <= fanout else half * CAP - value
        lane = iota((8, LANES), 1)
        begins = jnp.zeros((8, LANES), F32)
        for v in range(16):
            begins = begins + jnp.where(lane == v, bases[v], 0.0)
        lists[h, fanout + 2, 0:8, :] = begins.astype(I32)
        lists[h, fanout + 2, 8:16, :] = jnp.zeros((8, LANES), I32)


def list_copies(fanout, h, lists, ids, places, begins, sems):
    block = 16 * LANES

    def piece(k, length):
        at = pl.multiple_of((h * (fanout + 3) + k) * block, block)
        return lists.at[pl.ds(at, length)]

    last = fanout + 2
    copies = [
        pltpu.make_async_copy(piece(k, POSITIONS), ref, sems.at[k])
        for k, ref in enumerate(list(ids) + [places])
    ]
    copies.append(pltpu.make_async_copy(piece(last, LANES), begins, sems.at[last]))
    start_all(copies[fanout + 1 :] + copies[: fanout + 1])
    return copies


def look_up(fanout, copies, table, ids, places, begins, self_rows, mean_rows):
    for copy in [copies[0]] + copies[fanout + 1 :]:
        copy.wait()
    for v in range(1, fanout + 1):
        copies[v].wait()
        begin = begins[v - 1]
        end = begins[v]

        def body(i, carry, v=v, begin=begin):
            for u in range(UNROLL):
                at = begin + i * UNROLL + u
                to = places[at]
                self_rows[pl.ds(to, 1), :] = table[pl.ds(ids[0][at], 1), :]
                total = tree_sum([table[pl.ds(ids[k][at], 1), :] for k in range(1, v + 1)])
                mean_rows[pl.ds(to, 1), :] = total * (1.0 / v)
            return carry

        lax.fori_loop(0, jnp.right_shift(end - begin, UNROLL.bit_length() - 1), body, 0)


def write_out(x, width, self_rows, mean_rows, keep, send):
    lane = iota((CAP, LANES), 1)
    rest = 2 * width - LANES
    for ref, side in ((keep, x), (send, 1 - x)):
        turned = []
        for z in range(2):
            at = pl.multiple_of((z * 2 + side) * CAP, CAP)
            mean = jnp.where(lane < width, mean_rows[pl.ds(at, CAP), :], 0.0)
            turned.append(pltpu.roll(mean, width, 1))
            own = self_rows[pl.ds(at, CAP), :]
            ref[z, :, :] = jnp.where(lane < width, own, turned[z]).astype(BF16)
        right = pltpu.roll(turned[1], LANES // 2, 1)
        block = jnp.where(lane < LANES // 2, turned[0], right)
        used = (lane < rest) | ((lane >= LANES // 2) & (lane < LANES // 2 + rest))
        ref[2, :, :] = jnp.where(used, block, 0.0).astype(BF16)


def stage(source, staged, sems):
    blocks, _, part = staged.shape
    copies = [
        pltpu.make_async_copy(source.at[:, pl.ds(b * part, part)], staged.at[b], sems.at[b])
        for b in range(blocks)
    ]
    start_all(copies)
    return copies


def turn_staged(copies, staged, table, base):
    part = staged.shape[2]
    for b, copy in enumerate(copies):
        copy.wait()
        turn(staged.at[b], table, pl.multiple_of(base + b * part, part))


def own_kernel(which, halves, me, features, *refs):
    table, staged, sems = refs[-3:]
    length = features.shape[1]
    half = length // halves
    copies = stage(features.at[:, pl.ds(which * half, half)], staged, sems)
    turn_staged(copies, staged, table, me[2] * length + which * half)


def join_kernel(*refs):
    *parts, out = refs
    at = 0
    for part in parts:
        out[at : at + part.shape[0], :] = part[...]
        at += part.shape[0]


def hand_out(keep, send, keep_hbm, send_hbm, sems):
    copies = [
        pltpu.make_async_copy(send, send_hbm, sems.at[0]),
        pltpu.make_async_copy(keep, keep_hbm, sems.at[1]),
    ]
    start_all(copies)
    for copy in copies:
        copy.wait()


def first_kernel(
    fanout, me, lists, table_in, other, table, keep_hbm, send_hbm, *scratch
):
    del table_in
    ids = scratch[: fanout + 1]
    places, begins, self_rows, mean_rows, sems = scratch[fanout + 1 : fanout + 6]
    staged, staged_sems, keep, send, out_sems = scratch[fanout + 6 :]
    width, length = other.shape
    x, h, rep = me[0], me[1], me[2]
    staging = stage(other, staged, staged_sems)
    copies = list_copies(fanout, h, lists, ids, places, begins, sems)
    self_rows[...] = jnp.zeros_like(self_rows)
    mean_rows[...] = jnp.zeros_like(mean_rows)
    turn_staged(staging, staged, table, (1 - rep) * length)
    look_up(fanout, copies, table, ids, places, begins, self_rows, mean_rows)
    write_out(x, width, self_rows, mean_rows, keep, send)
    hand_out(keep, send, keep_hbm, send_hbm, out_sems)


def second_kernel(fanout, width, me, lists, table, keep_hbm, send_hbm, *scratch):
    ids = scratch[: fanout + 1]
    places, begins, self_rows, mean_rows, sems, keep, send, out_sems = scratch[fanout + 1 :]
    x, h = me[0], 1 - me[1]
    copies = list_copies(fanout, h, lists, ids, places, begins, sems)
    self_rows[...] = jnp.zeros_like(self_rows)
    mean_rows[...] = jnp.zeros_like(mean_rows)
    look_up(fanout, copies, table, ids, places, begins, self_rows, mean_rows)
    write_out(x, width, self_rows, mean_rows, keep, send)
    hand_out(keep, send, keep_hbm, send_hbm, out_sems)


def partials(blocks, weights):
    rest = weights.shape[0] - LANES
    return [
        jnp.dot(blocks[z], weights[0:LANES, :], preferred_element_type=F32)
        + jnp.dot(
            blocks[2, :, z * LANES // 2 : z * LANES // 2 + rest],
            weights[LANES:, :],
            preferred_element_type=F32,
        )
        for z in range(2)
    ]


def far_kernel(me, keep, got, weights, weights_got, out_0, out_1):
    zl = me[3]
    pre = [a + b for a, b in zip(partials(keep, weights), partials(got, weights_got))]
    out_0[...] = jnp.where(zl == 0, pre[0], pre[1]).astype(BF16)
    out_1[...] = jnp.where(zl == 0, pre[1], pre[0]).astype(BF16)


def near_kernel(me, keep_hbm, got, weights, weights_got, out_0, out_1, keep, sem):
    copy = pltpu.make_async_copy(keep_hbm, keep, sem)
    copy.start()
    zl = me[3]
    theirs = partials(got, weights_got)
    copy.wait()
    pre = [a + b for a, b in zip(partials(keep, weights), theirs)]
    out_0[...] = jnp.where(zl == 0, pre[0], pre[1])
    out_1[...] = jnp.where(zl == 0, pre[1], pre[0]).astype(BF16)


def last_kernel(
    mine, a, b, c, counts, bias_one, self_two, neigh_two, bias_two, out_weight, out_bias, out_hbm, out, sem
):
    pre = mine[...] + a[...].astype(F32) + b[...].astype(F32) + c[...].astype(F32)
    hidden = jnp.maximum(pre + bias_one[...], 0.0).astype(BF16)
    seeds = counts.shape[1]
    same = iota((seeds, seeds), 0) == iota((seeds, seeds), 1)
    count = jnp.sum(jnp.where(same, counts[...].astype(F32), 0.0), axis=1, keepdims=True)
    count = count.astype(I32)
    earlier = (iota((seeds, seeds), 0) > iota((seeds, seeds), 1)).astype(BF16)
    needs = jnp.broadcast_to((count + 1).astype(F32), (seeds, LANES)).astype(BF16)
    offset = jnp.dot(earlier, needs, preferred_element_type=F32)[:, 0:1].astype(I32)
    place = iota((seeds, CAP), 1) - offset
    is_self = (place == 0).astype(F32).astype(BF16)
    is_near = ((place >= 1) & (place <= count)).astype(F32).astype(BF16)
    own = jnp.dot(is_self, hidden, preferred_element_type=F32).astype(BF16)
    total = jnp.dot(is_near, hidden, preferred_element_type=F32)
    mean = (total / count.astype(F32)).astype(BF16)
    pre_two = (
        jnp.dot(own, self_two[...], preferred_element_type=F32)
        + jnp.dot(mean, neigh_two[...], preferred_element_type=F32)
        + bias_two[...]
    )
    hidden_two = jnp.maximum(pre_two, 0.0).astype(BF16)
    logits = lax.dot_general(
        hidden_two, out_weight[...], (((1,), (1,)), ((), ())), preferred_element_type=F32
    )
    out[...] = logits + out_bias[...]
    copy = pltpu.make_async_copy(out, out_hbm, sem)
    copy.start()
    copy.wait()


def params(limit):
    return pltpu.CompilerParams(vmem_limit_bytes=limit * MIB)


def shape(dims, dtype):
    return jax.ShapeDtypeStruct(dims, dtype)


def order_call(per_seed, me, own, got, self_ids, neighbour_ids, count_one):
    owners = sum(x.shape[0] for x in (own, *got))
    lists, most = pl.pallas_call(
        functools.partial(order_kernel, per_seed),
        out_shape=(shape((2, neighbour_ids.shape[0] + 3, 16, LANES), I32), shape((1,), I32)),
        in_specs=[SMEM] + [VMEM] * 8,
        out_specs=(VMEM, SMEM),
        scratch_shapes=[pltpu.VMEM((owners, own.shape[1]), I32)],
        compiler_params=params(10),
        name="order",
    )(me, own, *got, self_ids, neighbour_ids, count_one)
    return lists.reshape(-1), most[0]


def list_scratch(fanout):
    return (
        [pltpu.SMEM((POSITIONS,), I32) for _ in range(fanout + 2)]
        + [pltpu.SMEM((LANES,), I32)]
        + [pltpu.VMEM((4 * CAP + 8, LANES), F32) for _ in range(2)]
        + [pltpu.SemaphoreType.DMA((fanout + 3,))]
    )


def own_call(which, halves, me, features, *table):
    width, length = features.shape
    parts = 8 // halves
    return pl.pallas_call(
        functools.partial(own_kernel, which, halves),
        out_shape=shape((2 * length, LANES), F32),
        in_specs=[SMEM, HBM] + [VMEM] * len(table),
        out_specs=VMEM,
        scratch_shapes=[
            pltpu.VMEM((parts, width, length // 8), BF16),
            pltpu.SemaphoreType.DMA((parts,)),
        ],
        input_output_aliases={2: 0} if table else {},
        compiler_params=params(FIRST_MIB if table else OWN_MIB),
        name="own_rows",
    )(me, features, *table)


def join_call(*parts):
    rows = sum(part.shape[0] for part in parts)
    return pl.pallas_call(
        join_kernel,
        out_shape=shape((rows, parts[0].shape[1]), parts[0].dtype),
        in_specs=[VMEM] * len(parts),
        out_specs=VMEM,
        compiler_params=params(1),
        name="join",
    )(*parts)


def first_call(fanout, me, lists, table, other):
    width, length = other.shape
    dims = (3, CAP, LANES)
    return pl.pallas_call(
        functools.partial(first_kernel, fanout),
        out_shape=(shape((2 * length, LANES), F32), pltpu.HBM(dims, BF16), pltpu.HBM(dims, BF16)),
        in_specs=[SMEM, ANY, VMEM, HBM],
        out_specs=(VMEM, HBM, HBM),
        scratch_shapes=list_scratch(fanout)
        + [
            pltpu.VMEM((8, width, length // 8), BF16),
            pltpu.SemaphoreType.DMA((8,)),
            pltpu.VMEM(dims, BF16),
            pltpu.VMEM(dims, BF16),
            pltpu.SemaphoreType.DMA((2,)),
        ],
        input_output_aliases={2: 0},
        compiler_params=params(FIRST_MIB),
        name="first_half",
    )(me, lists, table, other)


def second_call(fanout, width, me, lists, table):
    dims = (3, CAP, LANES)
    halves = pltpu.HBM(dims, BF16)
    return pl.pallas_call(
        functools.partial(second_kernel, fanout, width),
        out_shape=(halves, halves),
        in_specs=[SMEM, ANY, VMEM],
        out_specs=(HBM, HBM),
        scratch_shapes=list_scratch(fanout)
        + [pltpu.VMEM(dims, BF16) for _ in range(2)]
        + [pltpu.SemaphoreType.DMA((2,))],
        compiler_params=params(10),
        name="second_half",
    )(me, lists, table)


def far_call(me, keep, got, weights, weights_got):
    part = shape((CAP, weights.shape[1]), BF16)
    return pl.pallas_call(
        far_kernel,
        out_shape=(part, part),
        in_specs=[SMEM] + [VMEM] * 4,
        out_specs=(VMEM, VMEM),
        compiler_params=params(10),
        name="project_far",
    )(me, keep, got, weights, weights_got)


def near_call(me, keep, got, weights, weights_got):
    dims = (CAP, weights.shape[1])
    return pl.pallas_call(
        near_kernel,
        out_shape=(shape(dims, F32), shape(dims, BF16)),
        in_specs=[SMEM, HBM] + [VMEM] * 3,
        out_specs=(VMEM, VMEM),
        scratch_shapes=[pltpu.VMEM(keep.shape, BF16), pltpu.SemaphoreType.DMA],
        compiler_params=params(10),
        name="project_near",
    )(me, pltpu.with_memory_space_constraint(keep, pltpu.HBM), got, weights, weights_got)


def last_call(*args):
    seeds = args[4].shape[1]
    classes = args[-1].shape[1]
    return pl.pallas_call(
        last_kernel,
        out_shape=pltpu.HBM((seeds, classes), F32),
        in_specs=[VMEM] * len(args),
        out_specs=HBM,
        scratch_shapes=[pltpu.VMEM((seeds, classes), F32), pltpu.SemaphoreType.DMA],
        compiler_params=params(10),
        name="layer_two",
    )(*args)


def main(
    features,
    self_ids,
    neighbour_ids,
    count_one,
    count_two,
    self_one,
    neigh_one,
    bias_one,
    self_two,
    neigh_two,
    bias_two,
    out_weight,
    out_bias,
):
    owners = lax.axis_size("col")
    seeds = count_two.shape[0]
    per_owner = self_ids.shape[0] // owners
    per_seed = per_owner // seeds
    fanout = neighbour_ids.shape[0]
    width = features.shape[0]
    col = lax.axis_index("col")
    rep = lax.axis_index("rep")
    z = col // 2
    me = jnp.stack([col % 2, 1 - z // 2, rep, z % 2, col]).astype(I32)

    def across(value, bit):
        return lax.ppermute(value, "col", [(i, i ^ bit) for i in range(owners)])

    other = lax.ppermute(features, "rep", [(0, 1), (1, 0)])
    held = pltpu.with_memory_space_constraint(features, pltpu.HBM)
    own = count_two[None, :]
    got_1 = across(own, 1)
    weights = join_call(self_one, neigh_one)
    table, got_1, weights = lax.optimization_barrier(
        (own_call(0, 2, me, held), got_1, weights)
    )
    pair = join_call(own, got_1)
    got = tuple(across(pair, bit) for bit in (4, 6, 2))
    weights_got = across(weights, 1)
    table, got, weights_got = lax.optimization_barrier(
        (own_call(1, 2, me, held, table), got, weights_got)
    )
    got = (got_1, got[2], got[0], got[1])
    lists, most = order_call(per_seed, me, own, got, self_ids, neighbour_ids, count_one)
    table, keep_far, send_far = first_call(fanout, me, lists, table, other)
    got_far = across(send_far, 1)
    keep_near, send_near = second_call(fanout, width, me, lists, table)
    far = far_call(me, keep_far, got_far, weights, weights_got)
    far, send_near = lax.optimization_barrier((far, send_near))
    far_got = [across(far[0], 4), across(far[1], 6)]
    got_near = across(send_near, 1)
    near = near_call(me, keep_near, got_near, weights, weights_got)
    far_got.append(across(near[1], 2))
    fast = last_call(
        near[0],
        *far_got,
        own,
        bias_one[None, :],
        self_two,
        neigh_two,
        bias_two[None, :],
        out_weight.T,
        out_bias[None, :],
    )
    return lax.cond(
        most > CAP,
        lambda: general(
            other,
            features,
            self_ids,
            neighbour_ids,
            count_one,
            count_two,
            self_one,
            neigh_one,
            bias_one,
            self_two,
            neigh_two,
            bias_two,
            out_weight,
            out_bias,
        ),
        lambda: fast,
    )


def local(*args):
    features, self_ids, neighbour_ids = args[0], args[1], args[2]
    sizes = (lax.axis_size("groups"), lax.axis_size("col"), lax.axis_size("rep"))
    small = (
        sizes == (2, 8, 2)
        and LANES // 2 < features.shape[0] <= 3 * LANES // 4
        and features.shape[1] <= 32768
        and self_ids.shape[0] * (neighbour_ids.shape[0] + 1) <= 2**17
        and neighbour_ids.shape[0] <= 15
    )
    if small:
        return main(*args)
    return general(lax.ppermute(features, "rep", [(0, 1), (1, 0)]), *args)


def solution(mesh):
    placed = (
        P("col", ("groups", "rep")),
        P(("groups", "rep")),
        P(None, ("groups", "rep")),
        P(("groups", "rep")),
        P(("groups", "col", "rep")),
        P("col", None),
        P("col", None),
        P(),
        P(),
        P(),
        P(),
        P(),
        P(),
    )
    return jax.shard_map(
        local,
        mesh=mesh,
        in_specs=placed,
        out_specs=P(("groups", "col", "rep"), None),
        check_vma=False,
    )
```

```python
import functools

import jax
import jax.numpy as jnp
import numpy as np
from jax import lax
from jax.experimental import pallas as pl
from jax.experimental.pallas import tpu as pltpu
from jax.sharding import PartitionSpec as P

CAP = 272
UNROLL = 8
POSITIONS = 10 * 128
FIRST_MIB = 12
OWN_MIB = 18
LANES = 128
MIB = 2**20
BF16 = jnp.bfloat16
F32 = jnp.float32
I32 = jnp.int32


def gathered(value, axis):
    copies = jnp.broadcast_to(value[None], (lax.axis_size(axis),) + value.shape)
    pieces = lax.all_to_all(copies, axis, split_axis=0, concat_axis=0, tiled=True)
    return pieces.reshape((-1,) + value.shape[1:])


def general(
    other,
    features,
    self_ids,
    neighbour_ids,
    count_one,
    count_two,
    self_one,
    neigh_one,
    bias_one,
    self_two,
    neigh_two,
    bias_two,
    out_weight,
    out_bias,
):
    mine = jnp.where(lax.axis_index("rep") == 0, 0, 1)
    table_cols = jnp.where(
        mine == 0,
        jnp.concatenate([features, other], axis=1),
        jnp.concatenate([other, features], axis=1),
    )
    table_rows = table_cols.T
    blocks = lax.axis_size("col")
    total_rows = self_ids.shape[0]
    per_owner = total_rows // blocks
    fanout = neighbour_ids.shape[0]
    width = table_rows.shape[1]
    all_ids = jnp.concatenate([self_ids[None, :], neighbour_ids], axis=0)
    fetched = jnp.take(table_rows, all_ids, axis=0)
    self_x = fetched[0]
    mask = (jnp.arange(fanout)[:, None] < count_one[None, :]).astype(BF16)
    summed = jnp.einsum("kmc,km->mc", fetched[1:], mask, preferred_element_type=F32)
    mean_one = (summed / count_one[:, None].astype(F32)).astype(BF16)
    full_self, full_neigh = gathered(self_one, "col"), gathered(neigh_one, "col")
    stacked = jnp.stack([self_x, mean_one], axis=0).reshape(2, blocks, per_owner, width)
    pieces = lax.all_to_all(stacked, "col", split_axis=1, concat_axis=3, tiled=True)
    pre_one = jnp.dot(pieces[0, 0], full_self, preferred_element_type=F32) + jnp.dot(
        pieces[1, 0], full_neigh, preferred_element_type=F32
    )
    hidden_one = jax.nn.relu(pre_one + bias_one).astype(BF16)
    seeds = count_two.shape[0]
    hidden = hidden_one.shape[1]
    grouped = hidden_one.reshape(seeds, per_owner // seeds, hidden)
    mask_two = (jnp.arange(grouped.shape[1] - 1)[None, :] < count_two[:, None]).astype(BF16)
    summed_two = jnp.einsum("skh,sk->sh", grouped[:, 1:, :], mask_two, preferred_element_type=F32)
    mean_two = (summed_two / count_two[:, None].astype(F32)).astype(BF16)
    pre_two = jnp.dot(grouped[:, 0, :], self_two, preferred_element_type=F32) + jnp.dot(
        mean_two, neigh_two, preferred_element_type=F32
    )
    hidden_two = jax.nn.relu(pre_two + bias_two).astype(BF16)
    return jnp.dot(hidden_two, out_weight, preferred_element_type=F32) + out_bias


def iota(shape, dim):
    return lax.broadcasted_iota(I32, shape, dim)


def tree_sum(terms):
    while len(terms) > 1:
        odd = [terms[-1]] if len(terms) % 2 else []
        terms = [a + b for a, b in zip(terms[::2], terms[1::2])] + odd
    return terms[0]


VMEM = pl.BlockSpec(memory_space=pltpu.VMEM)
SMEM = pl.BlockSpec(memory_space=pltpu.SMEM)
HBM = pl.BlockSpec(memory_space=pltpu.HBM)
ANY = pl.BlockSpec(memory_space=pl.ANY)


def start_all(copies):
    for copy in copies:
        copy.start()


def turn(source, table, base):
    width, length = source.shape
    step = 512
    unroll = 8

    def body(i, carry):
        for u in range(unroll):
            off = pl.multiple_of((i * unroll + u) * step, step)
            rows = source[:, pl.ds(off, step)].T.astype(F32)
            table[pl.ds(pl.multiple_of(base + off, step), step), 0:width] = rows
        return carry

    lax.fori_loop(0, length // step // unroll, body, 0)


def order_kernel(
    per_seed, me, own, got_1, got_2, got_4, got_6, self_ids, neighbour_ids, count_one, lists, most, counts_rel
):
    owners, seeds = counts_rel.shape
    fanout = neighbour_ids.shape[0]
    per_owner = count_one.shape[0] // owners
    half = owners // 2
    mine = me[4]
    counts_rel[0:1, :] = own[...]
    counts_rel[1:2, :] = got_1[...]
    counts_rel[2:4, :] = got_2[...]
    counts_rel[4:6, :] = got_4[...]
    counts_rel[6:8, :] = got_6[...]
    own_ids = self_ids[...].reshape(1, owners * per_owner)
    ones = count_one[...].reshape(1, owners * per_owner)
    counts = jnp.concatenate(
        [counts_rel[pl.ds(jnp.bitwise_xor(mine, c), 1), :] for c in range(owners)], axis=0
    ).astype(F32)
    needs = (counts + 1.0).astype(BF16)
    most[0] = jnp.max(jnp.sum(counts + 1.0, axis=1, keepdims=True)).astype(I32)
    column = iota((seeds, per_owner), 1).astype(F32)
    seed_of = jnp.floor((column + 0.5) * (1.0 / per_seed))
    seed = iota((seeds, per_owner), 0).astype(F32)
    t = column[0:1, :] - seed_of[0:1, :] * per_seed
    of_row = jnp.dot(
        counts.astype(BF16), (seed == seed_of).astype(BF16), preferred_element_type=F32
    )
    slot = t + jnp.dot(needs, (seed < seed_of).astype(BF16), preferred_element_type=F32)
    used = (t <= of_row) & (slot < CAP)
    slot = slot.astype(I32)
    keys = [
        jnp.where(used[c : c + 1, :], ones[:, c * per_owner : (c + 1) * per_owner], 0)
        for c in range(owners)
    ]
    kinds = [
        iota((16, per_owner), 0) == jnp.broadcast_to(key, (16, per_owner)) for key in keys
    ]
    stacked = jnp.concatenate([k.astype(F32).astype(BF16) for k in kinds], axis=0)
    left = (iota((per_owner, per_owner), 0) < iota((per_owner, per_owner), 1)).astype(BF16)
    prefix = jnp.dot(stacked, left, preferred_element_type=F32)
    total = jnp.dot(stacked, jnp.ones((per_owner, LANES), BF16), preferred_element_type=F32)
    for h in range(2):
        carry = jnp.zeros((16, LANES), F32)
        carries = []
        for c in range(h * half, (h + 1) * half):
            carries.append(carry)
            carry = carry + total[c * 16 : (c + 1) * 16, :]
        sizes = jnp.floor((carry + (UNROLL - 1)) * (1.0 / UNROLL)) * UNROLL
        bases = [jnp.zeros((1, LANES), F32)]
        for v in range(1, 16):
            bases.append(bases[-1] + sizes[v : v + 1, :])
        first = jnp.concatenate([bases[0]] + bases[:15], axis=0)
        sums = jnp.zeros((2 * (fanout + 2) * 16, LANES), F32)
        for i, c in enumerate(range(h * half, (h + 1) * half)):
            begin = (first + carries[i])[:, 0:1]
            spot = jnp.where(kinds[c], prefix[c * 16 : (c + 1) * 16, :] + begin, 0.0)
            spot = jnp.sum(spot, axis=0, keepdims=True).astype(I32)
            spot = jnp.where(keys[c] > 0, spot, -1)
            spot_lo = jnp.bitwise_and(spot, LANES - 1)
            spot_hi = jnp.right_shift(spot, 7)
            lane = (iota((LANES, per_owner), 0) == spot_lo).astype(F32).astype(BF16)
            at_hi = (iota((16, per_owner), 0) == spot_hi).astype(F32)
            columns = slice(c * per_owner, (c + 1) * per_owner)
            rows = [own_ids[:, columns]]
            rows += [neighbour_ids[k : k + 1, columns] for k in range(fanout)]
            rows += [half * CAP - (slot[c : c + 1, :] + i * CAP)]
            parts = []
            for row in rows:
                for byte in (jnp.right_shift(row, 8), jnp.bitwise_and(row, 255)):
                    value = jnp.broadcast_to(byte.astype(F32), (16, per_owner))
                    parts.append((at_hi * value).astype(BF16))
            sums = sums + lax.dot_general(
                jnp.concatenate(parts, axis=0),
                lane,
                (((1,), (1,)), ((), ())),
                preferred_element_type=F32,
            )
        for k in range(fanout + 2):
            hi = sums[32 * k : 32 * k + 16, :]
            lo = sums[32 * k + 16 : 32 * k + 32, :]
            value = (hi * 256.0 + lo).astype(I32)
            lists[h, k, :, :] = value if k <= fanout else half * CAP - value
        lane = iota((8, LANES), 1)
        begins = jnp.zeros((8, LANES), F32)
        for v in range(16):
            begins = begins + jnp.where(lane == v, bases[v], 0.0)
        lists[h, fanout + 2, 0:8, :] = begins.astype(I32)
        lists[h, fanout + 2, 8:16, :] = jnp.zeros((8, LANES), I32)


def list_copies(fanout, h, lists, ids, places, begins, sems):
    block = 16 * LANES

    def piece(k, length):
        at = pl.multiple_of((h * (fanout + 3) + k) * block, block)
        return lists.at[pl.ds(at, length)]

    last = fanout + 2
    copies = [
        pltpu.make_async_copy(piece(k, POSITIONS), ref, sems.at[k])
        for k, ref in enumerate(list(ids) + [places])
    ]
    copies.append(pltpu.make_async_copy(piece(last, LANES), begins, sems.at[last]))
    start_all(copies[fanout + 1 :] + copies[: fanout + 1])
    return copies


def look_up(fanout, copies, table, ids, places, begins, self_rows, mean_rows):
    for copy in [copies[0]] + copies[fanout + 1 :]:
        copy.wait()
    for v in range(1, fanout + 1):
        copies[v].wait()
        begin = begins[v - 1]
        end = begins[v]

        def body(i, carry, v=v, begin=begin):
            for u in range(UNROLL):
                at = begin + i * UNROLL + u
                to = places[at]
                self_rows[pl.ds(to, 1), :] = table[pl.ds(ids[0][at], 1), :]
                total = tree_sum([table[pl.ds(ids[k][at], 1), :] for k in range(1, v + 1)])
                mean_rows[pl.ds(to, 1), :] = total * (1.0 / v)
            return carry

        lax.fori_loop(0, jnp.right_shift(end - begin, UNROLL.bit_length() - 1), body, 0)


def write_out(x, width, self_rows, mean_rows, keep, send):
    lane = iota((CAP, LANES), 1)
    rest = 2 * width - LANES
    for ref, side in ((keep, x), (send, 1 - x)):
        turned = []
        for z in range(2):
            at = pl.multiple_of((z * 2 + side) * CAP, CAP)
            mean = jnp.where(lane < width, mean_rows[pl.ds(at, CAP), :], 0.0)
            turned.append(pltpu.roll(mean, width, 1))
            own = self_rows[pl.ds(at, CAP), :]
            ref[z, :, :] = jnp.where(lane < width, own, turned[z]).astype(BF16)
        right = pltpu.roll(turned[1], LANES // 2, 1)
        block = jnp.where(lane < LANES // 2, turned[0], right)
        used = (lane < rest) | ((lane >= LANES // 2) & (lane < LANES // 2 + rest))
        ref[2, :, :] = jnp.where(used, block, 0.0).astype(BF16)


def stage(source, staged, sems):
    blocks, _, part = staged.shape
    copies = [
        pltpu.make_async_copy(source.at[:, pl.ds(b * part, part)], staged.at[b], sems.at[b])
        for b in range(blocks)
    ]
    start_all(copies)
    return copies


def turn_staged(copies, staged, table, base):
    part = staged.shape[2]
    for b, copy in enumerate(copies):
        copy.wait()
        turn(staged.at[b], table, pl.multiple_of(base + b * part, part))


def own_kernel(which, halves, me, features, *refs):
    table, staged, sems = refs[-3:]
    length = features.shape[1]
    half = length // halves
    copies = stage(features.at[:, pl.ds(which * half, half)], staged, sems)
    turn_staged(copies, staged, table, me[2] * length + which * half)


def join_kernel(*refs):
    *parts, out = refs
    at = 0
    for part in parts:
        out[at : at + part.shape[0], :] = part[...]
        at += part.shape[0]


def hand_out(keep, send, keep_hbm, send_hbm, sems):
    copies = [
        pltpu.make_async_copy(send, send_hbm, sems.at[0]),
        pltpu.make_async_copy(keep, keep_hbm, sems.at[1]),
    ]
    start_all(copies)
    for copy in copies:
        copy.wait()


def first_kernel(
    fanout, me, lists, table_in, other, table, keep_hbm, send_hbm, *scratch
):
    del table_in
    ids = scratch[: fanout + 1]
    places, begins, self_rows, mean_rows, sems = scratch[fanout + 1 : fanout + 6]
    staged, staged_sems, keep, send, out_sems = scratch[fanout + 6 :]
    width, length = other.shape
    x, h, rep = me[0], me[1], me[2]
    staging = stage(other, staged, staged_sems)
    copies = list_copies(fanout, h, lists, ids, places, begins, sems)
    self_rows[...] = jnp.zeros_like(self_rows)
    mean_rows[...] = jnp.zeros_like(mean_rows)
    turn_staged(staging, staged, table, (1 - rep) * length)
    look_up(fanout, copies, table, ids, places, begins, self_rows, mean_rows)
    write_out(x, width, self_rows, mean_rows, keep, send)
    hand_out(keep, send, keep_hbm, send_hbm, out_sems)


def second_kernel(fanout, width, me, lists, table, keep_hbm, send_hbm, *scratch):
    ids = scratch[: fanout + 1]
    places, begins, self_rows, mean_rows, sems, keep, send, out_sems = scratch[fanout + 1 :]
    x, h = me[0], 1 - me[1]
    copies = list_copies(fanout, h, lists, ids, places, begins, sems)
    self_rows[...] = jnp.zeros_like(self_rows)
    mean_rows[...] = jnp.zeros_like(mean_rows)
    look_up(fanout, copies, table, ids, places, begins, self_rows, mean_rows)
    write_out(x, width, self_rows, mean_rows, keep, send)
    hand_out(keep, send, keep_hbm, send_hbm, out_sems)


def partials(blocks, weights):
    rest = weights.shape[0] - LANES
    return [
        jnp.dot(blocks[z], weights[0:LANES, :], preferred_element_type=F32)
        + jnp.dot(
            blocks[2, :, z * LANES // 2 : z * LANES // 2 + rest],
            weights[LANES:, :],
            preferred_element_type=F32,
        )
        for z in range(2)
    ]


def far_kernel(me, keep, got, weights, weights_got, out_0, out_1):
    zl = me[3]
    pre = [a + b for a, b in zip(partials(keep, weights), partials(got, weights_got))]
    out_0[...] = jnp.where(zl == 0, pre[0], pre[1]).astype(BF16)
    out_1[...] = jnp.where(zl == 0, pre[1], pre[0]).astype(BF16)


def near_kernel(me, keep_hbm, got, weights, weights_got, out_0, out_1, keep, sem):
    copy = pltpu.make_async_copy(keep_hbm, keep, sem)
    copy.start()
    zl = me[3]
    theirs = partials(got, weights_got)
    copy.wait()
    pre = [a + b for a, b in zip(partials(keep, weights), theirs)]
    out_0[...] = jnp.where(zl == 0, pre[0], pre[1])
    out_1[...] = jnp.where(zl == 0, pre[1], pre[0]).astype(BF16)


def last_kernel(
    mine, a, b, c, counts, bias_one, self_two, neigh_two, bias_two, out_weight, out_bias, out
):
    pre = mine[...] + a[...].astype(F32) + b[...].astype(F32) + c[...].astype(F32)
    hidden = jnp.maximum(pre + bias_one[...], 0.0).astype(BF16)
    seeds = counts.shape[1]
    same = iota((seeds, seeds), 0) == iota((seeds, seeds), 1)
    count = jnp.sum(jnp.where(same, counts[...].astype(F32), 0.0), axis=1, keepdims=True)
    count = count.astype(I32)
    earlier = (iota((seeds, seeds), 0) > iota((seeds, seeds), 1)).astype(BF16)
    needs = jnp.broadcast_to((count + 1).astype(F32), (seeds, LANES)).astype(BF16)
    offset = jnp.dot(earlier, needs, preferred_element_type=F32)[:, 0:1].astype(I32)
    place = iota((seeds, CAP), 1) - offset
    is_self = (place == 0).astype(F32).astype(BF16)
    is_near = ((place >= 1) & (place <= count)).astype(F32).astype(BF16)
    own = jnp.dot(is_self, hidden, preferred_element_type=F32).astype(BF16)
    total = jnp.dot(is_near, hidden, preferred_element_type=F32)
    mean = (total / count.astype(F32)).astype(BF16)
    pre_two = (
        jnp.dot(own, self_two[...], preferred_element_type=F32)
        + jnp.dot(mean, neigh_two[...], preferred_element_type=F32)
        + bias_two[...]
    )
    hidden_two = jnp.maximum(pre_two, 0.0).astype(BF16)
    logits = lax.dot_general(
        hidden_two, out_weight[...], (((1,), (1,)), ((), ())), preferred_element_type=F32
    )
    out[...] = logits + out_bias[...]


def params(limit):
    return pltpu.CompilerParams(vmem_limit_bytes=limit * MIB)


def shape(dims, dtype):
    return jax.ShapeDtypeStruct(dims, dtype)


def order_call(per_seed, me, own, got, self_ids, neighbour_ids, count_one):
    owners = sum(x.shape[0] for x in (own, *got))
    lists, most = pl.pallas_call(
        functools.partial(order_kernel, per_seed),
        out_shape=(shape((2, neighbour_ids.shape[0] + 3, 16, LANES), I32), shape((1,), I32)),
        in_specs=[SMEM] + [VMEM] * 8,
        out_specs=(VMEM, SMEM),
        scratch_shapes=[pltpu.VMEM((owners, own.shape[1]), I32)],
        compiler_params=params(10),
        name="order",
    )(me, own, *got, self_ids, neighbour_ids, count_one)
    return lists.reshape(-1), most[0]


def list_scratch(fanout):
    return (
        [pltpu.SMEM((POSITIONS,), I32) for _ in range(fanout + 2)]
        + [pltpu.SMEM((LANES,), I32)]
        + [pltpu.VMEM((4 * CAP + 8, LANES), F32) for _ in range(2)]
        + [pltpu.SemaphoreType.DMA((fanout + 3,))]
    )


def own_call(which, halves, me, features, *table):
    width, length = features.shape
    parts = 8 // halves
    return pl.pallas_call(
        functools.partial(own_kernel, which, halves),
        out_shape=shape((2 * length, LANES), F32),
        in_specs=[SMEM, HBM] + [VMEM] * len(table),
        out_specs=VMEM,
        scratch_shapes=[
            pltpu.VMEM((parts, width, length // 8), BF16),
            pltpu.SemaphoreType.DMA((parts,)),
        ],
        input_output_aliases={2: 0} if table else {},
        compiler_params=params(FIRST_MIB if table else OWN_MIB),
        name="own_rows",
    )(me, features, *table)


def join_call(*parts):
    rows = sum(part.shape[0] for part in parts)
    return pl.pallas_call(
        join_kernel,
        out_shape=shape((rows, parts[0].shape[1]), parts[0].dtype),
        in_specs=[VMEM] * len(parts),
        out_specs=VMEM,
        compiler_params=params(1),
        name="join",
    )(*parts)


def first_call(fanout, me, lists, table, other):
    width, length = other.shape
    dims = (3, CAP, LANES)
    return pl.pallas_call(
        functools.partial(first_kernel, fanout),
        out_shape=(shape((2 * length, LANES), F32), pltpu.HBM(dims, BF16), pltpu.HBM(dims, BF16)),
        in_specs=[SMEM, ANY, VMEM, HBM],
        out_specs=(VMEM, HBM, HBM),
        scratch_shapes=list_scratch(fanout)
        + [
            pltpu.VMEM((8, width, length // 8), BF16),
            pltpu.SemaphoreType.DMA((8,)),
            pltpu.VMEM(dims, BF16),
            pltpu.VMEM(dims, BF16),
            pltpu.SemaphoreType.DMA((2,)),
        ],
        input_output_aliases={2: 0},
        compiler_params=params(FIRST_MIB),
        name="first_half",
    )(me, lists, table, other)


def second_call(fanout, width, me, lists, table):
    dims = (3, CAP, LANES)
    halves = pltpu.HBM(dims, BF16)
    return pl.pallas_call(
        functools.partial(second_kernel, fanout, width),
        out_shape=(halves, halves),
        in_specs=[SMEM, ANY, VMEM],
        out_specs=(HBM, HBM),
        scratch_shapes=list_scratch(fanout)
        + [pltpu.VMEM(dims, BF16) for _ in range(2)]
        + [pltpu.SemaphoreType.DMA((2,))],
        compiler_params=params(10),
        name="second_half",
    )(me, lists, table)


def far_call(me, keep, got, weights, weights_got):
    part = shape((CAP, weights.shape[1]), BF16)
    return pl.pallas_call(
        far_kernel,
        out_shape=(part, part),
        in_specs=[SMEM] + [VMEM] * 4,
        out_specs=(VMEM, VMEM),
        compiler_params=params(10),
        name="project_far",
    )(me, keep, got, weights, weights_got)


def near_call(me, keep, got, weights, weights_got):
    dims = (CAP, weights.shape[1])
    return pl.pallas_call(
        near_kernel,
        out_shape=(shape(dims, F32), shape(dims, BF16)),
        in_specs=[SMEM, HBM] + [VMEM] * 3,
        out_specs=(VMEM, VMEM),
        scratch_shapes=[pltpu.VMEM(keep.shape, BF16), pltpu.SemaphoreType.DMA],
        compiler_params=params(10),
        name="project_near",
    )(me, pltpu.with_memory_space_constraint(keep, pltpu.HBM), got, weights, weights_got)


def last_call(*args):
    seeds = args[4].shape[1]
    classes = args[-1].shape[1]
    return pl.pallas_call(
        last_kernel,
        out_shape=shape((seeds, classes), F32),
        in_specs=[VMEM] * len(args),
        out_specs=VMEM,
        compiler_params=params(10),
        name="layer_two",
    )(*args)


def main(
    features,
    self_ids,
    neighbour_ids,
    count_one,
    count_two,
    self_one,
    neigh_one,
    bias_one,
    self_two,
    neigh_two,
    bias_two,
    out_weight,
    out_bias,
):
    owners = lax.axis_size("col")
    seeds = count_two.shape[0]
    per_owner = self_ids.shape[0] // owners
    per_seed = per_owner // seeds
    fanout = neighbour_ids.shape[0]
    width = features.shape[0]
    col = lax.axis_index("col")
    rep = lax.axis_index("rep")
    z = col // 2
    me = jnp.stack([col % 2, 1 - z // 2, rep, z % 2, col]).astype(I32)

    def across(value, bit):
        return lax.ppermute(value, "col", [(i, i ^ bit) for i in range(owners)])

    other = lax.ppermute(features, "rep", [(0, 1), (1, 0)])
    held = pltpu.with_memory_space_constraint(features, pltpu.HBM)
    own = count_two[None, :]
    got_1 = across(own, 1)
    weights = join_call(self_one, neigh_one)
    table, got_1, weights = lax.optimization_barrier(
        (own_call(0, 2, me, held), got_1, weights)
    )
    pair = join_call(own, got_1)
    got = tuple(across(pair, bit) for bit in (4, 6, 2))
    weights_got = across(weights, 1)
    table, got, weights_got = lax.optimization_barrier(
        (own_call(1, 2, me, held, table), got, weights_got)
    )
    got = (got_1, got[2], got[0], got[1])
    lists, most = order_call(per_seed, me, own, got, self_ids, neighbour_ids, count_one)
    table, keep_far, send_far = first_call(fanout, me, lists, table, other)
    got_far = across(send_far, 1)
    keep_near, send_near = second_call(fanout, width, me, lists, table)
    far = far_call(me, keep_far, got_far, weights, weights_got)
    far_got = [across(far[0], 4), across(far[1], 6)]
    got_near = across(send_near, 1)
    near = near_call(me, keep_near, got_near, weights, weights_got)
    far_got.append(across(near[1], 2))
    fast = last_call(
        near[0],
        *far_got,
        own,
        bias_one[None, :],
        self_two,
        neigh_two,
        bias_two[None, :],
        out_weight.T,
        out_bias[None, :],
    )
    return lax.cond(
        most > CAP,
        lambda: general(
            other,
            features,
            self_ids,
            neighbour_ids,
            count_one,
            count_two,
            self_one,
            neigh_one,
            bias_one,
            self_two,
            neigh_two,
            bias_two,
            out_weight,
            out_bias,
        ),
        lambda: fast,
    )


def local(*args):
    features, self_ids, neighbour_ids = args[0], args[1], args[2]
    sizes = (lax.axis_size("groups"), lax.axis_size("col"), lax.axis_size("rep"))
    small = (
        sizes == (2, 8, 2)
        and LANES // 2 < features.shape[0] <= 3 * LANES // 4
        and features.shape[1] <= 32768
        and self_ids.shape[0] * (neighbour_ids.shape[0] + 1) <= 2**17
        and neighbour_ids.shape[0] <= 15
    )
    if small:
        return main(*args)
    return general(lax.ppermute(features, "rep", [(0, 1), (1, 0)]), *args)


def solution(mesh):
    placed = (
        P("col", ("groups", "rep")),
        P(("groups", "rep")),
        P(None, ("groups", "rep")),
        P(("groups", "rep")),
        P(("groups", "col", "rep")),
        P("col", None),
        P("col", None),
        P(),
        P(),
        P(),
        P(),
        P(),
        P(),
    )
    return jax.shard_map(
        local,
        mesh=mesh,
        in_specs=placed,
        out_specs=P(("groups", "col", "rep"), None),
        check_vma=False,
    )
```
